128 devices in a mesh: gx: 16 (over x_lo, z, core), gy: 8 (over x_hi, y).
Axes of the slice: x: 4 (x_hi: 2, x_lo: 2; x = x_hi * 2 + x_lo), y: 4, z: 4, core: 2. Of those that a mesh axis runs over, the one named last changes fastest.
Arguments:
- pdf_old: float32 [16384, 19, 256], P(('gx', 'gy')), may hold values from -3 to 3
- tile_target: int32 [16384], P(('gx', 'gy')), may hold values from 0 to 16383, as said below
- porosity: float32 [256, 128, 128], P(('gx', 'gy')), may hold values from 0 to 0.6
- relaxation: float32 [256, 128, 128], P(('gx', 'gy')), may hold values from 0.6 to 1.8
- solid_mask: int32 [256, 128, 128], P('gx', 'gy'), may hold values 0 or 1
- force: float32 [3], replicated, may hold values from -0.1 to 0.1
Outputs:
- deviation_out: float32 [19, 256, 128, 128], P(None, 'gx', 'gy')
The draws below stay inside these ranges and needn't reach their ends.
Inputs may be any that keep to these rules, and one draw needn't show every extreme that they name: tile_target holds every tile index once. The tiles of one device go to at most 2 of their number to any one device (device = tile index // 128), and in every draw some device sends exactly 2 tiles to some device.
All inputs are finite; a program needn't handle non-finite values. No bound on the sum of `solid_mask` on one device may be relied on, other than what follows from the above.
Results may differ from the reference program's by a relative error of at most 0.00023.
Values sent between devices are 32-bit elements; how exact they have to be, the bound alone decides.
No kernel may reach another device: no remote copies, remote signals or barrier semaphores. Data moves between devices by JAX's collectives and lax.ppermute only.
A program may use at most 64 MiB of HBM per device.

```python
import jax
import jax.numpy as jnp
import numpy as np
from jax import lax

CX = 16
CY = 16
NZ = 128
TY = 2
STEPS = 2
NX = 256
NY = 128
TILES_DEV = 128
TILES = 16384
TILE_CELLS = 256
N_GX = 16
N_GY = 8


def draw_tile_target(key, part):
    dev_count = TILES // TILES_DEV
    capacity = 2 * TILES_DEV // dev_count
    half_cap = capacity // 2
    key_list = jax.random.split(key, 5)
    spread = jax.random.randint(key_list[0], (dev_count // 2,), 0, half_cap + 1).at[0].set(half_cap)
    multiple = jnp.stack([half_cap + spread, half_cap - spread], axis=1).reshape(dev_count)
    offsets = jnp.repeat(jnp.arange(dev_count), multiple, total_repeat_length=TILES_DEV)
    perm_first = jax.random.permutation(key_list[1], dev_count)
    perm_second = jax.random.permutation(key_list[2], dev_count)
    owner_dev = perm_second[(perm_first[:, None] + offsets[None, :]) % dev_count]
    orders = jax.vmap(lambda subkey: jax.random.permutation(subkey, TILES_DEV))(jax.random.split(key_list[3], dev_count))
    slot_ids = orders[owner_dev, jnp.arange(TILES_DEV)[None, :]]
    targets = owner_dev * TILES_DEV + slot_ids
    shuffle = jax.vmap(lambda subkey: jax.random.permutation(subkey, TILES_DEV))(jax.random.split(key_list[4], dev_count))
    targets = jnp.take_along_axis(targets, shuffle, axis=1)
    return targets.reshape(TILES).astype(jnp.int32)


def touch_ends(result, key, smallest, high):
    spot = [jax.random.randint(jax.random.fold_in(key, axis), (), 0, length) for axis, length in enumerate(result.shape)]
    widest = result.shape.index(max(result.shape))
    next_to = spot[:widest] + [(spot[widest] + 1) % result.shape[widest]] + spot[widest + 1:]
    return result.at[tuple(spot)].set(smallest).at[tuple(next_to)].set(high)


def shard_levels(rng, dims, shards, low, top_value):
    factor_of = 1.0
    for position, parts in shards:
        steps = jax.random.uniform(jax.random.fold_in(jax.random.fold_in(rng, 6), position), (parts,), jnp.float32, low / len(shards), top_value / len(shards))
        factor_of = factor_of * jnp.repeat(jnp.exp(steps), dims[position] // parts).reshape((-1,) + (1,) * (len(dims) - 1 - position))
    return factor_of


def centred(key, extent, scale, reach, cuts=(), dtype=jnp.bfloat16):
    entries = scale * jax.random.normal(key, extent, jnp.float32)
    if cuts:
        entries = entries * shard_levels(key, extent, cuts, -0.22, 0.18)
    return jnp.clip(entries, -reach, reach).astype(dtype)


def setup_inputs(seed: int = 0) -> dict:
    splits = jax.random.split(jax.random.key(seed), 7)
    pdf_old = centred(splits[0], (TILES, 19, TILE_CELLS), 0.5, 3.0, ((0, 128),), jnp.float32)
    tile_target = draw_tile_target(jax.random.fold_in(splits[6], 71), 0)
    porosity = jnp.clip(0.6 * jax.random.uniform(splits[2], (NX, NY, NZ), jnp.float32) ** shard_levels(splits[2], (NX, NY, NZ), ((0, 128),), -0.2, 0.2), 0.0, 0.6)
    relaxation = jnp.clip(0.6 + 1.1999999 * jax.random.uniform(splits[3], (NX, NY, NZ), jnp.float32) ** shard_levels(splits[3], (NX, NY, NZ), ((0, 128),), -0.2, 0.2), 0.6, 1.8)
    solid_mask = touch_ends((jax.random.randint(splits[4], (NX, NY, NZ), 0, 10) < 3).astype(jnp.int32), jax.random.fold_in(splits[4], 1), 0, 1)
    force = jnp.clip(jax.random.uniform(splits[5], (3,), jnp.float32, -0.1, 0.1), -0.1, 0.1)
    return dict(pdf_old=pdf_old, tile_target=tile_target, porosity=porosity, relaxation=relaxation, solid_mask=solid_mask, force=force)


VELOCITY = ((0, 0, 0), (1, 0, 0), (-1, 0, 0), (0, 1, 0), (0, -1, 0), (0, 0, 1), (0, 0, -1),
            (1, 1, 0), (-1, -1, 0), (1, -1, 0), (-1, 1, 0), (1, 0, 1), (-1, 0, -1),
            (1, 0, -1), (-1, 0, 1), (0, 1, 1), (0, -1, -1), (0, 1, -1), (0, -1, 1))
OPPOSITE = [0, 2, 1, 4, 3, 6, 5, 8, 7, 10, 9, 12, 11, 14, 13, 16, 15, 18, 17]
WEIGHT_LIST = [1.0 / 3.0] + [1.0 / 18.0] * 6 + [1.0 / 36.0] * 12
MAGIC = 0.1875


def lattice_weights(ndim):
    return jnp.array(WEIGHT_LIST, jnp.float32).reshape((19,) + (1,) * (ndim - 1))


def component(dist, axis_pos):
    plus_set = np.array([index for index in range(19) if VELOCITY[index][axis_pos] == 1])
    minus_set = np.array([index for index in range(19) if VELOCITY[index][axis_pos] == -1])
    return jnp.sum(dist[plus_set], axis=0) - jnp.sum(dist[minus_set], axis=0)


def collide(dist, porosity, omega_plus, solid_mask, force):
    weights = lattice_weights(dist.ndim)
    density = jnp.sum(dist, axis=0)
    flow = [component(dist, axis_pos) + 0.5 * force[axis_pos] for axis_pos in range(3)]
    speed_sq = flow[0] * flow[0] + flow[1] * flow[1] + flow[2] * flow[2]
    along = jnp.stack([VELOCITY[index][0] * flow[0] + VELOCITY[index][1] * flow[1] + VELOCITY[index][2] * flow[2] for index in range(19)])
    push = jnp.stack([VELOCITY[index][0] * force[0] + VELOCITY[index][1] * force[1] + VELOCITY[index][2] * force[2] for index in range(19)])
    push = push.reshape((19,) + (1,) * (dist.ndim - 1))
    reversed_dist = dist[np.array(OPPOSITE)]
    even_part = 0.5 * (dist + reversed_dist)
    odd_part = 0.5 * (dist - reversed_dist)
    eq_even = weights * (density + 4.5 * along * along - 1.5 * speed_sq)
    eq_odd = 3.0 * weights * along
    omega_minus = 1.0 / (MAGIC / (1.0 / omega_plus - 0.5) + 0.5)
    relaxed = dist - omega_plus * (even_part - eq_even) - omega_minus * (odd_part - eq_odd) + 3.0 * weights * push
    solid = porosity + solid_mask.astype(jnp.float32) * (1.0 - porosity)
    return (1.0 - solid) * relaxed + solid * reversed_dist


def reference(pdf_old, tile_target, porosity, relaxation, solid_mask, force):
    placed = jnp.zeros_like(pdf_old).at[tile_target].set(pdf_old)
    deviation = placed.reshape(N_GX, N_GY, CX, CY // TY, 19, TY, NZ).transpose(4, 0, 2, 1, 3, 5, 6).reshape(19, NX, NY, NZ)
    weights = lattice_weights(4)
    dist = weights * (1.0 + deviation)
    for step_index in range(STEPS):
        def plane_collide(items):
            return collide(items[0], items[1], items[2], items[3], force)

        post = lax.map(plane_collide, (jnp.moveaxis(dist, 1, 0), porosity, relaxation, solid_mask))
        post = jnp.moveaxis(post, 0, 1)
        dist = jnp.stack([jnp.roll(post[index], VELOCITY[index], axis=(0, 1, 2)) for index in range(19)])
    return dist / weights - 1.0
```

```python
import jax
import jax.numpy as jnp
from jax import lax
from jax.experimental import pallas as pl
from jax.experimental.pallas import tpu as pltpu
from jax.sharding import PartitionSpec as P

VELOCITY = (
    (0, 0, 0),
    (1, 0, 0),
    (-1, 0, 0),
    (0, 1, 0),
    (0, -1, 0),
    (0, 0, 1),
    (0, 0, -1),
    (1, 1, 0),
    (-1, -1, 0),
    (1, -1, 0),
    (-1, 1, 0),
    (1, 0, 1),
    (-1, 0, -1),
    (1, 0, -1),
    (-1, 0, 1),
    (0, 1, 1),
    (0, -1, -1),
    (0, 1, -1),
    (0, -1, 1),
)
WEIGHT = [1.0 / 3.0] + [1.0 / 18.0] * 6 + [1.0 / 36.0] * 12
INVERSE = [3.0] + [18.0] * 6 + [36.0] * 12
DEVICES = 128
HELD = 128
CAP = 2
ROWS = 40
EXT = 20
VMEM_LIMIT = 48 * 1024 * 1024
F32 = jnp.float32


def entries(axis, sign):
    far = [(q, 1) for q in range(19) if VELOCITY[q][axis] == sign]
    near = [(q, 0) for q in range(19) if VELOCITY[q][axis] in (0, sign)]
    return far + near


COUNT = 21


def collide(dist, solid, omega, force):
    plus = [None] * 19
    minus = [None] * 19
    for i in range(1, 19, 2):
        plus[i] = dist[i] + dist[i + 1]
        minus[i] = dist[i] - dist[i + 1]
    density = dist[0]
    for i in range(1, 19, 2):
        density = density + plus[i]
    flow = []
    for axis in range(3):
        total = None
        for i in range(1, 19, 2):
            c = VELOCITY[i][axis]
            if c:
                if total is None:
                    total = minus[i]
                else:
                    total = total + minus[i] if c == 1 else total - minus[i]
        flow.append(total + 0.5 * force[axis])
    base = density - 1.5 * (flow[0] * flow[0] + flow[1] * flow[1] + flow[2] * flow[2])
    open_ = 1.0 - solid
    a = open_ * omega
    b = open_ * ((2.0 - omega) / (1.0 - 0.125 * omega))
    keep = 0.5 - 0.5 * a
    turn = 0.5 - solid - 0.5 * b
    post = [None] * 19
    at = a * base
    post[0] = (keep + keep) * dist[0] + at * (1.0 / 3.0)
    drive = [b * flow[axis] + open_ * force[axis] for axis in range(3)]
    for group, w in ((range(1, 7, 2), 1.0 / 18.0), (range(7, 19, 2), 1.0 / 36.0)):
        even_base = at * w
        square = a * (4.5 * w)
        pull = [drive[axis] * (3.0 * w) for axis in range(3)]
        for i in group:
            along = None
            odd = None
            for axis in range(3):
                c = VELOCITY[i][axis]
                if c:
                    if along is None:
                        along, odd = flow[axis], pull[axis]
                    elif c == 1:
                        along, odd = along + flow[axis], odd + pull[axis]
                    else:
                        along, odd = along - flow[axis], odd - pull[axis]
            even = keep * plus[i] + (even_base + square * (along * along))
            odd = turn * minus[i] + odd
            post[i] = even + odd
            post[i + 1] = even - odd
    return post


def shift_z(value, q):
    c = VELOCITY[q][2]
    return value if c == 0 else pltpu.roll(value, c % 128, 1)


def pack_kernel(target, pdf, out, used):
    def clear(i, _):
        used[i] = 0
        return 0

    lax.fori_loop(0, DEVICES, clear, 0, unroll=8)
    empty = jnp.full((1, 128), -1.0, F32)

    def blank(i, _):
        out[pl.ds(i * ROWS + 38, 1), :] = empty
        return 0

    lax.fori_loop(0, DEVICES * CAP, blank, 0, unroll=8)

    def place(group, _):
        near = pdf.at[:, pl.ds(pl.multiple_of(group * 8, 8), 8), :]
        for i in range(8):
            t = target[group * 8 + i]
            owner = lax.shift_right_logical(t, 7)
            rank = used[owner]
            used[owner] = rank + 1
            start = (owner * CAP + rank) * ROWS
            for q in range(19):
                for r in range(2):
                    value = near[q, i : i + 1, r * 128 : (r + 1) * 128]
                    out[pl.ds(start + 2 * q + r, 1), :] = value
            out[pl.ds(start + 38, 1), :] = jnp.full((1, 128), (t & 127).astype(F32), F32)
        return 0

    lax.fori_loop(0, HELD // 8, place, 0)


def pack(target, pdf):
    return pl.pallas_call(
        pack_kernel,
        out_shape=jax.ShapeDtypeStruct((DEVICES * CAP * ROWS, 128), F32),
        in_specs=[
            pl.BlockSpec(memory_space=pltpu.SMEM),
            pl.BlockSpec(memory_space=pltpu.VMEM),
        ],
        out_specs=pl.BlockSpec(memory_space=pltpu.VMEM),
        scratch_shapes=[pltpu.SMEM((DEVICES,), jnp.int32)],
        compiler_params=pltpu.CompilerParams(vmem_limit_bytes=VMEM_LIMIT),
        cost_estimate=pl.CostEstimate(flops=0, bytes_accessed=8_000_000, transcendentals=0),
    )(target, pdf)


def first_kernel(source, force, arrived, coef, post, xup, xdn, yup, ydn, tiles, sems):
    def fetch(s, _):
        p = source[s]
        pltpu.make_async_copy(
            arrived.at[pl.ds(pl.multiple_of(p * ROWS, 8), ROWS), :],
            tiles.at[pl.ds(pl.multiple_of(s * ROWS, 8), ROWS), :],
            sems.at[lax.shift_right_logical(s, 3)],
        ).start()
        return 0

    lax.fori_loop(0, HELD, fetch, 0, unroll=4)
    f = [force[axis] for axis in range(3)]

    def plane(x, _):
        whole = pl.ds(pl.multiple_of(x * (8 * ROWS), 8), 8 * ROWS)
        pltpu.make_async_copy(
            arrived.at[pl.ds(0, 8 * ROWS), :], tiles.at[whole, :], sems.at[x]
        ).wait()
        for r in range(2):
            dist = []
            for q in range(19):
                value = tiles[pl.ds(x * (8 * ROWS) + 2 * q + r, 8, stride=ROWS), :]
                dist.append(WEIGHT[q] * value + WEIGHT[q])
            solid = coef[0, x, pl.ds(r, 8, stride=2), :]
            omega = coef[1, x, pl.ds(r, 8, stride=2), :]
            after = collide(dist, solid, omega, f)
            for q in range(19):
                post[q, x, pl.ds(r, 8, stride=2), :] = shift_z(after[q], q)
        return 0

    lax.fori_loop(0, 16, plane, 0)
    for out, sign in ((xup, 1), (xdn, -1)):
        for i, (q, layer) in enumerate(entries(0, sign)):
            out[i] = post[q, 15 - layer if sign == 1 else layer]
        for j in range(2):
            out[19 + j] = coef[j, 15 if sign == 1 else 0]
    for out, sign in ((yup, 1), (ydn, -1)):
        for i, (q, layer) in enumerate(entries(1, sign)):
            row = 15 - layer if sign == 1 else layer
            for x in range(16):
                out[i, x : x + 1, :] = post[q, x, row : row + 1, :]
        row = 15 if sign == 1 else 0
        for j in range(2):
            for x in range(16):
                out[19 + j, x : x + 1, :] = coef[j, x, row : row + 1, :]


def first(source, force, arrived, coef):
    face = jax.ShapeDtypeStruct((COUNT, 16, 128), F32)
    vmem = pl.BlockSpec(memory_space=pltpu.VMEM)
    smem = pl.BlockSpec(memory_space=pltpu.SMEM)
    return pl.pallas_call(
        first_kernel,
        out_shape=[jax.ShapeDtypeStruct((19, 16, 16, 128), F32)] + [face] * 4,
        in_specs=[smem, smem, pl.BlockSpec(memory_space=pl.ANY), vmem],
        out_specs=[vmem] * 5,
        scratch_shapes=[
            pltpu.VMEM((HELD * ROWS, 128), F32),
            pltpu.SemaphoreType.DMA((16,)),
        ],
        compiler_params=pltpu.CompilerParams(vmem_limit_bytes=VMEM_LIMIT),
        cost_estimate=pl.CostEstimate(flops=10_000_000, bytes_accessed=8_000_000, transcendentals=0),
    )(source, force, arrived, coef)


def join_kernel(left, right, yup, ydn, up, dn):
    zero = jnp.zeros((1, 128), F32)
    for own, out, sign in ((yup, up, 1), (ydn, dn, -1)):
        listed = entries(1, sign) + [(19, 0), (20, 0)]
        for i, (q, layer) in enumerate(listed):
            row = 15 - layer if sign == 1 else layer
            out[i * EXT + 2 : i * EXT + 18, :] = own[i]
            for half, toward in ((left, 1), (right, -1)):
                have = {e: n for n, e in enumerate(entries(0, toward) + [(19, 0), (20, 0)])}
                for deep in range(2):
                    at = (1 - deep) if toward == 1 else 18 + deep
                    n = have.get((q, deep))
                    value = zero if n is None else half[n, row : row + 1, :]
                    out[i * EXT + at : i * EXT + at + 1, :] = value
    for out in (up, dn):
        out[COUNT * EXT : COUNT * EXT + 4, :] = jnp.zeros((4, 128), F32)


def join(left, right, yup, ydn):
    side = jax.ShapeDtypeStruct((COUNT * EXT + 4, 128), F32)
    vmem = pl.BlockSpec(memory_space=pltpu.VMEM)
    return pl.pallas_call(
        join_kernel,
        out_shape=[side] * 2,
        in_specs=[vmem] * 4,
        out_specs=[vmem] * 2,
        compiler_params=pltpu.CompilerParams(vmem_limit_bytes=VMEM_LIMIT),
        cost_estimate=pl.CostEstimate(flops=0, bytes_accessed=1_000_000, transcendentals=0),
    )(left, right, yup, ydn)


def second_kernel(force, post, coef, left, right, below, above, out, wide, wcoef, again, sem):
    own = pltpu.make_async_copy(post, wide.at[:, pl.ds(2, 16), pl.ds(8, 16), :], sem)
    own.start()
    for x in range(16):
        for j in range(2):
            wcoef[j, x + 1, 8:24, :] = coef[j, x]
    for half, sign in ((left, 1), (right, -1)):
        for i, (q, layer) in enumerate(entries(0, sign)):
            wide[q, 1 - layer if sign == 1 else 18 + layer, 8:24, :] = half[i]
        for j in range(2):
            wcoef[j, 0 if sign == 1 else 17, 8:24, :] = half[19 + j]
    for half, sign in ((below, 1), (above, -1)):
        for i, (q, layer) in enumerate(entries(1, sign)):
            row = 7 - layer if sign == 1 else 24 + layer
            for x in range(EXT):
                wide[q, x, row : row + 1, :] = half[i * EXT + x : i * EXT + x + 1, :]
        row = 7 if sign == 1 else 24
        for j in range(2):
            for x in range(18):
                at = (19 + j) * EXT + x + 1
                wcoef[j, x, row : row + 1, :] = half[at : at + 1, :]
    f = [force[axis] for axis in range(3)]
    own.wait()

    def plane(x, _):
        for block in range(3):
            dist = []
            for q in range(19):
                cx, cy, _z = VELOCITY[q]
                dist.append(wide[q, x + 1 - cx, 7 + 8 * block - cy : 15 + 8 * block - cy, :])
            rows = slice(7 + 8 * block, 15 + 8 * block)
            after = collide(dist, wcoef[0, x, rows, :], wcoef[1, x, rows, :], f)
            for q in range(19):
                again[q, x, 8 * block : 8 * block + 8, :] = shift_z(after[q], q)
        return 0

    lax.fori_loop(0, 18, plane, 0)

    def finish(x, _):
        for q in range(19):
            cx, cy, _z = VELOCITY[q]
            for block in range(2):
                start = 8 * block + 1 - cy
                value = again[q, x + 1 - cx, start : start + 8, :]
                out[q, x, 8 * block : 8 * block + 8, :] = value * INVERSE[q] - 1.0
        return 0

    lax.fori_loop(0, 16, finish, 0)


def second(force, post, coef, left, right, below, above):
    vmem = pl.BlockSpec(memory_space=pltpu.VMEM)
    smem = pl.BlockSpec(memory_space=pltpu.SMEM)
    return pl.pallas_call(
        second_kernel,
        out_shape=jax.ShapeDtypeStruct((19, 16, 16, 128), F32),
        in_specs=[smem, pl.BlockSpec(memory_space=pl.ANY)] + [vmem] * 5,
        out_specs=vmem,
        scratch_shapes=[
            pltpu.VMEM((19, EXT, 32, 128), F32),
            pltpu.VMEM((2, 18, 32, 128), F32),
            pltpu.VMEM((19, 18, 24, 128), F32),
            pltpu.SemaphoreType.DMA,
        ],
        compiler_params=pltpu.CompilerParams(vmem_limit_bytes=VMEM_LIMIT),
        cost_estimate=pl.CostEstimate(flops=10_000_000, bytes_accessed=8_000_000, transcendentals=0),
    )(force, post, coef, left, right, below, above)


def ring(axis, step):
    n = lax.axis_size(axis)
    return [(i, (i + step) % n) for i in range(n)]


def blocks_of(porosity, relaxation):
    b = lax.axis_index("gy")
    hi, lo = b // 4, b % 4
    slab = jnp.stack([porosity, relaxation]).reshape(2, 2, 8, 16, 128)
    other = lax.dynamic_slice_in_dim(slab, (1 - hi) * 4, 4, axis=2)
    mine = lax.dynamic_slice_in_dim(slab, hi * 4, 4, axis=2)
    came = lax.ppermute(other, "gy", [(i, i ^ 4) for i in range(8)])
    first_ = jnp.where(hi == 0, mine, came)
    last = jnp.where(hi == 0, came, mine)
    both = jnp.stack([first_, last])
    parts = [lax.dynamic_index_in_dim(both, lo, axis=3, keepdims=False)]
    for k in range(1, 4):
        message = lax.dynamic_index_in_dim(both, (lo + k) % 4, axis=3, keepdims=False)
        pairs = [(i, (i // 4) * 4 + (i % 4 + k) % 4) for i in range(8)]
        parts.append(lax.ppermute(message, "gy", pairs))
    stacked = jnp.stack(parts)
    ordered = [
        lax.dynamic_index_in_dim(stacked, (lo - y + 4) % 4, axis=0, keepdims=False)
        for y in range(4)
    ]
    whole = jnp.stack(ordered)
    return whole.transpose(2, 1, 0, 3, 4, 5).reshape(2, 16, 16, 128)


def local(pdf_old, tile_target, porosity, relaxation, solid_mask, force):
    packed = pack(tile_target, pdf_old.transpose(1, 0, 2))
    arrived = lax.all_to_all(
        packed.reshape(DEVICES, CAP * ROWS, 128),
        ("gx", "gy"),
        split_axis=0,
        concat_axis=0,
        tiled=True,
    ).reshape(DEVICES * CAP * ROWS, 128)
    block = blocks_of(porosity, relaxation)
    solid = block[0] + solid_mask.astype(F32) * (1.0 - block[0])
    coef = jnp.stack([solid, block[1]])
    label = arrived.reshape(DEVICES * CAP, ROWS, 128)[:, 38, 0]
    hit = label[:, None] == jnp.arange(HELD, dtype=F32)[None, :]
    number = jnp.arange(DEVICES * CAP, dtype=jnp.int32)[:, None]
    source = jnp.sum(jnp.where(hit, number, 0), axis=0)
    post, xup, xdn, yup, ydn = first(source, force, arrived, coef)
    left = lax.ppermute(xup, "gx", ring("gx", 1))
    right = lax.ppermute(xdn, "gx", ring("gx", -1))
    up, dn = join(left, right, yup, ydn)
    below = lax.ppermute(up, "gy", ring("gy", 1))
    above = lax.ppermute(dn, "gy", ring("gy", -1))
    return second(force, post, coef, left, right, below, above)


def solution(mesh):
    return jax.shard_map(
        local,
        mesh=mesh,
        in_specs=(
            P(("gx", "gy"), None, None),
            P(("gx", "gy")),
            P(("gx", "gy"), None, None),
            P(("gx", "gy"), None, None),
            P("gx", "gy", None),
            P(),
        ),
        out_specs=P(None, "gx", "gy", None),
        check_vma=False,
    )
```

```python
import jax
import jax.numpy as jnp
from jax import lax
from jax.experimental import pallas as pl
from jax.experimental.pallas import tpu as pltpu
from jax.sharding import PartitionSpec as P

VELOCITY = (
    (0, 0, 0),
    (1, 0, 0),
    (-1, 0, 0),
    (0, 1, 0),
    (0, -1, 0),
    (0, 0, 1),
    (0, 0, -1),
    (1, 1, 0),
    (-1, -1, 0),
    (1, -1, 0),
    (-1, 1, 0),
    (1, 0, 1),
    (-1, 0, -1),
    (1, 0, -1),
    (-1, 0, 1),
    (0, 1, 1),
    (0, -1, -1),
    (0, 1, -1),
    (0, -1, 1),
)
WEIGHT = [1.0 / 3.0] + [1.0 / 18.0] * 6 + [1.0 / 36.0] * 12
INVERSE = [3.0] + [18.0] * 6 + [36.0] * 12
DEVICES = 128
HELD = 128
CAP = 2
TILE = 38
PAIR = 2 * TILE + 1
ROWS = 40
EXT = 20
VMEM_LIMIT = 48 * 1024 * 1024
VMEM_MOST = 61 * 1024 * 1024
F32 = jnp.float32


def entries(axis, sign):
    far = [(q, 1) for q in range(19) if VELOCITY[q][axis] == sign]
    near = [(q, 0) for q in range(19) if VELOCITY[q][axis] in (0, sign)]
    return far + near


COUNT = 21


def collide(dist, solid, omega, force):
    plus = [None] * 19
    minus = [None] * 19
    for i in range(1, 19, 2):
        plus[i] = dist[i] + dist[i + 1]
        minus[i] = dist[i] - dist[i + 1]
    density = dist[0]
    for i in range(1, 19, 2):
        density = density + plus[i]
    flow = []
    for axis in range(3):
        total = None
        for i in range(1, 19, 2):
            c = VELOCITY[i][axis]
            if c:
                if total is None:
                    total = minus[i]
                else:
                    total = total + minus[i] if c == 1 else total - minus[i]
        flow.append(total + 0.5 * force[axis])
    base = density - 1.5 * (flow[0] * flow[0] + flow[1] * flow[1] + flow[2] * flow[2])
    open_ = 1.0 - solid
    a = open_ * omega
    b = open_ * ((2.0 - omega) / (1.0 - 0.125 * omega))
    keep = 0.5 - 0.5 * a
    turn = 0.5 - solid - 0.5 * b
    post = [None] * 19
    at = a * base
    post[0] = (keep + keep) * dist[0] + at * (1.0 / 3.0)
    drive = [b * flow[axis] + open_ * force[axis] for axis in range(3)]
    for group, w in ((range(1, 7, 2), 1.0 / 18.0), (range(7, 19, 2), 1.0 / 36.0)):
        even_base = at * w
        square = a * (4.5 * w)
        pull = [drive[axis] * (3.0 * w) for axis in range(3)]
        for i in group:
            along = None
            odd = None
            for axis in range(3):
                c = VELOCITY[i][axis]
                if c:
                    if along is None:
                        along, odd = flow[axis], pull[axis]
                    elif c == 1:
                        along, odd = along + flow[axis], odd + pull[axis]
                    else:
                        along, odd = along - flow[axis], odd - pull[axis]
            even = keep * plus[i] + (even_base + square * (along * along))
            odd = turn * minus[i] + odd
            post[i] = even + odd
            post[i + 1] = even - odd
    return post


def shift_z(value, q):
    c = VELOCITY[q][2]
    return value if c == 0 else pltpu.roll(value, c % 128, 1)


def pack_kernel(target_hbm, pdf_hbm, out_hbm, target, used, pdf, out3, sems, small):
    listing = pltpu.make_async_copy(target_hbm, target, small.at[0])
    listing.start()
    quarters = []
    for part in range(4):
        rows = pl.ds(part * 64, 64)
        copy = pltpu.make_async_copy(pdf_hbm.at[:, rows, :], pdf.at[:, rows, :], sems.at[part])
        copy.start()
        quarters.append(copy)
    flat = pdf.reshape(19 * 256, 128)
    out = out3.reshape(DEVICES * PAIR, 128)

    empty = jnp.full((1, 128), -1.0, F32)

    def clear(i, _):
        used[i] = 0
        out[pl.ds(i * PAIR + 2 * TILE, 1), :] = empty
        return 0

    lax.fori_loop(0, DEVICES, clear, 0, unroll=8)
    half = lax.broadcasted_iota(jnp.int32, (1, 128), 1) // 64
    listing.wait()

    def place(k, _):
        t = target[k]
        owner = lax.shift_right_logical(t, 7)
        rank = used[owner]
        used[owner] = rank + 1
        start = owner * PAIR + rank * TILE
        near = lax.shift_right_logical(k, 3) * 16 + (k & 7)
        for r in range(2):
            for q in (0, 8, 16):
                n = min(8, 19 - q)
                value = flat[pl.ds(near + r * 8 + q * 256, n, stride=256), :]
                out[pl.ds(start + r * 19 + q, n), :] = value
        line = pl.ds(owner * PAIR + 2 * TILE, 1)
        out[line, :] = jnp.where(half == rank, (t & 127).astype(F32), out[line, :])
        return 0

    for part in range(4):
        quarters[part].wait()
        lax.fori_loop(part * 32, part * 32 + 32, place, 0, unroll=4)
    done = pltpu.make_async_copy(out3, out_hbm, small.at[1])
    done.start()
    done.wait()


def pack(target, pdf):
    hbm = pl.BlockSpec(memory_space=pltpu.HBM)
    return pl.pallas_call(
        pack_kernel,
        out_shape=jax.ShapeDtypeStruct((DEVICES * PAIR, 1, 128), F32),
        in_specs=[hbm, hbm],
        out_specs=hbm,
        scratch_shapes=[
            pltpu.SMEM((HELD,), jnp.int32),
            pltpu.SMEM((DEVICES,), jnp.int32),
            pltpu.VMEM((19, 256, 128), F32),
            pltpu.VMEM((DEVICES * PAIR, 1, 128), F32),
            pltpu.SemaphoreType.DMA((4,)),
            pltpu.SemaphoreType.DMA((2,)),
        ],
        compiler_params=pltpu.CompilerParams(vmem_limit_bytes=VMEM_MOST),
        cost_estimate=pl.CostEstimate(flops=0, bytes_accessed=8_000_000, transcendentals=0),
    )(target, pdf)


def first_kernel(force, arrived, coef, post, xup, xdn, yup, ydn, tiles, labels, found, source, sems, small):
    pull = pltpu.make_async_copy(arrived.at[:, 2 * TILE, 0, :], labels, small.at[0])
    pull.start()
    pull.wait()
    lane = lax.broadcasted_iota(jnp.int32, (8, 128), 1)
    lane_f = lane.astype(F32)
    sub = lax.broadcasted_iota(jnp.int32, (8, 128), 0)
    low = lane < 64
    total = jnp.zeros((8, 128), jnp.int32)
    for group in range(DEVICES // 8):
        line = labels[8 * group : 8 * group + 8, :]
        other = pltpu.roll(line, 64, 1)
        number = (sub + 8 * group) * 2
        total = total + jnp.where(jnp.where(low, line, other) == lane_f, number, 0)
        total = total + jnp.where(jnp.where(low, other, line) == lane_f, number + 1, 0)
    found[...] = jnp.broadcast_to(jnp.sum(total, axis=0, keepdims=True), (8, 128))
    hand = pltpu.make_async_copy(found, source, small.at[1])
    hand.start()
    hand.wait()

    def fetch(s, _):
        p = source[0, s]
        pltpu.make_async_copy(
            arrived.at[lax.shift_right_logical(p, 1), pl.ds((p & 1) * TILE, TILE), 0, :],
            tiles.at[pl.ds(pl.multiple_of(s * ROWS, 8), TILE), :],
            sems.at[lax.shift_right_logical(s, 3)],
        ).start()
        return 0

    lax.fori_loop(0, HELD, fetch, 0, unroll=4)
    f = [force[axis] for axis in range(3)]

    def plane(x, _):
        whole = tiles.at[pl.ds(0, 8 * TILE), :]
        pltpu.make_async_copy(whole, whole, sems.at[x]).wait()
        for r in range(2):
            dist = []
            for q in range(19):
                value = tiles[pl.ds(x * (8 * ROWS) + r * 19 + q, 8, stride=ROWS), :]
                dist.append(WEIGHT[q] * value + WEIGHT[q])
            solid = coef[0, x, pl.ds(r, 8, stride=2), :]
            omega = coef[1, x, pl.ds(r, 8, stride=2), :]
            after = collide(dist, solid, omega, f)
            for q in range(19):
                post[q, x, pl.ds(r, 8, stride=2), :] = shift_z(after[q], q)
        return 0

    lax.fori_loop(0, 16, plane, 0)
    for out, sign in ((xup, 1), (xdn, -1)):
        for i, (q, layer) in enumerate(entries(0, sign)):
            out[i] = post[q, 15 - layer if sign == 1 else layer]
        for j in range(2):
            out[19 + j] = coef[j, 15 if sign == 1 else 0]
    for out, sign in ((yup, 1), (ydn, -1)):
        for i, (q, layer) in enumerate(entries(1, sign)):
            row = 15 - layer if sign == 1 else layer
            for x in range(16):
                out[i, x : x + 1, :] = post[q, x, row : row + 1, :]
        row = 15 if sign == 1 else 0
        for j in range(2):
            for x in range(16):
                out[19 + j, x : x + 1, :] = coef[j, x, row : row + 1, :]


def first(force, arrived, coef):
    face = jax.ShapeDtypeStruct((COUNT, 16, 128), F32)
    vmem = pl.BlockSpec(memory_space=pltpu.VMEM)
    smem = pl.BlockSpec(memory_space=pltpu.SMEM)
    return pl.pallas_call(
        first_kernel,
        out_shape=[jax.ShapeDtypeStruct((19, 16, 16, 128), F32)] + [face] * 4,
        in_specs=[smem, pl.BlockSpec(memory_space=pltpu.HBM), vmem],
        out_specs=[vmem] * 5,
        scratch_shapes=[
            pltpu.VMEM((HELD * ROWS, 128), F32),
            pltpu.VMEM((DEVICES, 128), F32),
            pltpu.VMEM((8, 128), jnp.int32),
            pltpu.SMEM((8, 128), jnp.int32),
            pltpu.SemaphoreType.DMA((16,)),
            pltpu.SemaphoreType.DMA((2,)),
        ],
        compiler_params=pltpu.CompilerParams(vmem_limit_bytes=VMEM_LIMIT),
        cost_estimate=pl.CostEstimate(flops=10_000_000, bytes_accessed=8_000_000, transcendentals=0),
    )(force, arrived, coef)


def join_kernel(left, right, yup, ydn, up, dn):
    zero = jnp.zeros((1, 128), F32)
    for own, out, sign in ((yup, up, 1), (ydn, dn, -1)):
        listed = entries(1, sign) + [(19, 0), (20, 0)]
        for i, (q, layer) in enumerate(listed):
            row = 15 - layer if sign == 1 else layer
            out[i * EXT + 2 : i * EXT + 18, :] = own[i]
            for half, toward in ((left, 1), (right, -1)):
                have = {e: n for n, e in enumerate(entries(0, toward) + [(19, 0), (20, 0)])}
                for deep in range(2):
                    at = (1 - deep) if toward == 1 else 18 + deep
                    n = have.get((q, deep))
                    value = zero if n is None else half[n, row : row + 1, :]
                    out[i * EXT + at : i * EXT + at + 1, :] = value
    for out in (up, dn):
        out[COUNT * EXT : COUNT * EXT + 4, :] = jnp.zeros((4, 128), F32)


def join(left, right, yup, ydn):
    side = jax.ShapeDtypeStruct((COUNT * EXT + 4, 128), F32)
    vmem = pl.BlockSpec(memory_space=pltpu.VMEM)
    return pl.pallas_call(
        join_kernel,
        out_shape=[side] * 2,
        in_specs=[vmem] * 4,
        out_specs=[vmem] * 2,
        compiler_params=pltpu.CompilerParams(vmem_limit_bytes=VMEM_LIMIT),
        cost_estimate=pl.CostEstimate(flops=0, bytes_accessed=1_000_000, transcendentals=0),
    )(left, right, yup, ydn)


def second_kernel(force, post, coef, left, right, below, above, out, wide, wcoef, again, result, sem, sems):
    own = pltpu.make_async_copy(post, wide.at[:, pl.ds(2, 16), pl.ds(8, 16), :], sem)
    own.start()
    for x in range(16):
        for j in range(2):
            wcoef[j, x + 1, 8:24, :] = coef[j, x]
    for half, sign in ((left, 1), (right, -1)):
        for i, (q, layer) in enumerate(entries(0, sign)):
            wide[q, 1 - layer if sign == 1 else 18 + layer, 8:24, :] = half[i]
        for j in range(2):
            wcoef[j, 0 if sign == 1 else 17, 8:24, :] = half[19 + j]
    for half, sign in ((below, 1), (above, -1)):
        for i, (q, layer) in enumerate(entries(1, sign)):
            row = 7 - layer if sign == 1 else 24 + layer
            for x in range(EXT):
                wide[q, x, row : row + 1, :] = half[i * EXT + x : i * EXT + x + 1, :]
        row = 7 if sign == 1 else 24
        for j in range(2):
            for x in range(18):
                at = (19 + j) * EXT + x + 1
                wcoef[j, x, row : row + 1, :] = half[at : at + 1, :]
    f = [force[axis] for axis in range(3)]
    own.wait()

    def plane(x, _):
        for block in range(3):
            dist = []
            for q in range(19):
                cx, cy, _z = VELOCITY[q]
                dist.append(wide[q, x + 1 - cx, 7 + 8 * block - cy : 15 + 8 * block - cy, :])
            rows = slice(7 + 8 * block, 15 + 8 * block)
            after = collide(dist, wcoef[0, x, rows, :], wcoef[1, x, rows, :], f)
            for q in range(19):
                again[q, x, 8 * block : 8 * block + 8, :] = shift_z(after[q], q)
        return 0

    lax.fori_loop(0, 18, plane, 0)

    def finish(x, _):
        for q in range(19):
            cx, cy, _z = VELOCITY[q]
            for block in range(2):
                start = 8 * block + 1 - cy
                value = again[q, x + 1 - cx, start : start + 8, :]
                result[x, q, 8 * block : 8 * block + 8, :] = value * INVERSE[q] - 1.0
        pltpu.make_async_copy(result.at[x], out.at[:, x], sems.at[x]).start()
        return 0

    lax.fori_loop(0, 16, finish, 0)
    for x in range(16):
        pltpu.make_async_copy(result.at[x], out.at[:, x], sems.at[x]).wait()


def second(force, post, coef, left, right, below, above):
    vmem = pl.BlockSpec(memory_space=pltpu.VMEM)
    smem = pl.BlockSpec(memory_space=pltpu.SMEM)
    return pl.pallas_call(
        second_kernel,
        out_shape=jax.ShapeDtypeStruct((19, 16, 16, 128), F32),
        in_specs=[smem, pl.BlockSpec(memory_space=pl.ANY)] + [vmem] * 5,
        out_specs=pl.BlockSpec(memory_space=pltpu.HBM),
        scratch_shapes=[
            pltpu.VMEM((19, EXT, 32, 128), F32),
            pltpu.VMEM((2, 18, 32, 128), F32),
            pltpu.VMEM((19, 18, 24, 128), F32),
            pltpu.VMEM((16, 19, 16, 128), F32),
            pltpu.SemaphoreType.DMA,
            pltpu.SemaphoreType.DMA((16,)),
        ],
        compiler_params=pltpu.CompilerParams(vmem_limit_bytes=VMEM_LIMIT),
        cost_estimate=pl.CostEstimate(flops=10_000_000, bytes_accessed=8_000_000, transcendentals=0),
    )(force, post, coef, left, right, below, above)


def ring(axis, step):
    n = lax.axis_size(axis)
    return [(i, (i + step) % n) for i in range(n)]


def halves_of(porosity, relaxation):
    hi = lax.axis_index("gy") // 4
    slab = jnp.stack([porosity, relaxation]).reshape(2, 2, 8, 16, 128)
    other = lax.dynamic_slice_in_dim(slab, (1 - hi) * 4, 4, axis=2)
    mine = lax.dynamic_slice_in_dim(slab, hi * 4, 4, axis=2)
    return mine, lax.ppermute(other, "gy", [(i, i ^ 4) for i in range(8)])


def blocks_of(mine, came):
    b = lax.axis_index("gy")
    hi, lo = b // 4, b % 4
    both = jnp.stack([jnp.where(hi == 0, mine, came), jnp.where(hi == 0, came, mine)])
    parts = [lax.dynamic_index_in_dim(both, lo, axis=3, keepdims=False)]
    for k in range(1, 4):
        message = lax.dynamic_index_in_dim(both, lo ^ k, axis=3, keepdims=False)
        parts.append(lax.ppermute(message, "gy", [(i, i ^ k) for i in range(8)]))
    stacked = jnp.stack(parts)
    ordered = [
        lax.dynamic_index_in_dim(stacked, lo ^ y, axis=0, keepdims=False) for y in range(4)
    ]
    whole = jnp.stack(ordered)
    return whole.transpose(2, 1, 0, 3, 4, 5).reshape(2, 16, 16, 128)


def local(pdf_old, tile_target, porosity, relaxation, solid_mask, force):
    mine, came = halves_of(porosity, relaxation)
    rows = pdf_old.reshape(16, 8, 19, 2, 128).transpose(2, 0, 3, 1, 4).reshape(19, 256, 128)
    packed = pack(tile_target, rows)
    packed, came = lax.optimization_barrier((packed, came))
    arrived = lax.all_to_all(
        packed.reshape(DEVICES, PAIR, 1, 128), ("gx", "gy"), split_axis=0, concat_axis=0, tiled=True
    )
    block = blocks_of(mine, came)
    solid = block[0] + solid_mask.astype(F32) * (1.0 - block[0])
    coef = jnp.stack([solid, block[1]])
    post, xup, xdn, yup, ydn = first(force, arrived, coef)
    left = lax.ppermute(xup, "gx", ring("gx", 1))
    right = lax.ppermute(xdn, "gx", ring("gx", -1))
    up, dn = join(left, right, yup, ydn)
    below = lax.ppermute(up, "gy", ring("gy", 1))
    above = lax.ppermute(dn, "gy", ring("gy", -1))
    return second(force, post, coef, left, right, below, above)


def solution(mesh):
    return jax.shard_map(
        local,
        mesh=mesh,
        in_specs=(
            P(("gx", "gy"), None, None),
            P(("gx", "gy")),
            P(("gx", "gy"), None, None),
            P(("gx", "gy"), None, None),
            P("gx", "gy", None),
            P(),
        ),
        out_specs=P(None, "gx", "gy", None),
        check_vma=False,
    )
```

```python
import jax
import jax.numpy as jnp
from jax import lax
from jax.experimental import pallas as pl
from jax.experimental.pallas import tpu as pltpu
from jax.sharding import PartitionSpec as P

VELOCITY = (
    (0, 0, 0),
    (1, 0, 0),
    (-1, 0, 0),
    (0, 1, 0),
    (0, -1, 0),
    (0, 0, 1),
    (0, 0, -1),
    (1, 1, 0),
    (-1, -1, 0),
    (1, -1, 0),
    (-1, 1, 0),
    (1, 0, 1),
    (-1, 0, -1),
    (1, 0, -1),
    (-1, 0, 1),
    (0, 1, 1),
    (0, -1, -1),
    (0, 1, -1),
    (0, -1, 1),
)
WEIGHT = [1.0 / 3.0] + [1.0 / 18.0] * 6 + [1.0 / 36.0] * 12
INVERSE = [3.0] + [18.0] * 6 + [36.0] * 12
DEVICES = 128
HELD = 128
CAP = 2
TILE = 38
PAIR = 2 * TILE + 1
ROWS = 40
EXT = 20
VMEM_LIMIT = 48 * 1024 * 1024
VMEM_MOST = 61 * 1024 * 1024
F32 = jnp.float32


def entries(axis, sign):
    far = [(q, 1) for q in range(19) if VELOCITY[q][axis] == sign]
    near = [(q, 0) for q in range(19) if VELOCITY[q][axis] in (0, sign)]
    return far + near


COUNT = 21
SIDE_ROWS = 432


def collide(dist, solid, omega, force):
    plus = [None] * 19
    minus = [None] * 19
    for i in range(1, 19, 2):
        plus[i] = dist[i] + dist[i + 1]
        minus[i] = dist[i] - dist[i + 1]
    density = dist[0]
    for i in range(1, 19, 2):
        density = density + plus[i]
    flow = []
    for axis in range(3):
        total = None
        for i in range(1, 19, 2):
            c = VELOCITY[i][axis]
            if c:
                if total is None:
                    total = minus[i]
                else:
                    total = total + minus[i] if c == 1 else total - minus[i]
        flow.append(total + 0.5 * force[axis])
    base = density - 1.5 * (flow[0] * flow[0] + flow[1] * flow[1] + flow[2] * flow[2])
    open_ = 1.0 - solid
    a = open_ * omega
    b = open_ * ((2.0 - omega) / (1.0 - 0.125 * omega))
    keep = 0.5 - 0.5 * a
    turn = 0.5 - solid - 0.5 * b
    post = [None] * 19
    at = a * base
    post[0] = (keep + keep) * dist[0] + at * (1.0 / 3.0)
    drive = [b * flow[axis] + open_ * force[axis] for axis in range(3)]
    for group, w in ((range(1, 7, 2), 1.0 / 18.0), (range(7, 19, 2), 1.0 / 36.0)):
        even_base = at * w
        square = a * (4.5 * w)
        pull = [drive[axis] * (3.0 * w) for axis in range(3)]
        for i in group:
            along = None
            odd = None
            for axis in range(3):
                c = VELOCITY[i][axis]
                if c:
                    if along is None:
                        along, odd = flow[axis], pull[axis]
                    elif c == 1:
                        along, odd = along + flow[axis], odd + pull[axis]
                    else:
                        along, odd = along - flow[axis], odd - pull[axis]
            even = keep * plus[i] + (even_base + square * (along * along))
            odd = turn * minus[i] + odd
            post[i] = even + odd
            post[i + 1] = even - odd
    return post


def shift_z(value, q):
    c = VELOCITY[q][2]
    return value if c == 0 else pltpu.roll(value, c % 128, 1)


def pack_kernel(target_hbm, pdf_hbm, out_hbm, target, used, pdf, out3, sems, small):
    listing = pltpu.make_async_copy(target_hbm, target, small.at[0])
    listing.start()
    quarters = []
    for part in range(4):
        rows = pl.ds(part * 64, 64)
        copy = pltpu.make_async_copy(pdf_hbm.at[:, rows, :], pdf.at[:, rows, :], sems.at[part])
        copy.start()
        quarters.append(copy)
    flat = pdf.reshape(19 * 256, 128)
    out = out3.reshape(DEVICES * PAIR, 128)

    empty = jnp.full((1, 128), -1.0, F32)

    def clear(i, _):
        used[i] = 0
        out[pl.ds(i * PAIR + 2 * TILE, 1), :] = empty
        return 0

    lax.fori_loop(0, DEVICES, clear, 0, unroll=8)
    half = lax.broadcasted_iota(jnp.int32, (1, 128), 1) // 64
    listing.wait()

    def put(k, _):
        t = target[k]
        owner = lax.shift_right_logical(t, 7)
        rank = used[owner]
        used[owner] = rank + 1
        start = owner * PAIR + rank * TILE
        near = lax.shift_right_logical(k, 3) * 16 + (k & 7)
        for r in range(2):
            for q in (0, 8, 16):
                n = min(8, 19 - q)
                value = flat[pl.ds(near + r * 8 + q * 256, n, stride=256), :]
                out[pl.ds(start + r * 19 + q, n), :] = value
        line = pl.ds(owner * PAIR + 2 * TILE, 1)
        out[line, :] = jnp.where(half == rank, (t & 127).astype(F32), out[line, :])
        return 0

    for part in range(4):
        quarters[part].wait()
        lax.fori_loop(part * 32, part * 32 + 32, put, 0, unroll=4)
    done = pltpu.make_async_copy(out3, out_hbm, small.at[1])
    done.start()
    done.wait()


def pack(target, pdf):
    hbm = pl.BlockSpec(memory_space=pltpu.HBM)
    return pl.pallas_call(
        pack_kernel,
        out_shape=jax.ShapeDtypeStruct((DEVICES * PAIR, 1, 128), F32),
        in_specs=[hbm, hbm],
        out_specs=hbm,
        scratch_shapes=[
            pltpu.SMEM((HELD,), jnp.int32),
            pltpu.SMEM((DEVICES,), jnp.int32),
            pltpu.VMEM((19, 256, 128), F32),
            pltpu.VMEM((DEVICES * PAIR, 1, 128), F32),
            pltpu.SemaphoreType.DMA((4,)),
            pltpu.SemaphoreType.DMA((2,)),
        ],
        compiler_params=pltpu.CompilerParams(vmem_limit_bytes=VMEM_MOST),
        cost_estimate=pl.CostEstimate(flops=0, bytes_accessed=8_000_000, transcendentals=0),
    )(target, pdf)


def place_kernel(arrived, tiles, labels, found, source, sem, small):
    pull = pltpu.make_async_copy(arrived.at[:, 2 * TILE, 0, :], labels, small.at[0])
    pull.start()
    pull.wait()
    lane = lax.broadcasted_iota(jnp.int32, (8, 128), 1)
    lane_f = lane.astype(F32)
    sub = lax.broadcasted_iota(jnp.int32, (8, 128), 0)
    low = lane < 64
    total = jnp.zeros((8, 128), jnp.int32)
    for group in range(DEVICES // 8):
        line = labels[8 * group : 8 * group + 8, :]
        other = pltpu.roll(line, 64, 1)
        number = (sub + 8 * group) * 2
        total = total + jnp.where(jnp.where(low, line, other) == lane_f, number, 0)
        total = total + jnp.where(jnp.where(low, other, line) == lane_f, number + 1, 0)
    found[...] = jnp.broadcast_to(jnp.sum(total, axis=0, keepdims=True), (8, 128))
    hand = pltpu.make_async_copy(found, source, small.at[1])
    hand.start()
    hand.wait()

    def fetch(s, _):
        p = source[0, s]
        pltpu.make_async_copy(
            arrived.at[lax.shift_right_logical(p, 1), pl.ds((p & 1) * TILE, TILE), 0, :],
            tiles.at[pl.ds(pl.multiple_of(s * ROWS, 8), TILE), :],
            sem,
        ).start()
        return 0

    lax.fori_loop(0, HELD, fetch, 0, unroll=8)
    whole = tiles.at[pl.ds(0, HELD * TILE), :]
    pltpu.make_async_copy(whole, whole, sem).wait()


def place(arrived):
    return pl.pallas_call(
        place_kernel,
        out_shape=jax.ShapeDtypeStruct((HELD * ROWS, 128), F32),
        in_specs=[pl.BlockSpec(memory_space=pltpu.HBM)],
        out_specs=pl.BlockSpec(memory_space=pltpu.VMEM),
        scratch_shapes=[
            pltpu.VMEM((DEVICES, 128), F32),
            pltpu.VMEM((8, 128), jnp.int32),
            pltpu.SMEM((8, 128), jnp.int32),
            pltpu.SemaphoreType.DMA,
            pltpu.SemaphoreType.DMA((2,)),
        ],
        compiler_params=pltpu.CompilerParams(vmem_limit_bytes=VMEM_LIMIT),
        cost_estimate=pl.CostEstimate(flops=0, bytes_accessed=8_000_000, transcendentals=0),
    )(arrived)


def pick(flag, even, odd):
    return jnp.where(flag == 0, even, odd)


def plane_step(x, at, tiles, coef, post, f):
    for r in range(2):
        dist = []
        for q in range(19):
            value = tiles[pl.ds(x * (8 * ROWS) + r * 19 + q, 8, stride=ROWS), :]
            dist.append(WEIGHT[q] * value + WEIGHT[q])
        solid = coef[0, x, pl.ds(r, 8, stride=2), :]
        omega = coef[1, x, pl.ds(r, 8, stride=2), :]
        after = collide(dist, solid, omega, f)
        for q in range(19):
            post[q, at, pl.ds(r, 8, stride=2), :] = shift_z(after[q], q)


def edge_kernel(force, odd, tiles, coef, edge, xe, xo):
    f = [force[axis] for axis in range(3)]

    def plane(j, _):
        plane_step(jnp.where(j < 2, j, j + 12), j, tiles, coef, edge, f)
        return 0

    lax.fori_loop(0, 4, plane, 0)
    flag = odd[0]
    for i, ((qu, lu), (qd, ld)) in enumerate(zip(entries(0, 1), entries(0, -1))):
        up, dn = edge[qu, 3 - lu], edge[qd, ld]
        xe[i] = pick(flag, up, dn)
        xo[i] = pick(flag, dn, up)
    for j in range(2):
        up, dn = coef[j, 15], coef[j, 0]
        xe[19 + j] = pick(flag, up, dn)
        xo[19 + j] = pick(flag, dn, up)


def inner_kernel(force, tiles, coef, edge, inner, yup, ydn):
    f = [force[axis] for axis in range(3)]

    def plane(j, _):
        plane_step(j + 2, j, tiles, coef, inner, f)
        return 0

    lax.fori_loop(0, 12, plane, 0)
    for out, sign in ((yup, 1), (ydn, -1)):
        for i, (q, layer) in enumerate(entries(1, sign)):
            row = 15 - layer if sign == 1 else layer
            for x in range(16):
                if 2 <= x < 14:
                    value = inner[q, x - 2, row : row + 1, :]
                else:
                    value = edge[q, x if x < 2 else x - 12, row : row + 1, :]
                out[i, x : x + 1, :] = value
        row = 15 if sign == 1 else 0
        for j in range(2):
            for x in range(16):
                out[19 + j, x : x + 1, :] = coef[j, x, row : row + 1, :]


VMEM_SPEC = pl.BlockSpec(memory_space=pltpu.VMEM)
SMEM_SPEC = pl.BlockSpec(memory_space=pltpu.SMEM)
FACE = jax.ShapeDtypeStruct((COUNT, 16, 128), F32)
SIDE = jax.ShapeDtypeStruct((SIDE_ROWS, 128), F32)


def call(kernel, out_shape, operands, work, scalars=1, **more):
    return pl.pallas_call(
        kernel,
        out_shape=out_shape,
        in_specs=[SMEM_SPEC] * scalars + [VMEM_SPEC] * (len(operands) - scalars),
        compiler_params=pltpu.CompilerParams(vmem_limit_bytes=VMEM_LIMIT),
        cost_estimate=pl.CostEstimate(flops=work, bytes_accessed=work, transcendentals=0),
        **more,
    )(*operands)


def join_kernel(odd, xe, xo, yup, ydn, ye, yo):
    fx, fy = odd[0], odd[1]
    lists = [entries(1, sign) + [(19, 0), (20, 0)] for sign in (1, -1)]
    have = [
        {e: n for n, e in enumerate(entries(0, toward) + [(19, 0), (20, 0)])} for toward in (1, -1)
    ]

    def corner(direction, i, toward, deep):
        q, layer = lists[direction][i]
        n = have[toward].get((q, deep))
        if n is None:
            return jnp.zeros((1, 128), F32)
        row = 15 - layer if direction == 0 else layer
        even, odd_ = (xo, xe) if toward == 0 else (xe, xo)
        return pick(fx, even[n, row : row + 1, :], odd_[n, row : row + 1, :])

    for i in range(COUNT):
        up, dn = yup[i], ydn[i]
        ye[i * EXT + 2 : i * EXT + 18, :] = pick(fy, up, dn)
        yo[i * EXT + 2 : i * EXT + 18, :] = pick(fy, dn, up)
        for toward in range(2):
            for deep in range(2):
                at = i * EXT + ((1 - deep) if toward == 0 else 18 + deep)
                up, dn = corner(0, i, toward, deep), corner(1, i, toward, deep)
                ye[at : at + 1, :] = pick(fy, up, dn)
                yo[at : at + 1, :] = pick(fy, dn, up)
    for out in (ye, yo):
        out[COUNT * EXT : SIDE_ROWS, :] = jnp.zeros((SIDE_ROWS - COUNT * EXT, 128), F32)


def middle_kernel(force, odd, edge, inner, coef, xe, xo, out, wide, again, result, sems):
    flag = odd[0]
    for j in range(4):
        for q in range(19):
            wide[q, (j if j < 2 else j + 12) + 2, 8:24, :] = edge[q, j]

    def copy(x, _):
        for q in range(19):
            wide[q, x + 4, 8:24, :] = inner[q, x]
        return 0

    lax.fori_loop(0, 12, copy, 0)
    sides = []
    for toward, sign in ((0, 1), (1, -1)):
        even, odd_ = (xo, xe) if toward == 0 else (xe, xo)
        for i, (q, layer) in enumerate(entries(0, sign)):
            at = 1 - layer if toward == 0 else 18 + layer
            wide[q, at, 8:24, :] = pick(flag, even[i], odd_[i])
        sides.append([pick(flag, even[19 + j], odd_[19 + j]) for j in range(2)])
    f = [force[axis] for axis in range(3)]

    def one(x, solids, omegas):
        for block in range(2):
            dist = []
            for q in range(19):
                cx, cy, _z = VELOCITY[q]
                dist.append(wide[q, x + 1 - cx, 8 + 8 * block - cy : 16 + 8 * block - cy, :])
            after = collide(dist, solids[block], omegas[block], f)
            for q in range(19):
                again[q, x, 8 + 8 * block : 16 + 8 * block, :] = shift_z(after[q], q)

    def plane(x, _):
        solids = [coef[0, x - 1, 8 * block : 8 * block + 8, :] for block in range(2)]
        omegas = [coef[1, x - 1, 8 * block : 8 * block + 8, :] for block in range(2)]
        one(x, solids, omegas)
        return 0

    one(0, *[[v[0:8], v[8:16]] for v in sides[0]])
    one(17, *[[v[0:8], v[8:16]] for v in sides[1]])
    lax.fori_loop(1, 17, plane, 0)

    def finish(x, _):
        for q in range(19):
            cx, cy, _z = VELOCITY[q]
            for block in range(2):
                start = 8 + 8 * block - cy
                value = again[q, x + 1 - cx, start : start + 8, :]
                result[x, q, 8 * block : 8 * block + 8, :] = value * INVERSE[q] - 1.0
        pltpu.make_async_copy(result.at[x], out.at[:, x], sems.at[x]).start()
        return 0

    lax.fori_loop(0, 16, finish, 0)
    for x in range(16):
        pltpu.make_async_copy(result.at[x], out.at[:, x], sems.at[x]).wait()


def last_kernel(force, odd, mine_e, mine_o, came_e, came_o, _before, out, sides, rows, patch, sem):
    flag = odd[1]
    for block in range(SIDE_ROWS // 8):
        part = slice(8 * block, 8 * block + 8)
        me, mo, ce, co = mine_e[part, :], mine_o[part, :], came_e[part, :], came_o[part, :]
        sides[0, part, :] = pick(flag, co, ce)
        sides[1, part, :] = pick(flag, mo, me)
        sides[2, part, :] = pick(flag, ce, co)
        sides[3, part, :] = pick(flag, me, mo)
    f = [force[axis] for axis in range(3)]
    number = 0
    for side, sign in ((0, 1), (1, -1)):
        came = {e: n for n, e in enumerate(entries(1, sign))}
        mine = {e: n for n, e in enumerate(entries(1, -sign))}
        for line in range(2):
            for block in range(3):
                start = 1 + 8 * block
                dist = []
                for q in range(19):
                    cx, cy, _z = VELOCITY[q]
                    if cy == sign:
                        which, n = 0, came[(q, 1 - line)]
                    elif cy == 0:
                        which, n = (0, came[(q, 0)]) if line == 0 else (1, mine[(q, 0)])
                    else:
                        which, n = 1, mine[(q, line)]
                    at = n * EXT + start - cx
                    dist.append(sides[2 * side + which, at : at + 8, :])
                fixed = [
                    sides[2 * side + line, (19 + j) * EXT + start : (19 + j) * EXT + start + 8, :]
                    for j in range(2)
                ]
                after = collide(dist, fixed[0], fixed[1], f)
                for q in range(19):
                    if VELOCITY[q][1] == sign or (VELOCITY[q][1] == 0 and line == 1):
                        rows[line, q, 8 * block : 8 * block + 8, :] = shift_z(after[q], q)
        for q in range(19):
            cx, cy, _z = VELOCITY[q]
            targets = []
            if cy == sign:
                targets = [(0, 0), (1, 1)]
            elif cy == 0:
                targets = [(1, 0)]
            for line, depth in targets:
                value = rows[line, q, 1 - cx : 17 - cx, :]
                patch[number] = value * INVERSE[q] - 1.0
                y = depth if sign == 1 else 15 - depth
                pltpu.make_async_copy(patch.at[number], out.at[q, :, y, :], sem).start()
                number += 1
    pltpu.make_async_copy(patch, patch, sem).wait()


def swap(value, axis, first):
    n = lax.axis_size(axis)
    pairs = [(i, (i + 1) % n if (i % 2 == 0) == first else (i - 1) % n) for i in range(n)]
    return lax.ppermute(value, axis, pairs)


def halves_of(porosity, relaxation):
    hi = lax.axis_index("gy") // 4
    slab = jnp.stack([porosity, relaxation]).reshape(2, 2, 8, 16, 128)
    other = lax.dynamic_slice_in_dim(slab, (1 - hi) * 4, 4, axis=2)
    mine = lax.dynamic_slice_in_dim(slab, hi * 4, 4, axis=2)
    return mine, lax.ppermute(other, "gy", [(i, i ^ 4) for i in range(8)])


def blocks_of(mine, came):
    b = lax.axis_index("gy")
    hi, lo = b // 4, b % 4
    both = jnp.stack([jnp.where(hi == 0, mine, came), jnp.where(hi == 0, came, mine)])
    parts = [lax.dynamic_index_in_dim(both, lo, axis=3, keepdims=False)]
    for k in range(1, 4):
        message = lax.dynamic_index_in_dim(both, lo ^ k, axis=3, keepdims=False)
        parts.append(lax.ppermute(message, "gy", [(i, i ^ k) for i in range(8)]))
    stacked = jnp.stack(parts)
    ordered = [
        lax.dynamic_index_in_dim(stacked, lo ^ y, axis=0, keepdims=False) for y in range(4)
    ]
    whole = jnp.stack(ordered)
    return whole.transpose(2, 1, 0, 3, 4, 5).reshape(2, 16, 16, 128)


def local(pdf_old, tile_target, porosity, relaxation, solid_mask, force):
    mine, came = halves_of(porosity, relaxation)
    rows = pdf_old.reshape(16, 8, 19, 2, 128).transpose(2, 0, 3, 1, 4).reshape(19, 256, 128)
    packed = pack(tile_target, rows)
    packed, came = lax.optimization_barrier((packed, came))
    arrived = lax.all_to_all(
        packed.reshape(DEVICES, PAIR, 1, 128), ("gx", "gy"), split_axis=0, concat_axis=0, tiled=True
    )
    block = blocks_of(mine, came)
    solid = block[0] + solid_mask.astype(F32) * (1.0 - block[0])
    coef = jnp.stack([solid, block[1]])
    odd = jnp.stack([lax.axis_index("gx") % 2, lax.axis_index("gy") % 2]).astype(jnp.int32)
    tiles = place(arrived)
    posts = [jax.ShapeDtypeStruct((19, n, 16, 128), F32) for n in (4, 12)]
    edge, xe, xo = call(
        edge_kernel, [posts[0], FACE, FACE], (force, odd, tiles, coef), 2_000_000, scalars=2
    )
    from_xe, from_xo = swap(xe, "gx", True), swap(xo, "gx", False)
    inner, yup, ydn = call(
        inner_kernel, [posts[1], FACE, FACE], (force, tiles, coef, edge), 6_000_000
    )
    ye, yo = call(join_kernel, [SIDE, SIDE], (odd, from_xe, from_xo, yup, ydn), 500_000)
    from_ye, from_yo = swap(ye, "gy", True), swap(yo, "gy", False)
    hbm = pl.BlockSpec(memory_space=pltpu.HBM)
    result = call(
        middle_kernel,
        jax.ShapeDtypeStruct((19, 16, 16, 128), F32),
        (force, odd, edge, inner, coef, from_xe, from_xo),
        12_000_000,
        scalars=2,
        out_specs=hbm,
        scratch_shapes=[
            pltpu.VMEM((19, EXT, 32, 128), F32),
            pltpu.VMEM((19, 18, 32, 128), F32),
            pltpu.VMEM((16, 19, 16, 128), F32),
            pltpu.SemaphoreType.DMA((16,)),
        ],
    )
    return pl.pallas_call(
        last_kernel,
        out_shape=jax.ShapeDtypeStruct((19, 16, 16, 128), F32),
        in_specs=[SMEM_SPEC] * 2 + [VMEM_SPEC] * 4 + [hbm],
        out_specs=hbm,
        input_output_aliases={6: 0},
        scratch_shapes=[
            pltpu.VMEM((4, SIDE_ROWS, 128), F32),
            pltpu.VMEM((2, 19, 24, 128), F32),
            pltpu.VMEM((38, 16, 128), F32),
            pltpu.SemaphoreType.DMA,
        ],
        compiler_params=pltpu.CompilerParams(vmem_limit_bytes=VMEM_LIMIT),
        cost_estimate=pl.CostEstimate(flops=2_000_000, bytes_accessed=2_000_000, transcendentals=0),
    )(force, odd, ye, yo, from_ye, from_yo, result)


def solution(mesh):
    return jax.shard_map(
        local,
        mesh=mesh,
        in_specs=(
            P(("gx", "gy"), None, None),
            P(("gx", "gy")),
            P(("gx", "gy"), None, None),
            P(("gx", "gy"), None, None),
            P("gx", "gy", None),
            P(),
        ),
        out_specs=P(None, "gx", "gy", None),
        check_vma=False,
    )
```

```python
import jax
import jax.numpy as jnp
from jax import lax
from jax.experimental import pallas as pl
from jax.experimental.pallas import tpu as pltpu
from jax.sharding import PartitionSpec as P

VELOCITY = (
    (0, 0, 0),
    (1, 0, 0),
    (-1, 0, 0),
    (0, 1, 0),
    (0, -1, 0),
    (0, 0, 1),
    (0, 0, -1),
    (1, 1, 0),
    (-1, -1, 0),
    (1, -1, 0),
    (-1, 1, 0),
    (1, 0, 1),
    (-1, 0, -1),
    (1, 0, -1),
    (-1, 0, 1),
    (0, 1, 1),
    (0, -1, -1),
    (0, 1, -1),
    (0, -1, 1),
)
WEIGHT = [1.0 / 3.0] + [1.0 / 18.0] * 6 + [1.0 / 36.0] * 12
INVERSE = [3.0] + [18.0] * 6 + [36.0] * 12
DEVICES = 128
HELD = 128
CAP = 2
TILE = 38
PAIR = 2 * TILE + 1
ROWS = 40
EXT = 20
VMEM_LIMIT = 48 * 1024 * 1024
VMEM_MOST = 61 * 1024 * 1024
F32 = jnp.float32


def entries(axis, sign):
    far = [(q, 1) for q in range(19) if VELOCITY[q][axis] == sign]
    near = [(q, 0) for q in range(19) if VELOCITY[q][axis] in (0, sign)]
    return far + near


COUNT = 21
SIDE_ROWS = 432


def collide(dist, solid, omega, force):
    plus = [None] * 19
    minus = [None] * 19
    for i in range(1, 19, 2):
        plus[i] = dist[i] + dist[i + 1]
        minus[i] = dist[i] - dist[i + 1]
    density = dist[0]
    for i in range(1, 19, 2):
        density = density + plus[i]
    flow = []
    for axis in range(3):
        total = None
        for i in range(1, 19, 2):
            c = VELOCITY[i][axis]
            if c:
                if total is None:
                    total = minus[i]
                else:
                    total = total + minus[i] if c == 1 else total - minus[i]
        flow.append(total + 0.5 * force[axis])
    base = density - 1.5 * (flow[0] * flow[0] + flow[1] * flow[1] + flow[2] * flow[2])
    open_ = 1.0 - solid
    a = open_ * omega
    b = open_ * ((2.0 - omega) / (1.0 - 0.125 * omega))
    keep = 0.5 - 0.5 * a
    turn = 0.5 - solid - 0.5 * b
    post = [None] * 19
    at = a * base
    post[0] = (keep + keep) * dist[0] + at * (1.0 / 3.0)
    drive = [b * flow[axis] + open_ * force[axis] for axis in range(3)]
    for group, w in ((range(1, 7, 2), 1.0 / 18.0), (range(7, 19, 2), 1.0 / 36.0)):
        even_base = at * w
        square = a * (4.5 * w)
        pull = [drive[axis] * (3.0 * w) for axis in range(3)]
        for i in group:
            along = None
            odd = None
            for axis in range(3):
                c = VELOCITY[i][axis]
                if c:
                    if along is None:
                        along, odd = flow[axis], pull[axis]
                    elif c == 1:
                        along, odd = along + flow[axis], odd + pull[axis]
                    else:
                        along, odd = along - flow[axis], odd - pull[axis]
            even = keep * plus[i] + (even_base + square * (along * along))
            odd = turn * minus[i] + odd
            post[i] = even + odd
            post[i + 1] = even - odd
    return post


def shift_z(value, q):
    c = VELOCITY[q][2]
    return value if c == 0 else pltpu.roll(value, c % 128, 1)


def pack_kernel(target_hbm, pdf_hbm, out, target, used, pdf, tiles, labels, sems, small, sent):
    listing = pltpu.make_async_copy(target_hbm, target, small.at[0])
    listing.start()
    quarters = []
    for part in range(4):
        rows = pl.ds(part * 64, 64)
        copy = pltpu.make_async_copy(pdf_hbm.at[:, rows, :], pdf.at[:, rows, :], sems.at[part])
        copy.start()
        quarters.append(copy)
    flat = pdf.reshape(19 * 256, 128)
    rows_ = tiles.reshape(HELD * TILE, 128)
    empty = jnp.full((8, 128), -1.0, F32)
    for block in range(DEVICES // 8):
        labels[8 * block : 8 * block + 8, 0, :] = empty

    def clear(i, _):
        used[i] = 0
        return 0

    lax.fori_loop(0, DEVICES, clear, 0, unroll=8)
    half = lax.broadcasted_iota(jnp.int32, (1, 128), 1) // 64
    listing.wait()

    def put(k, _):
        t = target[k]
        owner = lax.shift_right_logical(t, 7)
        rank = used[owner]
        used[owner] = rank + 1
        near = lax.shift_right_logical(k, 3) * 16 + (k & 7)
        for r in range(2):
            for q in (0, 8, 16):
                n = min(8, 19 - q)
                value = flat[pl.ds(near + r * 8 + q * 256, n, stride=256), :]
                rows_[pl.ds(k * TILE + r * 19 + q, n), :] = value
        pltpu.make_async_copy(
            tiles.at[pl.ds(k * TILE, TILE)],
            out.at[owner, pl.ds(rank * TILE, TILE)],
            sent,
        ).start()
        line = labels[owner]
        labels[owner] = jnp.where(half == rank, (t & 127).astype(F32), line)
        return 0

    for part in range(4):
        quarters[part].wait()
        lax.fori_loop(part * 32, part * 32 + 32, put, 0, unroll=4)
    named = pltpu.make_async_copy(labels, out.at[:, 2 * TILE], small.at[1])
    named.start()
    pltpu.make_async_copy(tiles, tiles, sent).wait()
    named.wait()


def pack(target, pdf):
    hbm = pl.BlockSpec(memory_space=pltpu.HBM)
    return pl.pallas_call(
        pack_kernel,
        out_shape=jax.ShapeDtypeStruct((DEVICES, PAIR, 1, 128), F32),
        in_specs=[hbm, hbm],
        out_specs=hbm,
        scratch_shapes=[
            pltpu.SMEM((HELD,), jnp.int32),
            pltpu.SMEM((DEVICES,), jnp.int32),
            pltpu.VMEM((19, 256, 128), F32),
            pltpu.VMEM((HELD * TILE, 1, 128), F32),
            pltpu.VMEM((DEVICES, 1, 128), F32),
            pltpu.SemaphoreType.DMA((4,)),
            pltpu.SemaphoreType.DMA((2,)),
            pltpu.SemaphoreType.DMA,
        ],
        compiler_params=pltpu.CompilerParams(vmem_limit_bytes=VMEM_MOST),
        cost_estimate=pl.CostEstimate(flops=0, bytes_accessed=8_000_000, transcendentals=0),
    )(target, pdf)


def place_kernel(arrived, tiles, labels, found, source, sem, small):
    pull = pltpu.make_async_copy(arrived.at[:, 2 * TILE, 0, :], labels, small.at[0])
    pull.start()
    pull.wait()
    lane = lax.broadcasted_iota(jnp.int32, (8, 128), 1)
    lane_f = lane.astype(F32)
    sub = lax.broadcasted_iota(jnp.int32, (8, 128), 0)
    low = lane < 64
    total = jnp.zeros((8, 128), jnp.int32)
    for group in range(DEVICES // 8):
        line = labels[8 * group : 8 * group + 8, :]
        other = pltpu.roll(line, 64, 1)
        number = (sub + 8 * group) * 2
        total = total + jnp.where(jnp.where(low, line, other) == lane_f, number, 0)
        total = total + jnp.where(jnp.where(low, other, line) == lane_f, number + 1, 0)
    found[...] = jnp.broadcast_to(jnp.sum(total, axis=0, keepdims=True), (8, 128))
    hand = pltpu.make_async_copy(found, source, small.at[1])
    hand.start()
    hand.wait()

    def fetch(s, _):
        p = source[0, s]
        pltpu.make_async_copy(
            arrived.at[lax.shift_right_logical(p, 1), pl.ds((p & 1) * TILE, TILE), 0, :],
            tiles.at[pl.ds(pl.multiple_of(s * ROWS, 8), TILE), :],
            sem,
        ).start()
        return 0

    lax.fori_loop(0, HELD, fetch, 0, unroll=8)
    whole = tiles.at[pl.ds(0, HELD * TILE), :]
    pltpu.make_async_copy(whole, whole, sem).wait()


def place(arrived):
    return pl.pallas_call(
        place_kernel,
        out_shape=jax.ShapeDtypeStruct((HELD * ROWS, 128), F32),
        in_specs=[pl.BlockSpec(memory_space=pltpu.HBM)],
        out_specs=pl.BlockSpec(memory_space=pltpu.VMEM),
        scratch_shapes=[
            pltpu.VMEM((DEVICES, 128), F32),
            pltpu.VMEM((8, 128), jnp.int32),
            pltpu.SMEM((8, 128), jnp.int32),
            pltpu.SemaphoreType.DMA,
            pltpu.SemaphoreType.DMA((2,)),
        ],
        compiler_params=pltpu.CompilerParams(vmem_limit_bytes=VMEM_LIMIT),
        cost_estimate=pl.CostEstimate(flops=0, bytes_accessed=8_000_000, transcendentals=0),
    )(arrived)


def pick(flag, even, odd):
    return jnp.where(flag == 0, even, odd)


def plane_step(x, at, tiles, coef, post, f):
    for r in range(2):
        dist = []
        for q in range(19):
            value = tiles[pl.ds(x * (8 * ROWS) + r * 19 + q, 8, stride=ROWS), :]
            dist.append(WEIGHT[q] * value + WEIGHT[q])
        solid = coef[0, x, pl.ds(r, 8, stride=2), :]
        omega = coef[1, x, pl.ds(r, 8, stride=2), :]
        after = collide(dist, solid, omega, f)
        for q in range(19):
            post[q, at, pl.ds(r, 8, stride=2), :] = shift_z(after[q], q)


def edge_kernel(force, odd, tiles, coef, edge, xe, xo):
    f = [force[axis] for axis in range(3)]

    def plane(j, _):
        plane_step(jnp.where(j < 2, j, j + 12), j, tiles, coef, edge, f)
        return 0

    lax.fori_loop(0, 4, plane, 0)
    flag = odd[0]
    for i, ((qu, lu), (qd, ld)) in enumerate(zip(entries(0, 1), entries(0, -1))):
        up, dn = edge[qu, 3 - lu], edge[qd, ld]
        xe[i] = pick(flag, up, dn)
        xo[i] = pick(flag, dn, up)
    for j in range(2):
        up, dn = coef[j, 15], coef[j, 0]
        xe[19 + j] = pick(flag, up, dn)
        xo[19 + j] = pick(flag, dn, up)


def inner_kernel(force, tiles, coef, edge, inner, yup, ydn):
    f = [force[axis] for axis in range(3)]

    def plane(j, _):
        plane_step(j + 2, j, tiles, coef, inner, f)
        return 0

    lax.fori_loop(0, 12, plane, 0)
    for out, sign in ((yup, 1), (ydn, -1)):
        for i, (q, layer) in enumerate(entries(1, sign)):
            row = 15 - layer if sign == 1 else layer
            for x in range(16):
                if 2 <= x < 14:
                    value = inner[q, x - 2, row : row + 1, :]
                else:
                    value = edge[q, x if x < 2 else x - 12, row : row + 1, :]
                out[i, x : x + 1, :] = value
        row = 15 if sign == 1 else 0
        for j in range(2):
            for x in range(16):
                out[19 + j, x : x + 1, :] = coef[j, x, row : row + 1, :]


VMEM_SPEC = pl.BlockSpec(memory_space=pltpu.VMEM)
SMEM_SPEC = pl.BlockSpec(memory_space=pltpu.SMEM)
FACE = jax.ShapeDtypeStruct((COUNT, 16, 128), F32)
SIDE = jax.ShapeDtypeStruct((SIDE_ROWS, 128), F32)


def call(kernel, out_shape, operands, work, scalars=1, **more):
    return pl.pallas_call(
        kernel,
        out_shape=out_shape,
        in_specs=[SMEM_SPEC] * scalars + [VMEM_SPEC] * (len(operands) - scalars),
        compiler_params=pltpu.CompilerParams(vmem_limit_bytes=VMEM_LIMIT),
        cost_estimate=pl.CostEstimate(flops=work, bytes_accessed=work, transcendentals=0),
        **more,
    )(*operands)


def join_kernel(odd, xe, xo, yup, ydn, ye, yo):
    fx, fy = odd[0], odd[1]
    lists = [entries(1, sign) + [(19, 0), (20, 0)] for sign in (1, -1)]
    have = [
        {e: n for n, e in enumerate(entries(0, toward) + [(19, 0), (20, 0)])} for toward in (1, -1)
    ]

    def corner(direction, i, toward, deep):
        q, layer = lists[direction][i]
        n = have[toward].get((q, deep))
        if n is None:
            return jnp.zeros((1, 128), F32)
        row = 15 - layer if direction == 0 else layer
        even, odd_ = (xo, xe) if toward == 0 else (xe, xo)
        return pick(fx, even[n, row : row + 1, :], odd_[n, row : row + 1, :])

    for i in range(COUNT):
        up, dn = yup[i], ydn[i]
        ye[i * EXT + 2 : i * EXT + 18, :] = pick(fy, up, dn)
        yo[i * EXT + 2 : i * EXT + 18, :] = pick(fy, dn, up)
        for toward in range(2):
            for deep in range(2):
                at = i * EXT + ((1 - deep) if toward == 0 else 18 + deep)
                up, dn = corner(0, i, toward, deep), corner(1, i, toward, deep)
                ye[at : at + 1, :] = pick(fy, up, dn)
                yo[at : at + 1, :] = pick(fy, dn, up)
    for out in (ye, yo):
        out[COUNT * EXT : SIDE_ROWS, :] = jnp.zeros((SIDE_ROWS - COUNT * EXT, 128), F32)


def middle_kernel(force, odd, edge, inner, coef, xe, xo, out, wide, again, result, sems):
    flag = odd[0]
    for j in range(4):
        for q in range(19):
            wide[q, (j if j < 2 else j + 12) + 2, 8:24, :] = edge[q, j]

    def copy(x, _):
        for q in range(19):
            wide[q, x + 4, 8:24, :] = inner[q, x]
        return 0

    lax.fori_loop(0, 12, copy, 0)
    sides = []
    for toward, sign in ((0, 1), (1, -1)):
        even, odd_ = (xo, xe) if toward == 0 else (xe, xo)
        for i, (q, layer) in enumerate(entries(0, sign)):
            at = 1 - layer if toward == 0 else 18 + layer
            wide[q, at, 8:24, :] = pick(flag, even[i], odd_[i])
        sides.append([pick(flag, even[19 + j], odd_[19 + j]) for j in range(2)])
    f = [force[axis] for axis in range(3)]

    def one(x, solids, omegas):
        for block in range(2):
            dist = []
            for q in range(19):
                cx, cy, _z = VELOCITY[q]
                dist.append(wide[q, x + 1 - cx, 8 + 8 * block - cy : 16 + 8 * block - cy, :])
            after = collide(dist, solids[block], omegas[block], f)
            for q in range(19):
                again[q, x, 8 + 8 * block : 16 + 8 * block, :] = shift_z(after[q], q)

    def plane(x, _):
        solids = [coef[0, x - 1, 8 * block : 8 * block + 8, :] for block in range(2)]
        omegas = [coef[1, x - 1, 8 * block : 8 * block + 8, :] for block in range(2)]
        one(x, solids, omegas)
        return 0

    one(0, *[[v[0:8], v[8:16]] for v in sides[0]])
    one(17, *[[v[0:8], v[8:16]] for v in sides[1]])
    lax.fori_loop(1, 17, plane, 0)

    def finish(x, _):
        for q in range(19):
            cx, cy, _z = VELOCITY[q]
            for block in range(2):
                start = 8 + 8 * block - cy
                value = again[q, x + 1 - cx, start : start + 8, :]
                result[x, q, 8 * block : 8 * block + 8, :] = value * INVERSE[q] - 1.0
        pltpu.make_async_copy(result.at[x], out.at[:, x], sems.at[x]).start()
        return 0

    lax.fori_loop(0, 16, finish, 0)
    for x in range(16):
        pltpu.make_async_copy(result.at[x], out.at[:, x], sems.at[x]).wait()


def last_kernel(force, odd, mine_e, mine_o, came_e, came_o, _before, out, sides, rows, patch, sem):
    flag = odd[1]
    for block in range(SIDE_ROWS // 8):
        part = slice(8 * block, 8 * block + 8)
        me, mo, ce, co = mine_e[part, :], mine_o[part, :], came_e[part, :], came_o[part, :]
        sides[0, part, :] = pick(flag, co, ce)
        sides[1, part, :] = pick(flag, mo, me)
        sides[2, part, :] = pick(flag, ce, co)
        sides[3, part, :] = pick(flag, me, mo)
    f = [force[axis] for axis in range(3)]
    number = 0
    for side, sign in ((0, 1), (1, -1)):
        came = {e: n for n, e in enumerate(entries(1, sign))}
        mine = {e: n for n, e in enumerate(entries(1, -sign))}
        for line in range(2):
            for block in range(3):
                start = 1 + 8 * block
                dist = []
                for q in range(19):
                    cx, cy, _z = VELOCITY[q]
                    if cy == sign:
                        which, n = 0, came[(q, 1 - line)]
                    elif cy == 0:
                        which, n = (0, came[(q, 0)]) if line == 0 else (1, mine[(q, 0)])
                    else:
                        which, n = 1, mine[(q, line)]
                    at = n * EXT + start - cx
                    dist.append(sides[2 * side + which, at : at + 8, :])
                fixed = [
                    sides[2 * side + line, (19 + j) * EXT + start : (19 + j) * EXT + start + 8, :]
                    for j in range(2)
                ]
                after = collide(dist, fixed[0], fixed[1], f)
                for q in range(19):
                    if VELOCITY[q][1] == sign or (VELOCITY[q][1] == 0 and line == 1):
                        rows[line, q, 8 * block : 8 * block + 8, :] = shift_z(after[q], q)
        for q in range(19):
            cx, cy, _z = VELOCITY[q]
            targets = []
            if cy == sign:
                targets = [(0, 0), (1, 1)]
            elif cy == 0:
                targets = [(1, 0)]
            for line, depth in targets:
                value = rows[line, q, 1 - cx : 17 - cx, :]
                patch[number] = value * INVERSE[q] - 1.0
                y = depth if sign == 1 else 15 - depth
                pltpu.make_async_copy(patch.at[number], out.at[q, :, y, :], sem).start()
                number += 1
    pltpu.make_async_copy(patch, patch, sem).wait()


def swap(value, axis, first):
    n = lax.axis_size(axis)
    pairs = [(i, (i + 1) % n if (i % 2 == 0) == first else (i - 1) % n) for i in range(n)]
    return lax.ppermute(value, axis, pairs)


def halves_of(porosity, relaxation):
    hi = lax.axis_index("gy") // 4
    slab = jnp.stack([porosity, relaxation]).reshape(2, 2, 8, 16, 128)
    other = lax.dynamic_slice_in_dim(slab, (1 - hi) * 4, 4, axis=2)
    mine = lax.dynamic_slice_in_dim(slab, hi * 4, 4, axis=2)
    return mine, lax.ppermute(other, "gy", [(i, i ^ 4) for i in range(8)])


def pieces_of(mine, came):
    b = lax.axis_index("gy")
    hi, lo = b // 4, b % 4
    both = jnp.stack([jnp.where(hi == 0, mine, came), jnp.where(hi == 0, came, mine)])
    parts = [lax.dynamic_index_in_dim(both, lo, axis=3, keepdims=False)]
    for k in range(1, 4):
        message = lax.dynamic_index_in_dim(both, lo ^ k, axis=3, keepdims=False)
        parts.append(lax.ppermute(message, "gy", [(i, i ^ k) for i in range(8)]))
    return parts


def block_of(parts):
    lo = lax.axis_index("gy") % 4
    stacked = jnp.stack(parts)
    ordered = [
        lax.dynamic_index_in_dim(stacked, lo ^ y, axis=0, keepdims=False) for y in range(4)
    ]
    whole = jnp.stack(ordered)
    return whole.transpose(2, 1, 0, 3, 4, 5).reshape(2, 16, 16, 128)


def local(pdf_old, tile_target, porosity, relaxation, solid_mask, force):
    mine, came = halves_of(porosity, relaxation)
    rows = pdf_old.reshape(16, 8, 19, 2, 128).transpose(2, 0, 3, 1, 4).reshape(19, 256, 128)
    packed = pack(tile_target, rows)
    packed, came = lax.optimization_barrier((packed, came))
    arrived = lax.all_to_all(
        packed, ("gx", "gy"), split_axis=0, concat_axis=0, tiled=True
    )
    parts = pieces_of(mine, came)
    tiles, parts[0] = lax.optimization_barrier((place(arrived), parts[0]))
    block = block_of(parts)
    solid = block[0] + solid_mask.astype(F32) * (1.0 - block[0])
    coef = jnp.stack([solid, block[1]])
    odd = jnp.stack([lax.axis_index("gx") % 2, lax.axis_index("gy") % 2]).astype(jnp.int32)
    posts = [jax.ShapeDtypeStruct((19, n, 16, 128), F32) for n in (4, 12)]
    edge, xe, xo = call(
        edge_kernel, [posts[0], FACE, FACE], (force, odd, tiles, coef), 2_000_000, scalars=2
    )
    from_xe, from_xo = swap(xe, "gx", True), swap(xo, "gx", False)
    inner, yup, ydn = call(
        inner_kernel, [posts[1], FACE, FACE], (force, tiles, coef, edge), 6_000_000
    )
    ye, yo = call(join_kernel, [SIDE, SIDE], (odd, from_xe, from_xo, yup, ydn), 500_000)
    from_ye, from_yo = swap(ye, "gy", True), swap(yo, "gy", False)
    hbm = pl.BlockSpec(memory_space=pltpu.HBM)
    result = call(
        middle_kernel,
        jax.ShapeDtypeStruct((19, 16, 16, 128), F32),
        (force, odd, edge, inner, coef, from_xe, from_xo),
        12_000_000,
        scalars=2,
        out_specs=hbm,
        scratch_shapes=[
            pltpu.VMEM((19, EXT, 32, 128), F32),
            pltpu.VMEM((19, 18, 32, 128), F32),
            pltpu.VMEM((16, 19, 16, 128), F32),
            pltpu.SemaphoreType.DMA((16,)),
        ],
    )
    return pl.pallas_call(
        last_kernel,
        out_shape=jax.ShapeDtypeStruct((19, 16, 16, 128), F32),
        in_specs=[SMEM_SPEC] * 2 + [VMEM_SPEC] * 4 + [hbm],
        out_specs=hbm,
        input_output_aliases={6: 0},
        scratch_shapes=[
            pltpu.VMEM((4, SIDE_ROWS, 128), F32),
            pltpu.VMEM((2, 19, 24, 128), F32),
            pltpu.VMEM((38, 16, 128), F32),
            pltpu.SemaphoreType.DMA,
        ],
        compiler_params=pltpu.CompilerParams(vmem_limit_bytes=VMEM_LIMIT),
        cost_estimate=pl.CostEstimate(flops=2_000_000, bytes_accessed=2_000_000, transcendentals=0),
    )(force, odd, ye, yo, from_ye, from_yo, result)


def solution(mesh):
    return jax.shard_map(
        local,
        mesh=mesh,
        in_specs=(
            P(("gx", "gy"), None, None),
            P(("gx", "gy")),
            P(("gx", "gy"), None, None),
            P(("gx", "gy"), None, None),
            P("gx", "gy", None),
            P(),
        ),
        out_specs=P(None, "gx", "gy", None),
        check_vma=False,
    )
```

```python
import jax
import jax.numpy as jnp
from jax import lax
from jax.experimental import pallas as pl
from jax.experimental.pallas import tpu as pltpu
from jax.sharding import PartitionSpec as P

VELOCITY = (
    (0, 0, 0),
    (1, 0, 0),
    (-1, 0, 0),
    (0, 1, 0),
    (0, -1, 0),
    (0, 0, 1),
    (0, 0, -1),
    (1, 1, 0),
    (-1, -1, 0),
    (1, -1, 0),
    (-1, 1, 0),
    (1, 0, 1),
    (-1, 0, -1),
    (1, 0, -1),
    (-1, 0, 1),
    (0, 1, 1),
    (0, -1, -1),
    (0, 1, -1),
    (0, -1, 1),
)
WEIGHT = [1.0 / 3.0] + [1.0 / 18.0] * 6 + [1.0 / 36.0] * 12
INVERSE = [3.0] + [18.0] * 6 + [36.0] * 12
DEVICES = 128
HELD = 128
CAP = 2
TILE = 38
PAIR = 2 * TILE + 1
ROWS = 40
EXT = 20
VMEM_LIMIT = 48 * 1024 * 1024
VMEM_MOST = 61 * 1024 * 1024
F32 = jnp.float32


def entries(axis, sign):
    far = [(q, 1) for q in range(19) if VELOCITY[q][axis] == sign]
    near = [(q, 0) for q in range(19) if VELOCITY[q][axis] in (0, sign)]
    return far + near


COUNT = 21
SIDE_ROWS = 432


def collide(dist, solid, omega, force):
    plus = [None] * 19
    minus = [None] * 19
    for i in range(1, 19, 2):
        plus[i] = dist[i] + dist[i + 1]
        minus[i] = dist[i] - dist[i + 1]
    density = dist[0]
    for i in range(1, 19, 2):
        density = density + plus[i]
    flow = []
    for axis in range(3):
        total = None
        for i in range(1, 19, 2):
            c = VELOCITY[i][axis]
            if c:
                if total is None:
                    total = minus[i]
                else:
                    total = total + minus[i] if c == 1 else total - minus[i]
        flow.append(total + 0.5 * force[axis])
    base = density - 1.5 * (flow[0] * flow[0] + flow[1] * flow[1] + flow[2] * flow[2])
    open_ = 1.0 - solid
    a = open_ * omega
    b = open_ * ((2.0 - omega) / (1.0 - 0.125 * omega))
    keep = 0.5 - 0.5 * a
    turn = 0.5 - solid - 0.5 * b
    post = [None] * 19
    at = a * base
    post[0] = (keep + keep) * dist[0] + at * (1.0 / 3.0)
    drive = [b * flow[axis] + open_ * force[axis] for axis in range(3)]
    for group, w in ((range(1, 7, 2), 1.0 / 18.0), (range(7, 19, 2), 1.0 / 36.0)):
        even_base = at * w
        square = a * (4.5 * w)
        pull = [drive[axis] * (3.0 * w) for axis in range(3)]
        for i in group:
            along = None
            odd = None
            for axis in range(3):
                c = VELOCITY[i][axis]
                if c:
                    if along is None:
                        along, odd = flow[axis], pull[axis]
                    elif c == 1:
                        along, odd = along + flow[axis], odd + pull[axis]
                    else:
                        along, odd = along - flow[axis], odd - pull[axis]
            even = keep * plus[i] + (even_base + square * (along * along))
            odd = turn * minus[i] + odd
            post[i] = even + odd
            post[i + 1] = even - odd
    return post


def shift_z(value, q):
    c = VELOCITY[q][2]
    return value if c == 0 else pltpu.roll(value, c % 128, 1)


def pack_kernel(target_hbm, pdf_hbm, out, target, used, pdf, tiles, labels, sems, small, sent):
    listing = pltpu.make_async_copy(target_hbm, target, small.at[0])
    listing.start()
    quarters = []
    for part in range(4):
        rows = pl.ds(part * 64, 64)
        copy = pltpu.make_async_copy(pdf_hbm.at[:, rows, :], pdf.at[:, rows, :], sems.at[part])
        copy.start()
        quarters.append(copy)
    flat = pdf.reshape(19 * 256, 128)
    rows_ = tiles.reshape(HELD * TILE, 128)
    empty = jnp.full((8, 128), -1.0, F32)
    for block in range(DEVICES // 8):
        labels[8 * block : 8 * block + 8, 0, :] = empty

    def clear(i, _):
        used[i] = 0
        return 0

    lax.fori_loop(0, DEVICES, clear, 0, unroll=8)
    half = lax.broadcasted_iota(jnp.int32, (1, 128), 1) // 64
    listing.wait()

    def put(k, _):
        t = target[k]
        owner = lax.shift_right_logical(t, 7)
        rank = used[owner]
        used[owner] = rank + 1
        near = lax.shift_right_logical(k, 3) * 16 + (k & 7)
        for r in range(2):
            for q in (0, 8, 16):
                n = min(8, 19 - q)
                value = flat[pl.ds(near + r * 8 + q * 256, n, stride=256), :]
                rows_[pl.ds(k * TILE + r * 19 + q, n), :] = value
        pltpu.make_async_copy(
            tiles.at[pl.ds(k * TILE, TILE)],
            out.at[owner, pl.ds(rank * TILE, TILE)],
            sent,
        ).start()
        line = labels[owner]
        labels[owner] = jnp.where(half == rank, (t & 127).astype(F32), line)
        return 0

    for part in range(4):
        quarters[part].wait()
        lax.fori_loop(part * 32, part * 32 + 32, put, 0, unroll=4)
    named = pltpu.make_async_copy(labels, out.at[:, 2 * TILE], small.at[1])
    named.start()
    pltpu.make_async_copy(tiles, tiles, sent).wait()
    named.wait()


def pack(target, pdf):
    hbm = pl.BlockSpec(memory_space=pltpu.HBM)
    return pl.pallas_call(
        pack_kernel,
        out_shape=jax.ShapeDtypeStruct((DEVICES, PAIR, 1, 128), F32),
        in_specs=[hbm, hbm],
        out_specs=hbm,
        scratch_shapes=[
            pltpu.SMEM((HELD,), jnp.int32),
            pltpu.SMEM((DEVICES,), jnp.int32),
            pltpu.VMEM((19, 256, 128), F32),
            pltpu.VMEM((HELD * TILE, 1, 128), F32),
            pltpu.VMEM((DEVICES, 1, 128), F32),
            pltpu.SemaphoreType.DMA((4,)),
            pltpu.SemaphoreType.DMA((2,)),
            pltpu.SemaphoreType.DMA,
        ],
        compiler_params=pltpu.CompilerParams(vmem_limit_bytes=VMEM_MOST),
        cost_estimate=pl.CostEstimate(flops=0, bytes_accessed=8_000_000, transcendentals=0),
    )(target, pdf)


def pick(flag, even, odd):
    return jnp.where(flag == 0, even, odd)


def plane_step(x, at, tiles, coef, post, f):
    for r in range(2):
        dist = []
        for q in range(19):
            value = tiles[pl.ds(x * (8 * ROWS) + r * 19 + q, 8, stride=ROWS), :]
            dist.append(WEIGHT[q] * value + WEIGHT[q])
        solid = coef[0, x, pl.ds(r, 8, stride=2), :]
        omega = coef[1, x, pl.ds(r, 8, stride=2), :]
        after = collide(dist, solid, omega, f)
        for q in range(19):
            post[q, at, pl.ds(r, 8, stride=2), :] = shift_z(after[q], q)


def edge_kernel(
    odd, force, arrived, coef, tiles, edge, xe, xo, labels, found, source, sems, small
):
    pull = pltpu.make_async_copy(arrived.at[:, 2 * TILE, 0, :], labels, small.at[0])
    pull.start()
    f = [force[axis : axis + 1, :] for axis in range(3)]
    lane = lax.broadcasted_iota(jnp.int32, (8, 128), 1)
    lane_f = lane.astype(F32)
    sub = lax.broadcasted_iota(jnp.int32, (8, 128), 0)
    low = lane < 64
    total = jnp.zeros((8, 128), jnp.int32)
    pull.wait()
    for group in range(DEVICES // 8):
        line = labels[8 * group : 8 * group + 8, :]
        other = pltpu.roll(line, 64, 1)
        number = (sub + 8 * group) * 2
        total = total + jnp.where(jnp.where(low, line, other) == lane_f, number, 0)
        total = total + jnp.where(jnp.where(low, other, line) == lane_f, number + 1, 0)
    found[...] = jnp.broadcast_to(jnp.sum(total, axis=0, keepdims=True), (8, 128))
    hand = pltpu.make_async_copy(found, source, small.at[1])
    hand.start()
    hand.wait()

    def fetch(s):
        p = source[0, s]
        pltpu.make_async_copy(
            arrived.at[lax.shift_right_logical(p, 1), pl.ds((p & 1) * TILE, TILE), 0, :],
            tiles.at[pl.ds(pl.multiple_of(s * ROWS, 8), TILE), :],
            sems.at[lax.shift_right_logical(s, 3)],
        ).start()

    def arrive(x):
        whole = tiles.at[pl.ds(0, 8 * TILE), :]
        pltpu.make_async_copy(whole, whole, sems.at[x]).wait()

    for x in (0, 1, 14, 15):
        for i in range(8):
            fetch(8 * x + i)

    def plane(j, _):
        x = jnp.where(j < 2, j, j + 12)
        for i in range(24):
            fetch(16 + 24 * j + i)
        arrive(x)
        plane_step(x, j, tiles, coef, edge, f)
        return 0

    lax.fori_loop(0, 4, plane, 0)
    flag = odd[0]
    for i, ((qu, lu), (qd, ld)) in enumerate(zip(entries(0, 1), entries(0, -1))):
        up, dn = edge[qu, 3 - lu], edge[qd, ld]
        xe[i] = pick(flag, up, dn)
        xo[i] = pick(flag, dn, up)
    for j in range(2):
        up, dn = coef[j, 15], coef[j, 0]
        xe[19 + j] = pick(flag, up, dn)
        xo[19 + j] = pick(flag, dn, up)
    for x in range(2, 14):
        arrive(x)


def inner_kernel(force, tiles, coef, edge, inner, yup, ydn):
    f = [force[axis : axis + 1, :] for axis in range(3)]

    def plane(j, _):
        plane_step(j + 2, j, tiles, coef, inner, f)
        return 0

    lax.fori_loop(0, 12, plane, 0)
    for out, sign in ((yup, 1), (ydn, -1)):
        for i, (q, layer) in enumerate(entries(1, sign)):
            row = 15 - layer if sign == 1 else layer
            for x in range(16):
                if 2 <= x < 14:
                    value = inner[q, x - 2, row : row + 1, :]
                else:
                    value = edge[q, x if x < 2 else x - 12, row : row + 1, :]
                out[i, x : x + 1, :] = value
        row = 15 if sign == 1 else 0
        for j in range(2):
            for x in range(16):
                out[19 + j, x : x + 1, :] = coef[j, x, row : row + 1, :]


VMEM_SPEC = pl.BlockSpec(memory_space=pltpu.VMEM)
SMEM_SPEC = pl.BlockSpec(memory_space=pltpu.SMEM)
FACE = jax.ShapeDtypeStruct((COUNT, 16, 128), F32)
SIDE = jax.ShapeDtypeStruct((SIDE_ROWS, 128), F32)


def call(kernel, out_shape, operands, work, scalars=1, **more):
    return pl.pallas_call(
        kernel,
        out_shape=out_shape,
        in_specs=[SMEM_SPEC] * scalars + [VMEM_SPEC] * (len(operands) - scalars),
        compiler_params=pltpu.CompilerParams(vmem_limit_bytes=VMEM_LIMIT),
        cost_estimate=pl.CostEstimate(flops=work, bytes_accessed=work, transcendentals=0),
        **more,
    )(*operands)


def join_kernel(odd, xe, xo, yup, ydn, ye, yo):
    fx, fy = odd[0], odd[1]
    lists = [entries(1, sign) + [(19, 0), (20, 0)] for sign in (1, -1)]
    have = [
        {e: n for n, e in enumerate(entries(0, toward) + [(19, 0), (20, 0)])} for toward in (1, -1)
    ]

    def corner(direction, i, toward, deep):
        q, layer = lists[direction][i]
        n = have[toward].get((q, deep))
        if n is None:
            return jnp.zeros((1, 128), F32)
        row = 15 - layer if direction == 0 else layer
        even, odd_ = (xo, xe) if toward == 0 else (xe, xo)
        return pick(fx, even[n, row : row + 1, :], odd_[n, row : row + 1, :])

    for i in range(COUNT):
        up, dn = yup[i], ydn[i]
        ye[i * EXT + 2 : i * EXT + 18, :] = pick(fy, up, dn)
        yo[i * EXT + 2 : i * EXT + 18, :] = pick(fy, dn, up)
        for toward in range(2):
            for deep in range(2):
                at = i * EXT + ((1 - deep) if toward == 0 else 18 + deep)
                up, dn = corner(0, i, toward, deep), corner(1, i, toward, deep)
                ye[at : at + 1, :] = pick(fy, up, dn)
                yo[at : at + 1, :] = pick(fy, dn, up)
    for out in (ye, yo):
        out[COUNT * EXT : SIDE_ROWS, :] = jnp.zeros((SIDE_ROWS - COUNT * EXT, 128), F32)


def middle_kernel(odd, force, edge, inner, coef, xe, xo, out, wide, again, result, sems):
    flag = odd[0]
    for j in range(4):
        for q in range(19):
            wide[q, (j if j < 2 else j + 12) + 2, 8:24, :] = edge[q, j]

    def copy(x, _):
        for q in range(19):
            wide[q, x + 4, 8:24, :] = inner[q, x]
        return 0

    lax.fori_loop(0, 12, copy, 0)
    sides = []
    for toward, sign in ((0, 1), (1, -1)):
        even, odd_ = (xo, xe) if toward == 0 else (xe, xo)
        for i, (q, layer) in enumerate(entries(0, sign)):
            at = 1 - layer if toward == 0 else 18 + layer
            wide[q, at, 8:24, :] = pick(flag, even[i], odd_[i])
        sides.append([pick(flag, even[19 + j], odd_[19 + j]) for j in range(2)])
    f = [force[axis : axis + 1, :] for axis in range(3)]

    def one(x, solids, omegas):
        for block in range(2):
            dist = []
            for q in range(19):
                cx, cy, _z = VELOCITY[q]
                dist.append(wide[q, x + 1 - cx, 8 + 8 * block - cy : 16 + 8 * block - cy, :])
            after = collide(dist, solids[block], omegas[block], f)
            for q in range(19):
                again[q, x, 8 + 8 * block : 16 + 8 * block, :] = shift_z(after[q], q)

    def plane(x, _):
        solids = [coef[0, x - 1, 8 * block : 8 * block + 8, :] for block in range(2)]
        omegas = [coef[1, x - 1, 8 * block : 8 * block + 8, :] for block in range(2)]
        one(x, solids, omegas)
        return 0

    one(0, *[[v[0:8], v[8:16]] for v in sides[0]])
    one(17, *[[v[0:8], v[8:16]] for v in sides[1]])
    lax.fori_loop(1, 17, plane, 0)

    def finish(x, _):
        for q in range(19):
            cx, cy, _z = VELOCITY[q]
            for block in range(2):
                start = 8 + 8 * block - cy
                value = again[q, x + 1 - cx, start : start + 8, :]
                result[x, q, 8 * block : 8 * block + 8, :] = value * INVERSE[q] - 1.0
        pltpu.make_async_copy(result.at[x], out.at[:, x], sems.at[x]).start()
        return 0

    lax.fori_loop(0, 16, finish, 0)
    for x in range(16):
        pltpu.make_async_copy(result.at[x], out.at[:, x], sems.at[x]).wait()


def last_kernel(odd, force, mine_e, mine_o, came_e, came_o, _before, out, sides, rows, patch, sem):
    flag = odd[1]
    for block in range(SIDE_ROWS // 8):
        part = slice(8 * block, 8 * block + 8)
        me, mo, ce, co = mine_e[part, :], mine_o[part, :], came_e[part, :], came_o[part, :]
        sides[0, part, :] = pick(flag, co, ce)
        sides[1, part, :] = pick(flag, mo, me)
        sides[2, part, :] = pick(flag, ce, co)
        sides[3, part, :] = pick(flag, me, mo)
    f = [force[axis : axis + 1, :] for axis in range(3)]
    number = 0
    for side, sign in ((0, 1), (1, -1)):
        came = {e: n for n, e in enumerate(entries(1, sign))}
        mine = {e: n for n, e in enumerate(entries(1, -sign))}
        for line in range(2):
            for block in range(3):
                start = 1 + 8 * block
                dist = []
                for q in range(19):
                    cx, cy, _z = VELOCITY[q]
                    if cy == sign:
                        which, n = 0, came[(q, 1 - line)]
                    elif cy == 0:
                        which, n = (0, came[(q, 0)]) if line == 0 else (1, mine[(q, 0)])
                    else:
                        which, n = 1, mine[(q, line)]
                    at = n * EXT + start - cx
                    dist.append(sides[2 * side + which, at : at + 8, :])
                fixed = [
                    sides[2 * side + line, (19 + j) * EXT + start : (19 + j) * EXT + start + 8, :]
                    for j in range(2)
                ]
                after = collide(dist, fixed[0], fixed[1], f)
                for q in range(19):
                    if VELOCITY[q][1] == sign or (VELOCITY[q][1] == 0 and line == 1):
                        rows[line, q, 8 * block : 8 * block + 8, :] = shift_z(after[q], q)
        for q in range(19):
            cx, cy, _z = VELOCITY[q]
            targets = []
            if cy == sign:
                targets = [(0, 0), (1, 1)]
            elif cy == 0:
                targets = [(1, 0)]
            for line, depth in targets:
                value = rows[line, q, 1 - cx : 17 - cx, :]
                patch[number] = value * INVERSE[q] - 1.0
                y = depth if sign == 1 else 15 - depth
                pltpu.make_async_copy(patch.at[number], out.at[q, :, y, :], sem).start()
                number += 1
    pltpu.make_async_copy(patch, patch, sem).wait()


def swap(value, axis, first):
    n = lax.axis_size(axis)
    pairs = [(i, (i + 1) % n if (i % 2 == 0) == first else (i - 1) % n) for i in range(n)]
    return lax.ppermute(value, axis, pairs)


def halves_of(porosity, relaxation):
    lo = lax.axis_index("gy") % 2
    slab = jnp.stack([porosity, relaxation]).reshape(2, 2, 4, 2, 16, 128)
    other = lax.dynamic_index_in_dim(slab, 1 - lo, axis=3, keepdims=False)
    mine = lax.dynamic_index_in_dim(slab, lo, axis=3, keepdims=False)
    return mine, lax.ppermute(other, "gy", [(i, i ^ 1) for i in range(8)])


def pieces_of(mine, came):
    b = lax.axis_index("gy")
    hi, lo = b // 2, b % 2
    both = jnp.stack([jnp.where(lo == 0, mine, came), jnp.where(lo == 0, came, mine)])
    parts = [lax.dynamic_index_in_dim(both, hi, axis=3, keepdims=False)]
    for k in range(1, 4):
        message = lax.dynamic_index_in_dim(both, hi ^ k, axis=3, keepdims=False)
        parts.append(lax.ppermute(message, "gy", [(i, i ^ (2 * k)) for i in range(8)]))
    return parts


def block_of(parts):
    hi = lax.axis_index("gy") // 2
    stacked = jnp.stack(parts)
    ordered = [
        lax.dynamic_index_in_dim(stacked, hi ^ y, axis=0, keepdims=False) for y in range(4)
    ]
    whole = jnp.stack(ordered)
    return whole.transpose(2, 0, 1, 3, 4, 5).reshape(2, 16, 16, 128)


def local(pdf_old, tile_target, porosity, relaxation, solid_mask, force):
    mine, came = halves_of(porosity, relaxation)
    rows = pdf_old.reshape(16, 8, 19, 2, 128).transpose(2, 0, 3, 1, 4).reshape(19, 256, 128)
    packed = pack(tile_target, rows)
    packed, came = lax.optimization_barrier((packed, came))
    arrived = lax.all_to_all(
        packed, ("gx", "gy"), split_axis=0, concat_axis=0, tiled=True
    )
    block = block_of(pieces_of(mine, came))
    solid = block[0] + solid_mask.astype(F32) * (1.0 - block[0])
    coef = jnp.stack([solid, block[1]])
    odd = jnp.stack([lax.axis_index("gx") % 2, lax.axis_index("gy") % 2]).astype(jnp.int32)
    drive = jnp.broadcast_to(jnp.pad(force, (0, 5))[:, None], (8, 128))
    coef, odd, drive = lax.optimization_barrier((coef, odd, drive))
    hbm = pl.BlockSpec(memory_space=pltpu.HBM)
    posts = [jax.ShapeDtypeStruct((19, n, 16, 128), F32) for n in (4, 12)]
    tiles, edge, xe, xo = pl.pallas_call(
        edge_kernel,
        out_shape=[jax.ShapeDtypeStruct((HELD * ROWS, 128), F32), posts[0], FACE, FACE],
        in_specs=[SMEM_SPEC, VMEM_SPEC, hbm, VMEM_SPEC],
        out_specs=[VMEM_SPEC] * 4,
        scratch_shapes=[
            pltpu.VMEM((DEVICES, 128), F32),
            pltpu.VMEM((8, 128), jnp.int32),
            pltpu.SMEM((8, 128), jnp.int32),
            pltpu.SemaphoreType.DMA((16,)),
            pltpu.SemaphoreType.DMA((2,)),
        ],
        compiler_params=pltpu.CompilerParams(vmem_limit_bytes=VMEM_LIMIT),
        cost_estimate=pl.CostEstimate(flops=2_000_000, bytes_accessed=8_000_000, transcendentals=0),
    )(odd, drive, arrived, coef)
    from_xe, from_xo = swap(xe, "gx", True), swap(xo, "gx", False)
    inner, yup, ydn = call(
        inner_kernel, [posts[1], FACE, FACE], (drive, tiles, coef, edge), 6_000_000, scalars=0
    )
    ye, yo = call(join_kernel, [SIDE, SIDE], (odd, from_xe, from_xo, yup, ydn), 500_000)
    from_ye, from_yo = swap(ye, "gy", True), swap(yo, "gy", False)
    result = call(
        middle_kernel,
        jax.ShapeDtypeStruct((19, 16, 16, 128), F32),
        (odd, drive, edge, inner, coef, from_xe, from_xo),
        12_000_000,
        out_specs=hbm,
        scratch_shapes=[
            pltpu.VMEM((19, EXT, 32, 128), F32),
            pltpu.VMEM((19, 18, 32, 128), F32),
            pltpu.VMEM((16, 19, 16, 128), F32),
            pltpu.SemaphoreType.DMA((16,)),
        ],
    )
    return pl.pallas_call(
        last_kernel,
        out_shape=jax.ShapeDtypeStruct((19, 16, 16, 128), F32),
        in_specs=[SMEM_SPEC] + [VMEM_SPEC] * 5 + [hbm],
        out_specs=hbm,
        input_output_aliases={6: 0},
        scratch_shapes=[
            pltpu.VMEM((4, SIDE_ROWS, 128), F32),
            pltpu.VMEM((2, 19, 24, 128), F32),
            pltpu.VMEM((38, 16, 128), F32),
            pltpu.SemaphoreType.DMA,
        ],
        compiler_params=pltpu.CompilerParams(vmem_limit_bytes=VMEM_LIMIT),
        cost_estimate=pl.CostEstimate(flops=2_000_000, bytes_accessed=2_000_000, transcendentals=0),
    )(odd, drive, ye, yo, from_ye, from_yo, result)


def solution(mesh):
    return jax.shard_map(
        local,
        mesh=mesh,
        in_specs=(
            P(("gx", "gy"), None, None),
            P(("gx", "gy")),
            P(("gx", "gy"), None, None),
            P(("gx", "gy"), None, None),
            P("gx", "gy", None),
            P(),
        ),
        out_specs=P(None, "gx", "gy", None),
        check_vma=False,
    )
```

```python
import jax
import jax.numpy as jnp
from jax import lax
from jax.experimental import pallas as pl
from jax.experimental.pallas import tpu as pltpu
from jax.sharding import PartitionSpec as P

VELOCITY = (
    (0, 0, 0),
    (1, 0, 0),
    (-1, 0, 0),
    (0, 1, 0),
    (0, -1, 0),
    (0, 0, 1),
    (0, 0, -1),
    (1, 1, 0),
    (-1, -1, 0),
    (1, -1, 0),
    (-1, 1, 0),
    (1, 0, 1),
    (-1, 0, -1),
    (1, 0, -1),
    (-1, 0, 1),
    (0, 1, 1),
    (0, -1, -1),
    (0, 1, -1),
    (0, -1, 1),
)
WEIGHT = [1.0 / 3.0] + [1.0 / 18.0] * 6 + [1.0 / 36.0] * 12
INVERSE = [3.0] + [18.0] * 6 + [36.0] * 12
DEVICES = 128
HELD = 128
CAP = 2
TILE = 38
PAIR = 2 * TILE + 1
ROWS = 41
APART = 257
EXT = 20
VMEM_LIMIT = 48 * 1024 * 1024
VMEM_MOST = 61 * 1024 * 1024
F32 = jnp.float32


def entries(axis, sign):
    far = [(q, 1) for q in range(19) if VELOCITY[q][axis] == sign]
    near = [(q, 0) for q in range(19) if VELOCITY[q][axis] in (0, sign)]
    return far + near


COUNT = 21
SIDE_ROWS = 432


def collide(dist, solid, omega, force):
    plus = [None] * 19
    minus = [None] * 19
    for i in range(1, 19, 2):
        plus[i] = dist[i] + dist[i + 1]
        minus[i] = dist[i] - dist[i + 1]
    density = dist[0]
    for i in range(1, 19, 2):
        density = density + plus[i]
    flow = []
    for axis in range(3):
        total = None
        for i in range(1, 19, 2):
            c = VELOCITY[i][axis]
            if c:
                if total is None:
                    total = minus[i]
                else:
                    total = total + minus[i] if c == 1 else total - minus[i]
        flow.append(total + 0.5 * force[axis])
    base = density - 1.5 * (flow[0] * flow[0] + flow[1] * flow[1] + flow[2] * flow[2])
    open_ = 1.0 - solid
    a = open_ * omega
    b = open_ * ((2.0 - omega) / (1.0 - 0.125 * omega))
    keep = 0.5 - 0.5 * a
    turn = 0.5 - solid - 0.5 * b
    post = [None] * 19
    at = a * base
    post[0] = (keep + keep) * dist[0] + at * (1.0 / 3.0)
    drive = [b * flow[axis] + open_ * force[axis] for axis in range(3)]
    for group, w in ((range(1, 7, 2), 1.0 / 18.0), (range(7, 19, 2), 1.0 / 36.0)):
        even_base = at * w
        square = a * (4.5 * w)
        pull = [drive[axis] * (3.0 * w) for axis in range(3)]
        for i in group:
            along = None
            odd = None
            for axis in range(3):
                c = VELOCITY[i][axis]
                if c:
                    if along is None:
                        along, odd = flow[axis], pull[axis]
                    elif c == 1:
                        along, odd = along + flow[axis], odd + pull[axis]
                    else:
                        along, odd = along - flow[axis], odd - pull[axis]
            even = keep * plus[i] + (even_base + square * (along * along))
            odd = turn * minus[i] + odd
            post[i] = even + odd
            post[i + 1] = even - odd
    return post


def shift_z(value, q):
    c = VELOCITY[q][2]
    return value if c == 0 else pltpu.roll(value, c % 128, 1)


def pack_kernel(target_hbm, pdf_hbm, out, target, used, pdf, tiles, labels, sems, small, sent):
    listing = pltpu.make_async_copy(target_hbm, target, small.at[0])
    listing.start()
    quarters = []
    for part in range(4):
        rows = pl.ds(part * 64, 64)
        copy = pltpu.make_async_copy(pdf_hbm.at[:, rows, :], pdf.at[:, rows, 0, :], sems.at[part])
        copy.start()
        quarters.append(copy)
    flat = pdf.reshape(19 * APART, 128)
    rows_ = tiles.reshape(HELD * TILE, 128)
    empty = jnp.full((8, 128), -1.0, F32)
    for block in range(DEVICES // 8):
        labels[8 * block : 8 * block + 8, 0, :] = empty

    def clear(i, _):
        used[i] = 0
        return 0

    lax.fori_loop(0, DEVICES, clear, 0, unroll=8)
    half = lax.broadcasted_iota(jnp.int32, (1, 128), 1) // 64
    listing.wait()

    def put(k, _):
        t = target[k]
        owner = lax.shift_right_logical(t, 7)
        rank = used[owner]
        used[owner] = rank + 1
        near = lax.shift_right_logical(k, 3) * 16 + (k & 7)
        for r in range(2):
            for q in (0, 8, 16):
                n = min(8, 19 - q)
                value = flat[pl.ds(near + r * 8 + q * APART, n, stride=APART), :]
                rows_[pl.ds(k * TILE + r * 19 + q, n), :] = value
        pltpu.make_async_copy(
            tiles.at[pl.ds(k * TILE, TILE)],
            out.at[owner, pl.ds(rank * TILE, TILE)],
            sent,
        ).start()
        line = labels[owner]
        labels[owner] = jnp.where(half == rank, (t & 127).astype(F32), line)
        return 0

    for part in range(4):
        quarters[part].wait()
        lax.fori_loop(part * 32, part * 32 + 32, put, 0, unroll=4)
    named = pltpu.make_async_copy(labels, out.at[:, 2 * TILE], small.at[1])
    named.start()
    pltpu.make_async_copy(tiles, tiles, sent).wait()
    named.wait()


def pack(target, pdf):
    hbm = pl.BlockSpec(memory_space=pltpu.HBM)
    return pl.pallas_call(
        pack_kernel,
        out_shape=jax.ShapeDtypeStruct((DEVICES, PAIR, 1, 128), F32),
        in_specs=[hbm, hbm],
        out_specs=hbm,
        scratch_shapes=[
            pltpu.SMEM((HELD,), jnp.int32),
            pltpu.SMEM((DEVICES,), jnp.int32),
            pltpu.VMEM((19, APART, 1, 128), F32),
            pltpu.VMEM((HELD * TILE, 1, 128), F32),
            pltpu.VMEM((DEVICES, 1, 128), F32),
            pltpu.SemaphoreType.DMA((4,)),
            pltpu.SemaphoreType.DMA((2,)),
            pltpu.SemaphoreType.DMA,
        ],
        compiler_params=pltpu.CompilerParams(vmem_limit_bytes=VMEM_MOST),
        cost_estimate=pl.CostEstimate(flops=0, bytes_accessed=8_000_000, transcendentals=0),
    )(target, pdf)


def pick(flag, even, odd):
    return jnp.where(flag == 0, even, odd)


def plane_step(x, at, tiles, coef, post, f):
    for r in range(2):
        dist = []
        for q in range(19):
            value = tiles[pl.ds(at * (8 * ROWS) + r * 19 + q, 8, stride=ROWS), :]
            dist.append(WEIGHT[q] * value + WEIGHT[q])
        solid = coef[0, x, pl.ds(r, 8, stride=2), :]
        omega = coef[1, x, pl.ds(r, 8, stride=2), :]
        after = collide(dist, solid, omega, f)
        for q in range(19):
            post[q, at, pl.ds(r, 8, stride=2), :] = shift_z(after[q], q)


def fetch(source, arrived, tiles, sem, slot, at):
    p = source[0, slot]
    pltpu.make_async_copy(
        arrived.at[lax.shift_right_logical(p, 1), pl.ds((p & 1) * TILE, TILE), 0, :],
        tiles.at[pl.ds(at * ROWS, TILE), :],
        sem,
    ).start()


def arrive(tiles, sem):
    whole = tiles.at[pl.ds(0, 8 * TILE), :]
    pltpu.make_async_copy(whole, whole, sem).wait()


def edge_kernel(
    odd, force, arrived, coef, found, edge, xe, xo, tiles, labels, source, sems, small
):
    pull = pltpu.make_async_copy(arrived.at[:, 2 * TILE, 0, :], labels, small.at[0])
    pull.start()
    f = [force[axis : axis + 1, :] for axis in range(3)]
    lane = lax.broadcasted_iota(jnp.int32, (8, 128), 1)
    lane_f = lane.astype(F32)
    sub = lax.broadcasted_iota(jnp.int32, (8, 128), 0)
    low = lane < 64
    total = jnp.zeros((8, 128), jnp.int32)
    pull.wait()
    for group in range(DEVICES // 8):
        line = labels[8 * group : 8 * group + 8, :]
        other = pltpu.roll(line, 64, 1)
        number = (sub + 8 * group) * 2
        total = total + jnp.where(jnp.where(low, line, other) == lane_f, number, 0)
        total = total + jnp.where(jnp.where(low, other, line) == lane_f, number + 1, 0)
    found[...] = jnp.broadcast_to(jnp.sum(total, axis=0, keepdims=True), (8, 128))
    hand = pltpu.make_async_copy(found, source, small.at[1])
    hand.start()
    hand.wait()
    for j, x in enumerate((0, 1, 14, 15)):
        for i in range(8):
            fetch(source, arrived, tiles, sems.at[j], 8 * x + i, 8 * j + i)

    def plane(j, _):
        arrive(tiles, sems.at[j])
        plane_step(jnp.where(j < 2, j, j + 12), j, tiles, coef, edge, f)
        return 0

    lax.fori_loop(0, 4, plane, 0)
    for even in range(2):

        @pl.when(odd[0] == even)
        def _():
            for out, sign in ((xe, 1 - 2 * even), (xo, 2 * even - 1)):
                for i, (q, layer) in enumerate(entries(0, sign)):
                    out[i] = edge[q, 3 - layer if sign == 1 else layer]
                for j in range(2):
                    out[19 + j] = coef[j, 15 if sign == 1 else 0]


def inner_kernel(odd, force, found, arrived, coef, edge, inner, ye, yo, tiles, source, sems, small):
    hand = pltpu.make_async_copy(found, source, small)
    hand.start()
    f = [force[axis : axis + 1, :] for axis in range(3)]
    hand.wait()

    def ask(j):
        for i in range(8):
            fetch(source, arrived, tiles, sems.at[j], 16 + 8 * j + i, 8 * j + i)

    for j in range(4):
        ask(j)

    def plane(j, more):
        if more:
            ask(j + 4)
        arrive(tiles, sems.at[j])
        plane_step(j + 2, j, tiles, coef, inner, f)

    def early(j, _):
        plane(j, True)
        return 0

    def late(j, _):
        plane(j, False)
        return 0

    lax.fori_loop(0, 8, early, 0)
    lax.fori_loop(8, 12, late, 0)
    for even in range(2):

        @pl.when(odd[1] == even)
        def _():
            for out, sign in ((ye, 1 - 2 * even), (yo, 2 * even - 1)):
                for i, (q, layer) in enumerate(entries(1, sign)):
                    row = 15 - layer if sign == 1 else layer
                    for x in range(16):
                        if 2 <= x < 14:
                            value = inner[q, x - 2, row : row + 1, :]
                        else:
                            value = edge[q, x if x < 2 else x - 12, row : row + 1, :]
                        out[i * EXT + 2 + x : i * EXT + 3 + x, :] = value
                row = 15 if sign == 1 else 0
                for j in range(2):
                    for x in range(16):
                        at = (19 + j) * EXT + 2 + x
                        out[at : at + 1, :] = coef[j, x, row : row + 1, :]


VMEM_SPEC = pl.BlockSpec(memory_space=pltpu.VMEM)
SMEM_SPEC = pl.BlockSpec(memory_space=pltpu.SMEM)
FACE = jax.ShapeDtypeStruct((COUNT, 16, 128), F32)
SIDE = jax.ShapeDtypeStruct((SIDE_ROWS, 128), F32)


def call(kernel, out_shape, operands, work, scalars=1, **more):
    return pl.pallas_call(
        kernel,
        out_shape=out_shape,
        in_specs=[SMEM_SPEC] * scalars + [VMEM_SPEC] * (len(operands) - scalars),
        compiler_params=pltpu.CompilerParams(vmem_limit_bytes=VMEM_LIMIT),
        cost_estimate=pl.CostEstimate(flops=work, bytes_accessed=work, transcendentals=0),
        **more,
    )(*operands)


def join_kernel(odd, xe, xo, own_e, own_o, ye, yo):
    for own, out in ((own_e, ye), (own_o, yo)):
        for block in range(SIDE_ROWS // 8):
            out[8 * block : 8 * block + 8, :] = own[8 * block : 8 * block + 8, :]
    have = [
        {e: n for n, e in enumerate(entries(0, toward) + [(19, 0), (20, 0)])} for toward in (1, -1)
    ]
    zero = jnp.zeros((1, 128), F32)
    for even_x in range(2):
        for even_y in range(2):

            @pl.when((odd[0] == even_x) & (odd[1] == even_y))
            def _():
                halves = (xo, xe) if even_x == 0 else (xe, xo)
                for out, sign in ((ye, 1 - 2 * even_y), (yo, 2 * even_y - 1)):
                    for i, (q, layer) in enumerate(entries(1, sign) + [(19, 0), (20, 0)]):
                        row = 15 - layer if sign == 1 else layer
                        for toward in range(2):
                            for deep in range(2):
                                at = i * EXT + ((1 - deep) if toward == 0 else 18 + deep)
                                n = have[toward].get((q, deep))
                                value = zero if n is None else halves[toward][n, row : row + 1, :]
                                out[at : at + 1, :] = value


def middle_kernel(odd, force, edge, inner, coef, xe, xo, out, wide, again, result, sems):
    flag = odd[0]
    for j in range(4):
        for q in range(19):
            wide[q, (j if j < 2 else j + 12) + 2, 8:24, :] = edge[q, j]

    def copy(x, _):
        for q in range(19):
            wide[q, x + 4, 8:24, :] = inner[q, x]
        return 0

    lax.fori_loop(0, 12, copy, 0)
    sides = []
    for toward, sign in ((0, 1), (1, -1)):
        even, odd_ = (xo, xe) if toward == 0 else (xe, xo)
        for i, (q, layer) in enumerate(entries(0, sign)):
            at = 1 - layer if toward == 0 else 18 + layer
            wide[q, at, 8:24, :] = pick(flag, even[i], odd_[i])
        sides.append([pick(flag, even[19 + j], odd_[19 + j]) for j in range(2)])
    f = [force[axis : axis + 1, :] for axis in range(3)]

    def one(x, solids, omegas):
        for block in range(2):
            dist = []
            for q in range(19):
                cx, cy, _z = VELOCITY[q]
                dist.append(wide[q, x + 1 - cx, 8 + 8 * block - cy : 16 + 8 * block - cy, :])
            after = collide(dist, solids[block], omegas[block], f)
            for q in range(19):
                again[q, x, 8 + 8 * block : 16 + 8 * block, :] = shift_z(after[q], q)

    def plane(x, _):
        solids = [coef[0, x - 1, 8 * block : 8 * block + 8, :] for block in range(2)]
        omegas = [coef[1, x - 1, 8 * block : 8 * block + 8, :] for block in range(2)]
        one(x, solids, omegas)
        return 0

    one(0, *[[v[0:8], v[8:16]] for v in sides[0]])
    one(17, *[[v[0:8], v[8:16]] for v in sides[1]])
    lax.fori_loop(1, 17, plane, 0)

    def finish(x, _):
        for q in range(19):
            cx, cy, _z = VELOCITY[q]
            for block in range(2):
                start = 8 + 8 * block - cy
                value = again[q, x + 1 - cx, start : start + 8, :]
                result[x, q, 8 * block : 8 * block + 8, :] = value * INVERSE[q] - 1.0
        pltpu.make_async_copy(result.at[x], out.at[:, x], sems.at[x]).start()
        return 0

    lax.fori_loop(0, 16, finish, 0)
    for x in range(16):
        pltpu.make_async_copy(result.at[x], out.at[:, x], sems.at[x]).wait()


def last_side(side, sign, own, other, out, rows, patch, sem, f):
    came = {e: n for n, e in enumerate(entries(1, sign))}
    mine = {e: n for n, e in enumerate(entries(1, -sign))}
    for line in range(2):
        for block in range(3):
            start = 1 + 8 * block
            dist = []
            for q in range(19):
                cx, cy, _z = VELOCITY[q]
                if cy == sign:
                    which, n = other, came[(q, 1 - line)]
                elif cy == 0:
                    which, n = (other, came[(q, 0)]) if line == 0 else (own, mine[(q, 0)])
                else:
                    which, n = own, mine[(q, line)]
                at = n * EXT + start - cx
                dist.append(which[at : at + 8, :])
            where = other if line == 0 else own
            fixed = [where[(19 + j) * EXT + start : (19 + j) * EXT + start + 8, :] for j in range(2)]
            after = collide(dist, fixed[0], fixed[1], f)
            for q in range(19):
                if VELOCITY[q][1] == sign or (VELOCITY[q][1] == 0 and line == 1):
                    rows[line, q, 8 * block : 8 * block + 8, :] = shift_z(after[q], q)
    number = 19 * side
    for depth in range(2):
        listed = [q for q in range(19) if VELOCITY[q][1] in ((sign, 0) if depth == 0 else (sign,))]
        y = depth if sign == 1 else 15 - depth
        begin = 0
        for n, q in enumerate(listed):
            cx, cy, _z = VELOCITY[q]
            line = 1 if depth == 1 or cy == 0 else 0
            patch[number + n] = rows[line, q, 1 - cx : 17 - cx, :] * INVERSE[q] - 1.0
            if n + 1 == len(listed) or listed[n + 1] != q + 1:
                count = n + 1 - begin
                pltpu.make_async_copy(
                    patch.at[pl.ds(number + begin, count)],
                    out.at[pl.ds(q + 1 - count, count), :, y, :],
                    sem,
                ).start()
                begin = n + 1
        number += len(listed)


def last_kernel(odd, force, mine_e, mine_o, came_e, came_o, _before, out, rows, patch, sem):
    f = [force[axis : axis + 1, :] for axis in range(3)]
    for even in range(2):

        @pl.when(odd[1] == even)
        def _():
            low = (mine_o, came_o) if even == 0 else (mine_e, came_e)
            high = (mine_e, came_e) if even == 0 else (mine_o, came_o)
            last_side(0, 1, *low, out, rows, patch, sem, f)
            last_side(1, -1, *high, out, rows, patch, sem, f)

    pltpu.make_async_copy(patch, patch, sem).wait()


def swap(value, axis, first):
    n = lax.axis_size(axis)
    pairs = [(i, (i + 1) % n if (i % 2 == 0) == first else (i - 1) % n) for i in range(n)]
    return lax.ppermute(value, axis, pairs)


def halves_of(porosity, relaxation):
    lo = lax.axis_index("gy") % 2
    slab = jnp.stack([porosity, relaxation]).reshape(2, 2, 4, 2, 16, 128)
    other = lax.dynamic_index_in_dim(slab, 1 - lo, axis=3, keepdims=False)
    mine = lax.dynamic_index_in_dim(slab, lo, axis=3, keepdims=False)
    return mine, lax.ppermute(other, "gy", [(i, i ^ 1) for i in range(8)])


def pieces_of(mine, came):
    b = lax.axis_index("gy")
    hi, lo = b // 2, b % 2
    both = jnp.stack([jnp.where(lo == 0, mine, came), jnp.where(lo == 0, came, mine)])
    parts = [lax.dynamic_index_in_dim(both, hi, axis=3, keepdims=False)]
    for k in range(1, 4):
        message = lax.dynamic_index_in_dim(both, hi ^ k, axis=3, keepdims=False)
        parts.append(lax.ppermute(message, "gy", [(i, i ^ (2 * k)) for i in range(8)]))
    return parts


def block_of(parts):
    hi = lax.axis_index("gy") // 2
    stacked = jnp.stack(parts)
    ordered = [
        lax.dynamic_index_in_dim(stacked, hi ^ y, axis=0, keepdims=False) for y in range(4)
    ]
    whole = jnp.stack(ordered)
    return whole.transpose(2, 0, 1, 3, 4, 5).reshape(2, 16, 16, 128)


def local(pdf_old, tile_target, porosity, relaxation, solid_mask, force):
    mine, came = halves_of(porosity, relaxation)
    rows = pdf_old.reshape(16, 8, 19, 2, 128).transpose(2, 0, 3, 1, 4).reshape(19, 256, 128)
    packed = pack(tile_target, rows)
    packed, came = lax.optimization_barrier((packed, came))
    arrived = lax.all_to_all(
        packed, ("gx", "gy"), split_axis=0, concat_axis=0, tiled=True
    )
    block = block_of(pieces_of(mine, came))
    solid = block[0] + solid_mask.astype(F32) * (1.0 - block[0])
    coef = jnp.stack([solid, block[1]])
    odd = jnp.stack([lax.axis_index("gx") % 2, lax.axis_index("gy") % 2]).astype(jnp.int32)
    drive = jnp.broadcast_to(jnp.pad(force, (0, 5))[:, None], (8, 128))
    coef, odd, drive = lax.optimization_barrier((coef, odd, drive))
    hbm = pl.BlockSpec(memory_space=pltpu.HBM)
    posts = [jax.ShapeDtypeStruct((19, n, 16, 128), F32) for n in (4, 12)]
    found, edge, xe, xo = pl.pallas_call(
        edge_kernel,
        out_shape=[jax.ShapeDtypeStruct((8, 128), jnp.int32), posts[0], FACE, FACE],
        in_specs=[SMEM_SPEC, VMEM_SPEC, hbm, VMEM_SPEC],
        out_specs=[VMEM_SPEC] * 4,
        scratch_shapes=[
            pltpu.VMEM((32 * ROWS, 128), F32),
            pltpu.VMEM((DEVICES, 128), F32),
            pltpu.SMEM((8, 128), jnp.int32),
            pltpu.SemaphoreType.DMA((4,)),
            pltpu.SemaphoreType.DMA((2,)),
        ],
        compiler_params=pltpu.CompilerParams(vmem_limit_bytes=VMEM_LIMIT),
        cost_estimate=pl.CostEstimate(flops=2_000_000, bytes_accessed=8_000_000, transcendentals=0),
    )(odd, drive, arrived, coef)
    from_xo = swap(xo, "gx", False)
    from_xe = swap(xe, "gx", True)
    inner, own_ye, own_yo = pl.pallas_call(
        inner_kernel,
        out_shape=[posts[1], SIDE, SIDE],
        in_specs=[SMEM_SPEC, VMEM_SPEC, VMEM_SPEC, hbm, VMEM_SPEC, VMEM_SPEC],
        out_specs=[VMEM_SPEC] * 3,
        scratch_shapes=[
            pltpu.VMEM((96 * ROWS, 128), F32),
            pltpu.SMEM((8, 128), jnp.int32),
            pltpu.SemaphoreType.DMA((12,)),
            pltpu.SemaphoreType.DMA,
        ],
        compiler_params=pltpu.CompilerParams(vmem_limit_bytes=VMEM_LIMIT),
        cost_estimate=pl.CostEstimate(flops=6_000_000, bytes_accessed=8_000_000, transcendentals=0),
    )(odd, drive, found, arrived, coef, edge)
    ye, yo = call(join_kernel, [SIDE, SIDE], (odd, from_xe, from_xo, own_ye, own_yo), 500_000)
    from_yo = swap(yo, "gy", False)
    from_ye = swap(ye, "gy", True)
    result = call(
        middle_kernel,
        jax.ShapeDtypeStruct((19, 16, 16, 128), F32),
        (odd, drive, edge, inner, coef, from_xe, from_xo),
        12_000_000,
        out_specs=hbm,
        scratch_shapes=[
            pltpu.VMEM((19, EXT, 32, 128), F32),
            pltpu.VMEM((19, 18, 32, 128), F32),
            pltpu.VMEM((16, 19, 16, 128), F32),
            pltpu.SemaphoreType.DMA((16,)),
        ],
    )
    return pl.pallas_call(
        last_kernel,
        out_shape=jax.ShapeDtypeStruct((19, 16, 16, 128), F32),
        in_specs=[SMEM_SPEC] + [VMEM_SPEC] * 5 + [hbm],
        out_specs=hbm,
        input_output_aliases={6: 0},
        scratch_shapes=[
            pltpu.VMEM((2, 19, 24, 128), F32),
            pltpu.VMEM((38, 16, 128), F32),
            pltpu.SemaphoreType.DMA,
        ],
        compiler_params=pltpu.CompilerParams(vmem_limit_bytes=VMEM_LIMIT),
        cost_estimate=pl.CostEstimate(flops=2_000_000, bytes_accessed=2_000_000, transcendentals=0),
    )(odd, drive, ye, yo, from_ye, from_yo, result)


def solution(mesh):
    return jax.shard_map(
        local,
        mesh=mesh,
        in_specs=(
            P(("gx", "gy"), None, None),
            P(("gx", "gy")),
            P(("gx", "gy"), None, None),
            P(("gx", "gy"), None, None),
            P("gx", "gy", None),
            P(),
        ),
        out_specs=P(None, "gx", "gy", None),
        check_vma=False,
    )
```

```python
import jax
import jax.numpy as jnp
from jax import lax
from jax.experimental import pallas as pl
from jax.experimental.pallas import tpu as pltpu
from jax.sharding import PartitionSpec as P

VELOCITY = (
    (0, 0, 0),
    (1, 0, 0),
    (-1, 0, 0),
    (0, 1, 0),
    (0, -1, 0),
    (0, 0, 1),
    (0, 0, -1),
    (1, 1, 0),
    (-1, -1, 0),
    (1, -1, 0),
    (-1, 1, 0),
    (1, 0, 1),
    (-1, 0, -1),
    (1, 0, -1),
    (-1, 0, 1),
    (0, 1, 1),
    (0, -1, -1),
    (0, 1, -1),
    (0, -1, 1),
)
WEIGHT = [1.0 / 3.0] + [1.0 / 18.0] * 6 + [1.0 / 36.0] * 12
INVERSE = [3.0] + [18.0] * 6 + [36.0] * 12
DEVICES = 128
HELD = 128
CAP = 2
TILE = 38
PAIR = 2 * TILE + 1
ROWS = 41
APART = 257
EXT = 20
VMEM_LIMIT = 48 * 1024 * 1024
VMEM_MOST = 61 * 1024 * 1024
F32 = jnp.float32


def entries(axis, sign):
    far = [(q, 1) for q in range(19) if VELOCITY[q][axis] == sign]
    near = [(q, 0) for q in range(19) if VELOCITY[q][axis] in (0, sign)]
    return far + near


COUNT = 21
SIDE_ROWS = 432


def collide(dist, solid, omega, force):
    plus = [None] * 19
    minus = [None] * 19
    for i in range(1, 19, 2):
        plus[i] = dist[i] + dist[i + 1]
        minus[i] = dist[i] - dist[i + 1]
    density = dist[0]
    for i in range(1, 19, 2):
        density = density + plus[i]
    flow = []
    for axis in range(3):
        total = None
        for i in range(1, 19, 2):
            c = VELOCITY[i][axis]
            if c:
                if total is None:
                    total = minus[i]
                else:
                    total = total + minus[i] if c == 1 else total - minus[i]
        flow.append(total + 0.5 * force[axis])
    base = density - 1.5 * (flow[0] * flow[0] + flow[1] * flow[1] + flow[2] * flow[2])
    open_ = 1.0 - solid
    a = open_ * omega
    b = open_ * ((2.0 - omega) / (1.0 - 0.125 * omega))
    keep = 0.5 - 0.5 * a
    turn = 0.5 - solid - 0.5 * b
    post = [None] * 19
    at = a * base
    post[0] = (keep + keep) * dist[0] + at * (1.0 / 3.0)
    drive = [b * flow[axis] + open_ * force[axis] for axis in range(3)]
    for group, w in ((range(1, 7, 2), 1.0 / 18.0), (range(7, 19, 2), 1.0 / 36.0)):
        even_base = at * w
        square = a * (4.5 * w)
        pull = [drive[axis] * (3.0 * w) for axis in range(3)]
        for i in group:
            along = None
            odd = None
            for axis in range(3):
                c = VELOCITY[i][axis]
                if c:
                    if along is None:
                        along, odd = flow[axis], pull[axis]
                    elif c == 1:
                        along, odd = along + flow[axis], odd + pull[axis]
                    else:
                        along, odd = along - flow[axis], odd - pull[axis]
            even = keep * plus[i] + (even_base + square * (along * along))
            odd = turn * minus[i] + odd
            post[i] = even + odd
            post[i + 1] = even - odd
    return post


def shift_z(value, q):
    c = VELOCITY[q][2]
    return value if c == 0 else pltpu.roll(value, c % 128, 1)


def pack_kernel(target_hbm, pdf_hbm, out, target, used, pdf, tiles, labels, sems, small, sent):
    listing = pltpu.make_async_copy(target_hbm, target, small.at[0])
    listing.start()
    quarters = []
    for part in range(4):
        rows = pl.ds(part * 64, 64)
        copy = pltpu.make_async_copy(pdf_hbm.at[:, rows, :], pdf.at[:, rows, 0, :], sems.at[part])
        copy.start()
        quarters.append(copy)
    flat = pdf.reshape(19 * APART, 128)
    rows_ = tiles.reshape(HELD * TILE, 128)
    empty = jnp.full((8, 128), -1.0, F32)
    for block in range(DEVICES // 8):
        labels[8 * block : 8 * block + 8, 0, :] = empty

    def clear(i, _):
        used[i] = 0
        return 0

    lax.fori_loop(0, DEVICES, clear, 0, unroll=8)
    half = lax.broadcasted_iota(jnp.int32, (1, 128), 1) // 64
    listing.wait()

    def put(k, _):
        t = target[k]
        owner = lax.shift_right_logical(t, 7)
        rank = used[owner]
        used[owner] = rank + 1
        near = lax.shift_right_logical(k, 3) * 16 + (k & 7)
        for r in range(2):
            for q in (0, 8, 16):
                n = min(8, 19 - q)
                value = flat[pl.ds(near + r * 8 + q * APART, n, stride=APART), :]
                rows_[pl.ds(k * TILE + r * 19 + q, n), :] = value
        pltpu.make_async_copy(
            tiles.at[pl.ds(k * TILE, TILE)],
            out.at[owner, pl.ds(rank * TILE, TILE)],
            sent,
        ).start()
        line = labels[owner]
        labels[owner] = jnp.where(half == rank, (t & 127).astype(F32), line)
        return 0

    for part in range(4):
        quarters[part].wait()
        lax.fori_loop(part * 32, part * 32 + 32, put, 0, unroll=4)
    named = pltpu.make_async_copy(labels, out.at[:, 2 * TILE], small.at[1])
    named.start()
    pltpu.make_async_copy(tiles, tiles, sent).wait()
    named.wait()


def pack(target, pdf):
    hbm = pl.BlockSpec(memory_space=pltpu.HBM)
    return pl.pallas_call(
        pack_kernel,
        out_shape=jax.ShapeDtypeStruct((DEVICES, PAIR, 1, 128), F32),
        in_specs=[hbm, hbm],
        out_specs=hbm,
        scratch_shapes=[
            pltpu.SMEM((HELD,), jnp.int32),
            pltpu.SMEM((DEVICES,), jnp.int32),
            pltpu.VMEM((19, APART, 1, 128), F32),
            pltpu.VMEM((HELD * TILE, 1, 128), F32),
            pltpu.VMEM((DEVICES, 1, 128), F32),
            pltpu.SemaphoreType.DMA((4,)),
            pltpu.SemaphoreType.DMA((2,)),
            pltpu.SemaphoreType.DMA,
        ],
        compiler_params=pltpu.CompilerParams(vmem_limit_bytes=VMEM_MOST),
        cost_estimate=pl.CostEstimate(flops=0, bytes_accessed=8_000_000, transcendentals=0),
    )(target, pdf)


def pick(flag, even, odd):
    return jnp.where(flag == 0, even, odd)


def plane_step(x, at, tiles, coef, post, f):
    for r in range(2):
        dist = []
        for q in range(19):
            value = tiles[pl.ds(at * (8 * ROWS) + r * 19 + q, 8, stride=ROWS), :]
            dist.append(WEIGHT[q] * value + WEIGHT[q])
        solid = coef[0, x, pl.ds(r, 8, stride=2), :]
        omega = coef[1, x, pl.ds(r, 8, stride=2), :]
        after = collide(dist, solid, omega, f)
        for q in range(19):
            post[q, at, pl.ds(r, 8, stride=2), :] = shift_z(after[q], q)


def fetch(source, arrived, tiles, sem, slot, at):
    p = source[0, slot]
    pltpu.make_async_copy(
        arrived.at[lax.shift_right_logical(p, 1), pl.ds((p & 1) * TILE, TILE), 0, :],
        tiles.at[pl.ds(at * ROWS, TILE), :],
        sem,
    ).start()


def arrive(tiles, sem):
    whole = tiles.at[pl.ds(0, 8 * TILE), :]
    pltpu.make_async_copy(whole, whole, sem).wait()


def edge_kernel(
    odd, force, arrived, coef, found, edge, xo, xe, tiles, labels, source, sems, small
):
    pull = pltpu.make_async_copy(arrived.at[:, 2 * TILE, 0, :], labels, small.at[0])
    pull.start()
    f = [force[axis : axis + 1, :] for axis in range(3)]
    lane = lax.broadcasted_iota(jnp.int32, (8, 128), 1)
    lane_f = lane.astype(F32)
    sub = lax.broadcasted_iota(jnp.int32, (8, 128), 0)
    low = lane < 64
    total = jnp.zeros((8, 128), jnp.int32)
    pull.wait()
    for group in range(DEVICES // 8):
        line = labels[8 * group : 8 * group + 8, :]
        other = pltpu.roll(line, 64, 1)
        number = (sub + 8 * group) * 2
        total = total + jnp.where(jnp.where(low, line, other) == lane_f, number, 0)
        total = total + jnp.where(jnp.where(low, other, line) == lane_f, number + 1, 0)
    found[...] = jnp.broadcast_to(jnp.sum(total, axis=0, keepdims=True), (8, 128))
    hand = pltpu.make_async_copy(found, source, small.at[1])
    hand.start()
    hand.wait()
    for j, x in enumerate((0, 1, 14, 15)):
        for i in range(8):
            fetch(source, arrived, tiles, sems.at[j], 8 * x + i, 8 * j + i)

    def plane(j, _):
        arrive(tiles, sems.at[j])
        plane_step(jnp.where(j < 2, j, j + 12), j, tiles, coef, edge, f)
        return 0

    lax.fori_loop(0, 4, plane, 0)
    for even in range(2):

        @pl.when(odd[0] == even)
        def _():
            for out, sign in ((xe, 1 - 2 * even), (xo, 2 * even - 1)):
                for i, (q, layer) in enumerate(entries(0, sign)):
                    out[i] = edge[q, 3 - layer if sign == 1 else layer]
                for j in range(2):
                    out[19 + j] = coef[j, 15 if sign == 1 else 0]


def inner_kernel(odd, force, found, arrived, coef, edge, inner, yo, ye, tiles, source, sems, small):
    hand = pltpu.make_async_copy(found, source, small)
    hand.start()
    f = [force[axis : axis + 1, :] for axis in range(3)]
    hand.wait()

    for j in range(12):
        for i in range(8):
            fetch(source, arrived, tiles, sems.at[j], 16 + 8 * j + i, 8 * j + i)

    def plane(j, _):
        arrive(tiles, sems.at[j])
        plane_step(j + 2, j, tiles, coef, inner, f)
        return 0

    lax.fori_loop(0, 12, plane, 0)
    for even in range(2):

        @pl.when(odd[1] == even)
        def _():
            for out, sign in ((ye, 1 - 2 * even), (yo, 2 * even - 1)):
                for i, (q, layer) in enumerate(entries(1, sign)):
                    row = 15 - layer if sign == 1 else layer
                    for x in range(16):
                        if 2 <= x < 14:
                            value = inner[q, x - 2, row : row + 1, :]
                        else:
                            value = edge[q, x if x < 2 else x - 12, row : row + 1, :]
                        out[i * EXT + 2 + x : i * EXT + 3 + x, :] = value
                row = 15 if sign == 1 else 0
                for j in range(2):
                    for x in range(16):
                        at = (19 + j) * EXT + 2 + x
                        out[at : at + 1, :] = coef[j, x, row : row + 1, :]


VMEM_SPEC = pl.BlockSpec(memory_space=pltpu.VMEM)
SMEM_SPEC = pl.BlockSpec(memory_space=pltpu.SMEM)
FACE = jax.ShapeDtypeStruct((COUNT, 16, 128), F32)
SIDE = jax.ShapeDtypeStruct((SIDE_ROWS, 128), F32)


def call(kernel, out_shape, operands, work, scalars=1, **more):
    return pl.pallas_call(
        kernel,
        out_shape=out_shape,
        in_specs=[SMEM_SPEC] * scalars + [VMEM_SPEC] * (len(operands) - scalars),
        compiler_params=pltpu.CompilerParams(vmem_limit_bytes=VMEM_LIMIT),
        cost_estimate=pl.CostEstimate(flops=work, bytes_accessed=work, transcendentals=0),
        **more,
    )(*operands)


def join_kernel(odd, xo, xe, own_o, own_e, yo, ye):
    for own, out in ((own_e, ye), (own_o, yo)):
        for block in range(SIDE_ROWS // 8):
            out[8 * block : 8 * block + 8, :] = own[8 * block : 8 * block + 8, :]
    have = [
        {e: n for n, e in enumerate(entries(0, toward) + [(19, 0), (20, 0)])} for toward in (1, -1)
    ]
    zero = jnp.zeros((1, 128), F32)
    for even_x in range(2):
        for even_y in range(2):

            @pl.when((odd[0] == even_x) & (odd[1] == even_y))
            def _():
                halves = (xo, xe) if even_x == 0 else (xe, xo)
                for out, sign in ((ye, 1 - 2 * even_y), (yo, 2 * even_y - 1)):
                    for i, (q, layer) in enumerate(entries(1, sign) + [(19, 0), (20, 0)]):
                        row = 15 - layer if sign == 1 else layer
                        for toward in range(2):
                            for deep in range(2):
                                at = i * EXT + ((1 - deep) if toward == 0 else 18 + deep)
                                n = have[toward].get((q, deep))
                                value = zero if n is None else halves[toward][n, row : row + 1, :]
                                out[at : at + 1, :] = value


def middle_kernel(odd, force, edge, inner, coef, xo, xe, out, wide, again, result, sems):
    flag = odd[0]
    for j in range(4):
        for q in range(19):
            wide[q, (j if j < 2 else j + 12) + 2, 8:24, :] = edge[q, j]

    def copy(x, _):
        for q in range(19):
            wide[q, x + 4, 8:24, :] = inner[q, x]
        return 0

    lax.fori_loop(0, 12, copy, 0)
    sides = []
    for toward, sign in ((0, 1), (1, -1)):
        even, odd_ = (xo, xe) if toward == 0 else (xe, xo)
        for i, (q, layer) in enumerate(entries(0, sign)):
            at = 1 - layer if toward == 0 else 18 + layer
            wide[q, at, 8:24, :] = pick(flag, even[i], odd_[i])
        sides.append([pick(flag, even[19 + j], odd_[19 + j]) for j in range(2)])
    f = [force[axis : axis + 1, :] for axis in range(3)]

    def one(x, solids, omegas):
        for block in range(2):
            dist = []
            for q in range(19):
                cx, cy, _z = VELOCITY[q]
                dist.append(wide[q, x + 1 - cx, 8 + 8 * block - cy : 16 + 8 * block - cy, :])
            after = collide(dist, solids[block], omegas[block], f)
            for q in range(19):
                again[q, x, 8 + 8 * block : 16 + 8 * block, :] = shift_z(after[q], q)

    def plane(x, _):
        solids = [coef[0, x - 1, 8 * block : 8 * block + 8, :] for block in range(2)]
        omegas = [coef[1, x - 1, 8 * block : 8 * block + 8, :] for block in range(2)]
        one(x, solids, omegas)
        return 0

    one(0, *[[v[0:8], v[8:16]] for v in sides[0]])
    one(17, *[[v[0:8], v[8:16]] for v in sides[1]])
    lax.fori_loop(1, 17, plane, 0)

    def finish(x, _):
        for q in range(19):
            cx, cy, _z = VELOCITY[q]
            for block in range(2):
                start = 8 + 8 * block - cy
                value = again[q, x + 1 - cx, start : start + 8, :]
                result[x, q, 8 * block : 8 * block + 8, :] = value * INVERSE[q] - 1.0
        pltpu.make_async_copy(result.at[x], out.at[:, x], sems.at[x]).start()
        return 0

    lax.fori_loop(0, 16, finish, 0)
    for x in range(16):
        pltpu.make_async_copy(result.at[x], out.at[:, x], sems.at[x]).wait()


def last_side(side, sign, own, other, out, rows, patch, sem, f):
    came = {e: n for n, e in enumerate(entries(1, sign))}
    mine = {e: n for n, e in enumerate(entries(1, -sign))}
    for line in range(2):
        for block in range(3):
            start = 1 + 8 * block
            dist = []
            for q in range(19):
                cx, cy, _z = VELOCITY[q]
                if cy == sign:
                    which, n = other, came[(q, 1 - line)]
                elif cy == 0:
                    which, n = (other, came[(q, 0)]) if line == 0 else (own, mine[(q, 0)])
                else:
                    which, n = own, mine[(q, line)]
                at = n * EXT + start - cx
                dist.append(which[at : at + 8, :])
            where = other if line == 0 else own
            fixed = [where[(19 + j) * EXT + start : (19 + j) * EXT + start + 8, :] for j in range(2)]
            after = collide(dist, fixed[0], fixed[1], f)
            for q in range(19):
                if VELOCITY[q][1] == sign or (VELOCITY[q][1] == 0 and line == 1):
                    rows[line, q, 8 * block : 8 * block + 8, :] = shift_z(after[q], q)
    number = 19 * side
    for depth in range(2):
        listed = [q for q in range(19) if VELOCITY[q][1] in ((sign, 0) if depth == 0 else (sign,))]
        y = depth if sign == 1 else 15 - depth
        begin = 0
        for n, q in enumerate(listed):
            cx, cy, _z = VELOCITY[q]
            line = 1 if depth == 1 or cy == 0 else 0
            patch[number + n] = rows[line, q, 1 - cx : 17 - cx, :] * INVERSE[q] - 1.0
            if n + 1 == len(listed) or listed[n + 1] != q + 1:
                count = n + 1 - begin
                pltpu.make_async_copy(
                    patch.at[pl.ds(number + begin, count)],
                    out.at[pl.ds(q + 1 - count, count), :, y, :],
                    sem,
                ).start()
                begin = n + 1
        number += len(listed)


def last_kernel(odd, force, mine_o, mine_e, came_o, came_e, _before, out, rows, patch, sem):
    f = [force[axis : axis + 1, :] for axis in range(3)]
    for even in range(2):

        @pl.when(odd[1] == even)
        def _():
            low = (mine_o, came_o) if even == 0 else (mine_e, came_e)
            high = (mine_e, came_e) if even == 0 else (mine_o, came_o)
            last_side(0, 1, *low, out, rows, patch, sem, f)
            last_side(1, -1, *high, out, rows, patch, sem, f)

    pltpu.make_async_copy(patch, patch, sem).wait()


def swap(value, axis, first):
    n = lax.axis_size(axis)
    pairs = [(i, (i + 1) % n if (i % 2 == 0) == first else (i - 1) % n) for i in range(n)]
    return lax.ppermute(value, axis, pairs)


def halves_of(porosity, relaxation):
    lo = lax.axis_index("gy") % 2
    slab = jnp.stack([porosity, relaxation]).reshape(2, 2, 4, 2, 16, 128)
    other = lax.dynamic_index_in_dim(slab, 1 - lo, axis=3, keepdims=False)
    mine = lax.dynamic_index_in_dim(slab, lo, axis=3, keepdims=False)
    return mine, lax.ppermute(other, "gy", [(i, i ^ 1) for i in range(8)])


def pieces_of(mine, came):
    b = lax.axis_index("gy")
    hi, lo = b // 2, b % 2
    both = jnp.stack([jnp.where(lo == 0, mine, came), jnp.where(lo == 0, came, mine)])
    parts = [lax.dynamic_index_in_dim(both, hi, axis=3, keepdims=False)]
    for k in range(1, 4):
        message = lax.dynamic_index_in_dim(both, hi ^ k, axis=3, keepdims=False)
        parts.append(lax.ppermute(message, "gy", [(i, i ^ (2 * k)) for i in range(8)]))
    return parts


def block_of(parts):
    hi = lax.axis_index("gy") // 2
    stacked = jnp.stack(parts)
    ordered = [
        lax.dynamic_index_in_dim(stacked, hi ^ y, axis=0, keepdims=False) for y in range(4)
    ]
    whole = jnp.stack(ordered)
    return whole.transpose(2, 0, 1, 3, 4, 5).reshape(2, 16, 16, 128)


def local(pdf_old, tile_target, porosity, relaxation, solid_mask, force):
    mine, came = halves_of(porosity, relaxation)
    rows = pdf_old.reshape(16, 8, 19, 2, 128).transpose(2, 0, 3, 1, 4).reshape(19, 256, 128)
    packed = pack(tile_target, rows)
    packed, came = lax.optimization_barrier((packed, came))
    arrived = lax.all_to_all(
        packed, ("gx", "gy"), split_axis=0, concat_axis=0, tiled=True
    )
    block = block_of(pieces_of(mine, came))
    solid = block[0] + solid_mask.astype(F32) * (1.0 - block[0])
    coef = jnp.stack([solid, block[1]])
    odd = jnp.stack([lax.axis_index("gx") % 2, lax.axis_index("gy") % 2]).astype(jnp.int32)
    drive = jnp.broadcast_to(jnp.pad(force, (0, 5))[:, None], (8, 128))
    coef, odd, drive = lax.optimization_barrier((coef, odd, drive))
    hbm = pl.BlockSpec(memory_space=pltpu.HBM)
    posts = [jax.ShapeDtypeStruct((19, n, 16, 128), F32) for n in (4, 12)]
    found, edge, xo, xe = pl.pallas_call(
        edge_kernel,
        out_shape=[jax.ShapeDtypeStruct((8, 128), jnp.int32), posts[0], FACE, FACE],
        in_specs=[SMEM_SPEC, VMEM_SPEC, hbm, VMEM_SPEC],
        out_specs=[VMEM_SPEC] * 4,
        scratch_shapes=[
            pltpu.VMEM((32 * ROWS, 128), F32),
            pltpu.VMEM((DEVICES, 128), F32),
            pltpu.SMEM((8, 128), jnp.int32),
            pltpu.SemaphoreType.DMA((4,)),
            pltpu.SemaphoreType.DMA((2,)),
        ],
        compiler_params=pltpu.CompilerParams(vmem_limit_bytes=VMEM_LIMIT),
        cost_estimate=pl.CostEstimate(flops=2_000_000, bytes_accessed=8_000_000, transcendentals=0),
    )(odd, drive, arrived, coef)
    from_xo = swap(xo, "gx", False)
    from_xe = swap(xe, "gx", True)
    inner, own_yo, own_ye = pl.pallas_call(
        inner_kernel,
        out_shape=[posts[1], SIDE, SIDE],
        in_specs=[SMEM_SPEC, VMEM_SPEC, VMEM_SPEC, hbm, VMEM_SPEC, VMEM_SPEC],
        out_specs=[VMEM_SPEC] * 3,
        scratch_shapes=[
            pltpu.VMEM((96 * ROWS, 128), F32),
            pltpu.SMEM((8, 128), jnp.int32),
            pltpu.SemaphoreType.DMA((12,)),
            pltpu.SemaphoreType.DMA,
        ],
        compiler_params=pltpu.CompilerParams(vmem_limit_bytes=VMEM_LIMIT),
        cost_estimate=pl.CostEstimate(flops=6_000_000, bytes_accessed=8_000_000, transcendentals=0),
    )(odd, drive, found, arrived, coef, edge)
    yo, ye = call(join_kernel, [SIDE, SIDE], (odd, from_xo, from_xe, own_yo, own_ye), 500_000)
    from_yo = swap(yo, "gy", False)
    from_ye = swap(ye, "gy", True)
    result = call(
        middle_kernel,
        jax.ShapeDtypeStruct((19, 16, 16, 128), F32),
        (odd, drive, edge, inner, coef, from_xo, from_xe),
        12_000_000,
        out_specs=hbm,
        scratch_shapes=[
            pltpu.VMEM((19, EXT, 32, 128), F32),
            pltpu.VMEM((19, 18, 32, 128), F32),
            pltpu.VMEM((16, 19, 16, 128), F32),
            pltpu.SemaphoreType.DMA((16,)),
        ],
    )
    return pl.pallas_call(
        last_kernel,
        out_shape=jax.ShapeDtypeStruct((19, 16, 16, 128), F32),
        in_specs=[SMEM_SPEC] + [VMEM_SPEC] * 5 + [hbm],
        out_specs=hbm,
        input_output_aliases={6: 0},
        scratch_shapes=[
            pltpu.VMEM((2, 19, 24, 128), F32),
            pltpu.VMEM((38, 16, 128), F32),
            pltpu.SemaphoreType.DMA,
        ],
        compiler_params=pltpu.CompilerParams(vmem_limit_bytes=VMEM_LIMIT),
        cost_estimate=pl.CostEstimate(flops=2_000_000, bytes_accessed=2_000_000, transcendentals=0),
    )(odd, drive, yo, ye, from_yo, from_ye, result)


def solution(mesh):
    return jax.shard_map(
        local,
        mesh=mesh,
        in_specs=(
            P(("gx", "gy"), None, None),
            P(("gx", "gy")),
            P(("gx", "gy"), None, None),
            P(("gx", "gy"), None, None),
            P("gx", "gy", None),
            P(),
        ),
        out_specs=P(None, "gx", "gy", None),
        check_vma=False,
    )
```

```python
import jax
import jax.numpy as jnp
from jax import lax
from jax.experimental import pallas as pl
from jax.experimental.pallas import tpu as pltpu
from jax.sharding import PartitionSpec as P

VELOCITY = (
    (0, 0, 0),
    (1, 0, 0),
    (-1, 0, 0),
    (0, 1, 0),
    (0, -1, 0),
    (0, 0, 1),
    (0, 0, -1),
    (1, 1, 0),
    (-1, -1, 0),
    (1, -1, 0),
    (-1, 1, 0),
    (1, 0, 1),
    (-1, 0, -1),
    (1, 0, -1),
    (-1, 0, 1),
    (0, 1, 1),
    (0, -1, -1),
    (0, 1, -1),
    (0, -1, 1),
)
WEIGHT = [1.0 / 3.0] + [1.0 / 18.0] * 6 + [1.0 / 36.0] * 12
INVERSE = [3.0] + [18.0] * 6 + [36.0] * 12
DEVICES = 128
HELD = 128
CAP = 2
TILE = 38
PAIR = 2 * TILE + 1
ROWS = 41
APART = 257
EXT = 20
VMEM_LIMIT = 48 * 1024 * 1024
VMEM_MOST = 61 * 1024 * 1024
F32 = jnp.float32


def entries(axis, sign):
    far = [(q, 1) for q in range(19) if VELOCITY[q][axis] == sign]
    near = [(q, 0) for q in range(19) if VELOCITY[q][axis] in (0, sign)]
    return far + near


COUNT = 21
SIDE_ROWS = 432
CORNER_ROWS = 88


def collide(dist, solid, omega, force):
    plus = [None] * 19
    minus = [None] * 19
    for i in range(1, 19, 2):
        plus[i] = dist[i] + dist[i + 1]
        minus[i] = dist[i] - dist[i + 1]
    density = dist[0]
    for i in range(1, 19, 2):
        density = density + plus[i]
    flow = []
    for axis in range(3):
        total = None
        for i in range(1, 19, 2):
            c = VELOCITY[i][axis]
            if c:
                if total is None:
                    total = minus[i]
                else:
                    total = total + minus[i] if c == 1 else total - minus[i]
        flow.append(total + 0.5 * force[axis])
    base = density - 1.5 * (flow[0] * flow[0] + flow[1] * flow[1] + flow[2] * flow[2])
    open_ = 1.0 - solid
    a = open_ * omega
    b = open_ * ((2.0 - omega) / (1.0 - 0.125 * omega))
    keep = 0.5 - 0.5 * a
    turn = 0.5 - solid - 0.5 * b
    post = [None] * 19
    at = a * base
    post[0] = (keep + keep) * dist[0] + at * (1.0 / 3.0)
    drive = [b * flow[axis] + open_ * force[axis] for axis in range(3)]
    for group, w in ((range(1, 7, 2), 1.0 / 18.0), (range(7, 19, 2), 1.0 / 36.0)):
        even_base = at * w
        square = a * (4.5 * w)
        pull = [drive[axis] * (3.0 * w) for axis in range(3)]
        for i in group:
            along = None
            odd = None
            for axis in range(3):
                c = VELOCITY[i][axis]
                if c:
                    if along is None:
                        along, odd = flow[axis], pull[axis]
                    elif c == 1:
                        along, odd = along + flow[axis], odd + pull[axis]
                    else:
                        along, odd = along - flow[axis], odd - pull[axis]
            even = keep * plus[i] + (even_base + square * (along * along))
            odd = turn * minus[i] + odd
            post[i] = even + odd
            post[i + 1] = even - odd
    return post


def shift_z(value, q):
    c = VELOCITY[q][2]
    return value if c == 0 else pltpu.roll(value, c % 128, 1)


def pack_kernel(target_hbm, pdf_hbm, out, target, used, pdf, tiles, labels, sems, small, sent):
    listing = pltpu.make_async_copy(target_hbm, target, small.at[0])
    listing.start()
    quarters = []
    for part in range(4):
        rows = pl.ds(part * 64, 64)
        copy = pltpu.make_async_copy(pdf_hbm.at[:, rows, :], pdf.at[:, rows, 0, :], sems.at[part])
        copy.start()
        quarters.append(copy)
    flat = pdf.reshape(19 * APART, 128)
    rows_ = tiles.reshape(HELD * TILE, 128)
    empty = jnp.full((8, 128), -1.0, F32)
    for block in range(DEVICES // 8):
        labels[8 * block : 8 * block + 8, 0, :] = empty

    def clear(i, _):
        used[i] = 0
        return 0

    lax.fori_loop(0, DEVICES, clear, 0, unroll=8)
    half = lax.broadcasted_iota(jnp.int32, (1, 128), 1) // 64
    listing.wait()

    def put(k, _):
        t = target[k]
        owner = lax.shift_right_logical(t, 7)
        rank = used[owner]
        used[owner] = rank + 1
        near = lax.shift_right_logical(k, 3) * 16 + (k & 7)
        for r in range(2):
            for q in (0, 8, 16):
                n = min(8, 19 - q)
                value = flat[pl.ds(near + r * 8 + q * APART, n, stride=APART), :]
                rows_[pl.ds(k * TILE + r * 19 + q, n), :] = value
        pltpu.make_async_copy(
            tiles.at[pl.ds(k * TILE, TILE)],
            out.at[owner, pl.ds(rank * TILE, TILE)],
            sent,
        ).start()
        line = labels[owner]
        labels[owner] = jnp.where(half == rank, (t & 127).astype(F32), line)
        return 0

    for part in range(4):
        quarters[part].wait()
        lax.fori_loop(part * 32, part * 32 + 32, put, 0, unroll=4)
    named = pltpu.make_async_copy(labels, out.at[:, 2 * TILE], small.at[1])
    named.start()
    pltpu.make_async_copy(tiles, tiles, sent).wait()
    named.wait()


def pack(target, pdf):
    hbm = pl.BlockSpec(memory_space=pltpu.HBM)
    return pl.pallas_call(
        pack_kernel,
        out_shape=jax.ShapeDtypeStruct((DEVICES, PAIR, 1, 128), F32),
        in_specs=[hbm, hbm],
        out_specs=hbm,
        scratch_shapes=[
            pltpu.SMEM((HELD,), jnp.int32),
            pltpu.SMEM((DEVICES,), jnp.int32),
            pltpu.VMEM((19, APART, 1, 128), F32),
            pltpu.VMEM((HELD * TILE, 1, 128), F32),
            pltpu.VMEM((DEVICES, 1, 128), F32),
            pltpu.SemaphoreType.DMA((4,)),
            pltpu.SemaphoreType.DMA((2,)),
            pltpu.SemaphoreType.DMA,
        ],
        compiler_params=pltpu.CompilerParams(vmem_limit_bytes=VMEM_MOST),
        cost_estimate=pl.CostEstimate(flops=0, bytes_accessed=8_000_000, transcendentals=0),
    )(target, pdf)


def pick(flag, even, odd):
    return jnp.where(flag == 0, even, odd)


def plane_step(x, place, at, tiles, coef, post, f):
    for r in range(2):
        dist = []
        for q in range(19):
            value = tiles[pl.ds(place * (8 * ROWS) + r * 19 + q, 8, stride=ROWS), :]
            dist.append(WEIGHT[q] * value + WEIGHT[q])
        solid = coef[0, x, pl.ds(r, 8, stride=2), :]
        omega = coef[1, x, pl.ds(r, 8, stride=2), :]
        after = collide(dist, solid, omega, f)
        for q in range(19):
            post[q, at, pl.ds(r, 8, stride=2), :] = shift_z(after[q], q)


def fetch(source, arrived, tiles, sem, slot, at):
    p = source[0, slot]
    pltpu.make_async_copy(
        arrived.at[lax.shift_right_logical(p, 1), pl.ds((p & 1) * TILE, TILE), 0, :],
        tiles.at[pl.ds(at * ROWS, TILE), :],
        sem,
    ).start()


def arrive(tiles, sem):
    whole = tiles.at[pl.ds(0, 8 * TILE), :]
    pltpu.make_async_copy(whole, whole, sem).wait()


def edge_kernel(
    odd, force, arrived, coef, tiles, edge, xe, xo, labels, found, source, sems, small
):
    pull = pltpu.make_async_copy(arrived.at[:, 2 * TILE, 0, :], labels, small.at[0])
    pull.start()
    f = [force[axis : axis + 1, :] for axis in range(3)]
    lane = lax.broadcasted_iota(jnp.int32, (8, 128), 1)
    lane_f = lane.astype(F32)
    sub = lax.broadcasted_iota(jnp.int32, (8, 128), 0)
    low = lane < 64
    total = jnp.zeros((8, 128), jnp.int32)
    pull.wait()
    for group in range(DEVICES // 8):
        line = labels[8 * group : 8 * group + 8, :]
        other = pltpu.roll(line, 64, 1)
        number = (sub + 8 * group) * 2
        total = total + jnp.where(jnp.where(low, line, other) == lane_f, number, 0)
        total = total + jnp.where(jnp.where(low, other, line) == lane_f, number + 1, 0)
    found[...] = jnp.broadcast_to(jnp.sum(total, axis=0, keepdims=True), (8, 128))
    hand = pltpu.make_async_copy(found, source, small.at[1])
    hand.start()
    hand.wait()
    for x in (0, 1, 14, 15):
        for i in range(8):
            fetch(source, arrived, tiles, sems.at[x], 8 * x + i, 8 * x + i)

    def plane(j, _):
        x = jnp.where(j < 2, j, j + 12)
        for i in range(24):
            slot = 16 + 24 * j + i
            fetch(source, arrived, tiles, sems.at[2 + 3 * j + i // 8], slot, slot)
        arrive(tiles, sems.at[x])
        plane_step(x, x, j, tiles, coef, edge, f)
        return 0

    lax.fori_loop(0, 4, plane, 0)
    for even in range(2):

        @pl.when(odd[0] == even)
        def _():
            for out, sign in ((xe, 1 - 2 * even), (xo, 2 * even - 1)):
                for i, (q, layer) in enumerate(entries(0, sign)):
                    out[i] = edge[q, 3 - layer if sign == 1 else layer]
                for j in range(2):
                    out[19 + j] = coef[j, 15 if sign == 1 else 0]

    for x in range(2, 14):
        arrive(tiles, sems.at[x])


def inner_kernel(odd, force, tiles, coef, edge, inner, ye, yo):
    f = [force[axis : axis + 1, :] for axis in range(3)]

    def plane(j, _):
        plane_step(j + 2, j + 2, j, tiles, coef, inner, f)
        return 0

    lax.fori_loop(0, 12, plane, 0)
    for even in range(2):

        @pl.when(odd[1] == even)
        def _():
            for out, sign in ((ye, 1 - 2 * even), (yo, 2 * even - 1)):
                for i, (q, layer) in enumerate(entries(1, sign)):
                    row = 15 - layer if sign == 1 else layer
                    for x in range(16):
                        if 2 <= x < 14:
                            value = inner[q, x - 2, row : row + 1, :]
                        else:
                            value = edge[q, x if x < 2 else x - 12, row : row + 1, :]
                        out[i, x : x + 1, :] = value
                row = 15 if sign == 1 else 0
                for j in range(2):
                    for x in range(16):
                        out[19 + j, x : x + 1, :] = coef[j, x, row : row + 1, :]


VMEM_SPEC = pl.BlockSpec(memory_space=pltpu.VMEM)
SMEM_SPEC = pl.BlockSpec(memory_space=pltpu.SMEM)
FACE = jax.ShapeDtypeStruct((COUNT, 16, 128), F32)
SIDE = jax.ShapeDtypeStruct((SIDE_ROWS, 128), F32)
CORNER = jax.ShapeDtypeStruct((CORNER_ROWS, 128), F32)


def call(kernel, out_shape, operands, work, scalars=1, **more):
    return pl.pallas_call(
        kernel,
        out_shape=out_shape,
        in_specs=[SMEM_SPEC] * scalars + [VMEM_SPEC] * (len(operands) - scalars),
        compiler_params=pltpu.CompilerParams(vmem_limit_bytes=VMEM_LIMIT),
        cost_estimate=pl.CostEstimate(flops=work, bytes_accessed=work, transcendentals=0),
        **more,
    )(*operands)


def corner_kernel(odd, xe, xo, ce, co):
    have = [
        {e: n for n, e in enumerate(entries(0, toward) + [(19, 0), (20, 0)])} for toward in (1, -1)
    ]
    zero = jnp.zeros((1, 128), F32)
    for out in (ce, co):
        out[CORNER_ROWS - 8 : CORNER_ROWS, :] = jnp.zeros((8, 128), F32)
    for even_x in range(2):
        for even_y in range(2):

            @pl.when((odd[0] == even_x) & (odd[1] == even_y))
            def _():
                halves = (xo, xe) if even_x == 0 else (xe, xo)
                for out, sign in ((ce, 1 - 2 * even_y), (co, 2 * even_y - 1)):
                    for i, (q, layer) in enumerate(entries(1, sign) + [(19, 0), (20, 0)]):
                        row = 15 - layer if sign == 1 else layer
                        for column, (toward, deep) in enumerate(((0, 1), (0, 0), (1, 0), (1, 1))):
                            n = have[toward].get((q, deep))
                            value = zero if n is None else halves[toward][n, row : row + 1, :]
                            at = 4 * i + column
                            out[at : at + 1, :] = value


def widen(rows, ends, out):
    for i in range(COUNT):
        at = i * EXT
        out[at : at + 2, :] = ends[4 * i : 4 * i + 2, :]
        out[at + 2 : at + 18, :] = rows[i]
        out[at + 18 : at + 20, :] = ends[4 * i + 2 : 4 * i + 4, :]
    out[COUNT * EXT : SIDE_ROWS, :] = jnp.zeros((SIDE_ROWS - COUNT * EXT, 128), F32)


def middle_kernel(
    odd, force, edge, inner, coef, xe, xo, ye, yo, ce, co, out, own_e, own_o, wide, again, result, sems
):
    flag = odd[0]
    for j in range(4):
        for q in range(19):
            wide[q, (j if j < 2 else j + 12) + 2, 8:24, :] = edge[q, j]

    def copy(x, _):
        for q in range(19):
            wide[q, x + 4, 8:24, :] = inner[q, x]
        return 0

    lax.fori_loop(0, 12, copy, 0)
    sides = []
    for toward, sign in ((0, 1), (1, -1)):
        even, odd_ = (xo, xe) if toward == 0 else (xe, xo)
        for i, (q, layer) in enumerate(entries(0, sign)):
            at = 1 - layer if toward == 0 else 18 + layer
            wide[q, at, 8:24, :] = pick(flag, even[i], odd_[i])
        sides.append([pick(flag, even[19 + j], odd_[19 + j]) for j in range(2)])
    f = [force[axis : axis + 1, :] for axis in range(3)]

    def one(x, solids, omegas):
        for block in range(2):
            dist = []
            for q in range(19):
                cx, cy, _z = VELOCITY[q]
                dist.append(wide[q, x + 1 - cx, 8 + 8 * block - cy : 16 + 8 * block - cy, :])
            after = collide(dist, solids[block], omegas[block], f)
            for q in range(19):
                again[q, x, 8 + 8 * block : 16 + 8 * block, :] = shift_z(after[q], q)

    def plane(x, _):
        solids = [coef[0, x - 1, 8 * block : 8 * block + 8, :] for block in range(2)]
        omegas = [coef[1, x - 1, 8 * block : 8 * block + 8, :] for block in range(2)]
        one(x, solids, omegas)
        return 0

    one(0, *[[v[0:8], v[8:16]] for v in sides[0]])
    one(17, *[[v[0:8], v[8:16]] for v in sides[1]])
    lax.fori_loop(1, 17, plane, 0)

    def finish(x, _):
        for q in range(19):
            cx, cy, _z = VELOCITY[q]
            for block in range(2):
                start = 8 + 8 * block - cy
                value = again[q, x + 1 - cx, start : start + 8, :]
                result[x, q, 8 * block : 8 * block + 8, :] = value * INVERSE[q] - 1.0
        pltpu.make_async_copy(result.at[x], out.at[:, x], sems.at[x]).start()
        return 0

    lax.fori_loop(0, 16, finish, 0)
    widen(ye, ce, own_e)
    widen(yo, co, own_o)
    for x in range(16):
        pltpu.make_async_copy(result.at[x], out.at[:, x], sems.at[x]).wait()


def last_side(side, sign, own, other, out, rows, patch, sem, f):
    came = {e: n for n, e in enumerate(entries(1, sign))}
    mine = {e: n for n, e in enumerate(entries(1, -sign))}
    for line in range(2):
        for block in range(3):
            start = 1 + 8 * block
            dist = []
            for q in range(19):
                cx, cy, _z = VELOCITY[q]
                if cy == sign:
                    which, n = other, came[(q, 1 - line)]
                elif cy == 0:
                    which, n = (other, came[(q, 0)]) if line == 0 else (own, mine[(q, 0)])
                else:
                    which, n = own, mine[(q, line)]
                at = n * EXT + start - cx
                dist.append(which[at : at + 8, :])
            where = other if line == 0 else own
            fixed = [where[(19 + j) * EXT + start : (19 + j) * EXT + start + 8, :] for j in range(2)]
            after = collide(dist, fixed[0], fixed[1], f)
            for q in range(19):
                if VELOCITY[q][1] == sign or (VELOCITY[q][1] == 0 and line == 1):
                    rows[line, q, 8 * block : 8 * block + 8, :] = shift_z(after[q], q)
    number = 19 * side
    for depth in range(2):
        listed = [q for q in range(19) if VELOCITY[q][1] in ((sign, 0) if depth == 0 else (sign,))]
        y = depth if sign == 1 else 15 - depth
        begin = 0
        for n, q in enumerate(listed):
            cx, cy, _z = VELOCITY[q]
            line = 1 if depth == 1 or cy == 0 else 0
            patch[number + n] = rows[line, q, 1 - cx : 17 - cx, :] * INVERSE[q] - 1.0
            if n + 1 == len(listed) or listed[n + 1] != q + 1:
                count = n + 1 - begin
                pltpu.make_async_copy(
                    patch.at[pl.ds(number + begin, count)],
                    out.at[pl.ds(q + 1 - count, count), :, y, :],
                    sem,
                ).start()
                begin = n + 1
        number += len(listed)


def last_kernel(
    odd, force, mine_e, mine_o, rows_e, rows_o, ends_e, ends_o, _before, out, came_e, came_o, rows, patch, sem
):
    widen(rows_e, ends_e, came_e)
    widen(rows_o, ends_o, came_o)
    f = [force[axis : axis + 1, :] for axis in range(3)]
    for even in range(2):

        @pl.when(odd[1] == even)
        def _():
            low = (mine_o, came_o) if even == 0 else (mine_e, came_e)
            high = (mine_e, came_e) if even == 0 else (mine_o, came_o)
            last_side(0, 1, *low, out, rows, patch, sem, f)
            last_side(1, -1, *high, out, rows, patch, sem, f)

    pltpu.make_async_copy(patch, patch, sem).wait()


def swap(value, axis, first):
    n = lax.axis_size(axis)
    pairs = [(i, (i + 1) % n if (i % 2 == 0) == first else (i - 1) % n) for i in range(n)]
    return lax.ppermute(value, axis, pairs)


def halves_of(porosity, relaxation):
    lo = lax.axis_index("gy") % 2
    slab = jnp.stack([porosity, relaxation]).reshape(2, 2, 4, 2, 16, 128)
    other = lax.dynamic_index_in_dim(slab, 1 - lo, axis=3, keepdims=False)
    mine = lax.dynamic_index_in_dim(slab, lo, axis=3, keepdims=False)
    return mine, lax.ppermute(other, "gy", [(i, i ^ 1) for i in range(8)])


def pieces_of(mine, came):
    b = lax.axis_index("gy")
    hi, lo = b // 2, b % 2
    both = jnp.stack([jnp.where(lo == 0, mine, came), jnp.where(lo == 0, came, mine)])
    parts = [lax.dynamic_index_in_dim(both, hi, axis=3, keepdims=False)]
    for k in range(1, 4):
        message = lax.dynamic_index_in_dim(both, hi ^ k, axis=3, keepdims=False)
        parts.append(lax.ppermute(message, "gy", [(i, i ^ (2 * k)) for i in range(8)]))
    return parts


def block_of(parts):
    hi = lax.axis_index("gy") // 2
    stacked = jnp.stack(parts)
    ordered = [
        lax.dynamic_index_in_dim(stacked, hi ^ y, axis=0, keepdims=False) for y in range(4)
    ]
    whole = jnp.stack(ordered)
    return whole.transpose(2, 0, 1, 3, 4, 5).reshape(2, 16, 16, 128)


def local(pdf_old, tile_target, porosity, relaxation, solid_mask, force):
    mine, came = halves_of(porosity, relaxation)
    rows = pdf_old.reshape(16, 8, 19, 2, 128).transpose(2, 0, 3, 1, 4).reshape(19, 256, 128)
    packed = pack(tile_target, rows)
    packed, came = lax.optimization_barrier((packed, came))
    arrived = lax.all_to_all(
        packed, ("gx", "gy"), split_axis=0, concat_axis=0, tiled=True
    )
    block = block_of(pieces_of(mine, came))
    solid = block[0] + solid_mask.astype(F32) * (1.0 - block[0])
    coef = jnp.stack([solid, block[1]])
    odd = jnp.stack([lax.axis_index("gx") % 2, lax.axis_index("gy") % 2]).astype(jnp.int32)
    drive = jnp.broadcast_to(jnp.pad(force, (0, 5))[:, None], (8, 128))
    coef, odd, drive = lax.optimization_barrier((coef, odd, drive))
    hbm = pl.BlockSpec(memory_space=pltpu.HBM)
    posts = [jax.ShapeDtypeStruct((19, n, 16, 128), F32) for n in (4, 12)]
    tiles, edge, xe, xo = pl.pallas_call(
        edge_kernel,
        out_shape=[jax.ShapeDtypeStruct((HELD * ROWS, 128), F32), posts[0], FACE, FACE],
        in_specs=[SMEM_SPEC, VMEM_SPEC, hbm, VMEM_SPEC],
        out_specs=[VMEM_SPEC] * 4,
        scratch_shapes=[
            pltpu.VMEM((DEVICES, 128), F32),
            pltpu.VMEM((8, 128), jnp.int32),
            pltpu.SMEM((8, 128), jnp.int32),
            pltpu.SemaphoreType.DMA((16,)),
            pltpu.SemaphoreType.DMA((2,)),
        ],
        compiler_params=pltpu.CompilerParams(vmem_limit_bytes=VMEM_LIMIT),
        cost_estimate=pl.CostEstimate(flops=2_000_000, bytes_accessed=8_000_000, transcendentals=0),
    )(odd, drive, arrived, coef)
    from_xe, from_xo = swap(xe, "gx", True), swap(xo, "gx", False)
    inner, ye, yo = call(
        inner_kernel, [posts[1], FACE, FACE], (odd, drive, tiles, coef, edge), 6_000_000
    )
    from_ye, from_yo = swap(ye, "gy", True), swap(yo, "gy", False)
    ce, co = call(corner_kernel, [CORNER, CORNER], (odd, from_xe, from_xo), 200_000)
    from_ce, from_co = swap(ce, "gy", True), swap(co, "gy", False)
    result, own_e, own_o = call(
        middle_kernel,
        [jax.ShapeDtypeStruct((19, 16, 16, 128), F32), SIDE, SIDE],
        (odd, drive, edge, inner, coef, from_xe, from_xo, ye, yo, ce, co),
        12_000_000,
        out_specs=[hbm, VMEM_SPEC, VMEM_SPEC],
        scratch_shapes=[
            pltpu.VMEM((19, EXT, 32, 128), F32),
            pltpu.VMEM((19, 18, 32, 128), F32),
            pltpu.VMEM((16, 19, 16, 128), F32),
            pltpu.SemaphoreType.DMA((16,)),
        ],
    )
    return pl.pallas_call(
        last_kernel,
        out_shape=jax.ShapeDtypeStruct((19, 16, 16, 128), F32),
        in_specs=[SMEM_SPEC] + [VMEM_SPEC] * 7 + [hbm],
        out_specs=hbm,
        input_output_aliases={8: 0},
        scratch_shapes=[
            pltpu.VMEM((SIDE_ROWS, 128), F32),
            pltpu.VMEM((SIDE_ROWS, 128), F32),
            pltpu.VMEM((2, 19, 24, 128), F32),
            pltpu.VMEM((38, 16, 128), F32),
            pltpu.SemaphoreType.DMA,
        ],
        compiler_params=pltpu.CompilerParams(vmem_limit_bytes=VMEM_LIMIT),
        cost_estimate=pl.CostEstimate(flops=2_000_000, bytes_accessed=2_000_000, transcendentals=0),
    )(odd, drive, own_e, own_o, from_ye, from_yo, from_ce, from_co, result)


def solution(mesh):
    return jax.shard_map(
        local,
        mesh=mesh,
        in_specs=(
            P(("gx", "gy"), None, None),
            P(("gx", "gy")),
            P(("gx", "gy"), None, None),
            P(("gx", "gy"), None, None),
            P("gx", "gy", None),
            P(),
        ),
        out_specs=P(None, "gx", "gy", None),
        check_vma=False,
    )
```

```python
from functools import partial

import jax
import jax.numpy as jnp
from jax import lax
from jax.experimental import pallas as pl
from jax.experimental.pallas import tpu as pltpu
from jax.sharding import PartitionSpec as P

VELOCITY = (
    (0, 0, 0),
    (1, 0, 0),
    (-1, 0, 0),
    (0, 1, 0),
    (0, -1, 0),
    (0, 0, 1),
    (0, 0, -1),
    (1, 1, 0),
    (-1, -1, 0),
    (1, -1, 0),
    (-1, 1, 0),
    (1, 0, 1),
    (-1, 0, -1),
    (1, 0, -1),
    (-1, 0, 1),
    (0, 1, 1),
    (0, -1, -1),
    (0, 1, -1),
    (0, -1, 1),
)
WEIGHT = [1.0 / 3.0] + [1.0 / 18.0] * 6 + [1.0 / 36.0] * 12
INVERSE = [3.0] + [18.0] * 6 + [36.0] * 12
DEVICES = 128
HELD = 128
CAP = 2
TILE = 38
PAIR = 2 * TILE + 1
ROWS = 41
APART = 257
EXT = 20
VMEM_LIMIT = 48 * 1024 * 1024
VMEM_MOST = 61 * 1024 * 1024
F32 = jnp.float32


def entries(axis, sign):
    far = [(q, 1) for q in range(19) if VELOCITY[q][axis] == sign]
    near = [(q, 0) for q in range(19) if VELOCITY[q][axis] in (0, sign)]
    return far + near


COUNT = 21
SIDE_ROWS = 432
CORNER_ROWS = 88


def collide(dist, solid, omega, force):
    plus = [None] * 19
    minus = [None] * 19
    for i in range(1, 19, 2):
        plus[i] = dist[i] + dist[i + 1]
        minus[i] = dist[i] - dist[i + 1]
    density = dist[0]
    for i in range(1, 19, 2):
        density = density + plus[i]
    flow = []
    for axis in range(3):
        total = None
        for i in range(1, 19, 2):
            c = VELOCITY[i][axis]
            if c:
                if total is None:
                    total = minus[i]
                else:
                    total = total + minus[i] if c == 1 else total - minus[i]
        flow.append(total + 0.5 * force[axis])
    base = density - 1.5 * (flow[0] * flow[0] + flow[1] * flow[1] + flow[2] * flow[2])
    open_ = 1.0 - solid
    a = open_ * omega
    b = open_ * ((2.0 - omega) / (1.0 - 0.125 * omega))
    keep = 0.5 - 0.5 * a
    turn = 0.5 - solid - 0.5 * b
    post = [None] * 19
    at = a * base
    post[0] = (keep + keep) * dist[0] + at * (1.0 / 3.0)
    drive = [b * flow[axis] + open_ * force[axis] for axis in range(3)]
    for group, w in ((range(1, 7, 2), 1.0 / 18.0), (range(7, 19, 2), 1.0 / 36.0)):
        even_base = at * w
        square = a * (4.5 * w)
        pull = [drive[axis] * (3.0 * w) for axis in range(3)]
        for i in group:
            along = None
            odd = None
            for axis in range(3):
                c = VELOCITY[i][axis]
                if c:
                    if along is None:
                        along, odd = flow[axis], pull[axis]
                    elif c == 1:
                        along, odd = along + flow[axis], odd + pull[axis]
                    else:
                        along, odd = along - flow[axis], odd - pull[axis]
            even = keep * plus[i] + (even_base + square * (along * along))
            odd = turn * minus[i] + odd
            post[i] = even + odd
            post[i + 1] = even - odd
    return post


def shift_z(value, q):
    c = VELOCITY[q][2]
    return value if c == 0 else pltpu.roll(value, c % 128, 1)


def pack_kernel(target_hbm, pdf_hbm, out, target, used, pdf, tiles, labels, sems, small, sent):
    listing = pltpu.make_async_copy(target_hbm, target, small.at[0])
    listing.start()
    quarters = []
    for part in range(4):
        rows = pl.ds(part * 64, 64)
        copy = pltpu.make_async_copy(pdf_hbm.at[:, rows, :], pdf.at[:, rows, 0, :], sems.at[part])
        copy.start()
        quarters.append(copy)
    flat = pdf.reshape(19 * APART, 128)
    rows_ = tiles.reshape(HELD * TILE, 128)
    empty = jnp.full((8, 128), -1.0, F32)
    for block in range(DEVICES // 8):
        labels[8 * block : 8 * block + 8, 0, :] = empty

    def clear(i, _):
        used[i] = 0
        return 0

    lax.fori_loop(0, DEVICES, clear, 0, unroll=8)
    half = lax.broadcasted_iota(jnp.int32, (1, 128), 1) // 64
    listing.wait()

    def put(k, _):
        t = target[k]
        owner = lax.shift_right_logical(t, 7)
        rank = used[owner]
        used[owner] = rank + 1
        near = lax.shift_right_logical(k, 3) * 16 + (k & 7)
        for r in range(2):
            for q in (0, 8, 16):
                n = min(8, 19 - q)
                value = flat[pl.ds(near + r * 8 + q * APART, n, stride=APART), :]
                rows_[pl.ds(k * TILE + r * 19 + q, n), :] = value
        pltpu.make_async_copy(
            tiles.at[pl.ds(k * TILE, TILE)],
            out.at[owner, pl.ds(rank * TILE, TILE)],
            sent,
        ).start()
        line = labels[owner]
        labels[owner] = jnp.where(half == rank, (t & 127).astype(F32), line)
        return 0

    for part in range(4):
        quarters[part].wait()
        lax.fori_loop(part * 32, part * 32 + 32, put, 0, unroll=4)
    named = pltpu.make_async_copy(labels, out.at[:, 2 * TILE], small.at[1])
    named.start()
    pltpu.make_async_copy(tiles, tiles, sent).wait()
    named.wait()


def pack(target, pdf):
    hbm = pl.BlockSpec(memory_space=pltpu.HBM)
    return pl.pallas_call(
        pack_kernel,
        out_shape=jax.ShapeDtypeStruct((DEVICES, PAIR, 1, 128), F32),
        in_specs=[hbm, hbm],
        out_specs=hbm,
        scratch_shapes=[
            pltpu.SMEM((HELD,), jnp.int32),
            pltpu.SMEM((DEVICES,), jnp.int32),
            pltpu.VMEM((19, APART, 1, 128), F32),
            pltpu.VMEM((HELD * TILE, 1, 128), F32),
            pltpu.VMEM((DEVICES, 1, 128), F32),
            pltpu.SemaphoreType.DMA((4,)),
            pltpu.SemaphoreType.DMA((2,)),
            pltpu.SemaphoreType.DMA,
        ],
        compiler_params=pltpu.CompilerParams(vmem_limit_bytes=VMEM_MOST),
        cost_estimate=pl.CostEstimate(flops=0, bytes_accessed=8_000_000, transcendentals=0),
    )(target, pdf)


def pick(flag, even, odd):
    return jnp.where(flag == 0, even, odd)


def plane_step(x, place, at, tiles, coef, post, f):
    for r in range(2):
        dist = []
        for q in range(19):
            value = tiles[pl.ds(place * (8 * ROWS) + r * 19 + q, 8, stride=ROWS), :]
            dist.append(WEIGHT[q] * value + WEIGHT[q])
        solid = coef[0, x, pl.ds(r, 8, stride=2), :]
        omega = coef[1, x, pl.ds(r, 8, stride=2), :]
        after = collide(dist, solid, omega, f)
        for q in range(19):
            post[q, at, pl.ds(8 + r, 8, stride=2), :] = shift_z(after[q], q)


def fetch(source, arrived, tiles, sem, slot, at):
    p = source[0, slot]
    pltpu.make_async_copy(
        arrived.at[lax.shift_right_logical(p, 1), pl.ds((p & 1) * TILE, TILE), 0, :],
        tiles.at[pl.ds(at * ROWS, TILE), :],
        sem,
    ).start()


def arrive(tiles, sem):
    whole = tiles.at[pl.ds(0, 8 * TILE), :]
    pltpu.make_async_copy(whole, whole, sem).wait()


def by_parity(flag, make):
    for even in range(2):

        @pl.when(flag == even)
        def _():
            make(1 - 2 * even)


def x_face(out, sign, edge, coef):
    for i, (q, layer) in enumerate(entries(0, sign)):
        out[i] = edge[q, 3 - layer if sign == 1 else layer, 8:24, :]
    for j in range(2):
        out[19 + j] = coef[j, 15 if sign == 1 else 0]


def y_face(out, sign, planes, coef):
    for i, (q, layer) in enumerate(entries(1, sign)):
        row = 8 + (15 - layer if sign == 1 else layer)
        for x in range(16):
            ref, at = plane_of(x, planes)
            out[i, x : x + 1, :] = ref[q, at, row : row + 1, :]
    row = 15 if sign == 1 else 0
    for j in range(2):
        for x in range(16):
            out[19 + j, x : x + 1, :] = coef[j, x, row : row + 1, :]


def plane_of(x, planes):
    if x < 2:
        return planes[0], x
    if x < 8:
        return planes[1], x - 2
    return (planes[2], x - 8) if x < 14 else (planes[0], x - 12)


def edge_kernel(
    odd, force, arrived, coef, tiles, edge, xe, labels, found, source, sems, small
):
    pull = pltpu.make_async_copy(arrived.at[:, 2 * TILE, 0, :], labels, small.at[0])
    pull.start()
    f = [force[axis : axis + 1, :] for axis in range(3)]
    lane = lax.broadcasted_iota(jnp.int32, (8, 128), 1)
    lane_f = lane.astype(F32)
    sub = lax.broadcasted_iota(jnp.int32, (8, 128), 0)
    low = lane < 64
    total = jnp.zeros((8, 128), jnp.int32)
    pull.wait()
    for group in range(DEVICES // 8):
        line = labels[8 * group : 8 * group + 8, :]
        other = pltpu.roll(line, 64, 1)
        number = (sub + 8 * group) * 2
        total = total + jnp.where(jnp.where(low, line, other) == lane_f, number, 0)
        total = total + jnp.where(jnp.where(low, other, line) == lane_f, number + 1, 0)
    found[...] = jnp.broadcast_to(jnp.sum(total, axis=0, keepdims=True), (8, 128))
    hand = pltpu.make_async_copy(found, source, small.at[1])
    hand.start()
    hand.wait()
    for x in (0, 1, 14, 15):
        for i in range(8):
            fetch(source, arrived, tiles, sems.at[x], 8 * x + i, 8 * x + i)

    def plane(j, _):
        x = jnp.where(j < 2, j, j + 12)
        for i in range(24):
            slot = 16 + 24 * j + i
            fetch(source, arrived, tiles, sems.at[2 + 3 * j + i // 8], slot, slot)
        arrive(tiles, sems.at[x])
        plane_step(x, x, j, tiles, coef, edge, f)
        return 0

    lax.fori_loop(0, 4, plane, 0)
    by_parity(odd[0], lambda sign: x_face(xe, sign, edge, coef))
    for x in range(2, 14):
        arrive(tiles, sems.at[x])


def inner_kernel(start, odd, force, tiles, coef, edge, *refs):
    inner, message = refs[-2:]
    f = [force[axis : axis + 1, :] for axis in range(3)]

    def plane(j, _):
        plane_step(j + start, j + start, j, tiles, coef, inner, f)
        return 0

    lax.fori_loop(0, 6, plane, 0)
    if start == 2:
        by_parity(odd[0], lambda sign: x_face(message, -sign, edge, coef))
    else:
        by_parity(odd[1], lambda sign: y_face(message, sign, (edge, refs[0], inner), coef))


VMEM_SPEC = pl.BlockSpec(memory_space=pltpu.VMEM)
SMEM_SPEC = pl.BlockSpec(memory_space=pltpu.SMEM)
FACE = jax.ShapeDtypeStruct((COUNT, 16, 128), F32)
SIDE = jax.ShapeDtypeStruct((SIDE_ROWS, 128), F32)
CORNER = jax.ShapeDtypeStruct((CORNER_ROWS, 128), F32)


def call(kernel, out_shape, operands, work, scalars=1, **more):
    return pl.pallas_call(
        kernel,
        out_shape=out_shape,
        in_specs=[SMEM_SPEC] * scalars + [VMEM_SPEC] * (len(operands) - scalars),
        compiler_params=pltpu.CompilerParams(vmem_limit_bytes=VMEM_LIMIT),
        cost_estimate=pl.CostEstimate(flops=work, bytes_accessed=work, transcendentals=0),
        **more,
    )(*operands)


def corners(out, turn, odd, xe, xo):
    have = [
        {e: n for n, e in enumerate(entries(0, toward) + [(19, 0), (20, 0)])} for toward in (1, -1)
    ]
    zero = jnp.zeros((1, 128), F32)
    out[CORNER_ROWS - 8 : CORNER_ROWS, :] = jnp.zeros((8, 128), F32)
    for even_x in range(2):
        for even_y in range(2):

            @pl.when((odd[0] == even_x) & (odd[1] == even_y))
            def _():
                halves = (xo, xe) if even_x == 0 else (xe, xo)
                sign = turn * (1 - 2 * even_y)
                for i, (q, layer) in enumerate(entries(1, sign) + [(19, 0), (20, 0)]):
                    row = 15 - layer if sign == 1 else layer
                    for column, (toward, deep) in enumerate(((0, 1), (0, 0), (1, 0), (1, 1))):
                        n = have[toward].get((q, deep))
                        value = zero if n is None else halves[toward][n, row : row + 1, :]
                        out[4 * i + column : 4 * i + column + 1, :] = value


def widen(rows, ends, out):
    for i in range(COUNT):
        at = i * EXT
        out[at : at + 2, :] = ends[4 * i : 4 * i + 2, :]
        out[at + 2 : at + 18, :] = rows[i]
        out[at + 18 : at + 20, :] = ends[4 * i + 2 : 4 * i + 4, :]
    out[COUNT * EXT : SIDE_ROWS, :] = jnp.zeros((SIDE_ROWS - COUNT * EXT, 128), F32)


def second_plane(x, plane, coef, again, at, f):
    for block in range(2):
        dist = []
        for q in range(19):
            cx, cy, _z = VELOCITY[q]
            ref, n = plane(x - cx)
            dist.append(ref[q, n, 8 + 8 * block - cy : 16 + 8 * block - cy, :])
        solid, omega = [coef(j, x, slice(8 * block, 8 * block + 8)) for j in range(2)]
        after = collide(dist, solid, omega, f)
        for q in range(19):
            again[q, at, 8 + 8 * block : 16 + 8 * block, :] = shift_z(after[q], q)


def low_kernel(odd, force, edge, inner_a, inner_b, coef, _before, again, yo):
    f = [force[axis : axis + 1, :] for axis in range(3)]
    planes = (edge, inner_a, inner_b)
    for x in range(1, 8):
        second_plane(
            x, lambda p: plane_of(p, planes), lambda j, p, rows: coef[j, p, rows, :], again, x - 1, f
        )
    by_parity(odd[1], lambda sign: y_face(yo, -sign, planes, coef))


def high_kernel(odd, force, edge, inner_a, inner_b, coef, xe, xo, _before, again, ce):
    corners(ce, 1, odd, xe, xo)
    f = [force[axis : axis + 1, :] for axis in range(3)]
    planes = (edge, inner_a, inner_b)
    for x in range(8, 15):
        second_plane(
            x, lambda p: plane_of(p, planes), lambda j, p, rows: coef[j, p, rows, :], again, x - 8, f
        )


def again_of(x, planes):
    if 1 <= x < 8:
        return planes[0], x - 1
    if 8 <= x < 15:
        return planes[1], x - 8
    return planes[2], {-1: 0, 0: 1, 15: 2, 16: 3}[x]


def output_planes(listed, planes, out, result, sem):
    for n, x in enumerate(listed):
        for q in range(19):
            cx, cy, _z = VELOCITY[q]
            ref, at = again_of(x - cx, planes)
            for block in range(2):
                start = 8 + 8 * block - cy
                value = ref[q, at, start : start + 8, :]
                result[n, q, 8 * block : 8 * block + 8, :] = value * INVERSE[q] - 1.0
        pltpu.make_async_copy(result.at[n], out.at[:, x], sem).start()


def outer_kernel(
    odd, force, edge, inner_a, inner_b, coef, xe, xo, low, high, outer, co, out, halo, fixed, result, sem
):
    corners(co, -1, odd, xe, xo)
    output_planes(range(2, 14), (low, high, None), out, result, sem)

    def copy(sign):
        for toward, (face, side) in enumerate(((xo, 1), (xe, -1)) if sign == 1 else ((xe, 1), (xo, -1))):
            for i, (q, layer) in enumerate(entries(0, side)):
                halo[q, 2 * toward + layer, 8:24, :] = face[i]
            for j in range(2):
                fixed[j, toward] = face[19 + j]

    by_parity(odd[0], copy)
    f = [force[axis : axis + 1, :] for axis in range(3)]
    planes = (edge, inner_a, inner_b)

    def plane(x):
        if x < 0:
            return halo, -1 - x
        return (halo, x - 14) if x > 15 else plane_of(x, planes)

    def coefficient(j, x, rows):
        if x < 0:
            return fixed[j, 0, rows, :]
        return fixed[j, 1, rows, :] if x > 15 else coef[j, x, rows, :]

    for n, x in enumerate((-1, 0, 15, 16)):
        second_plane(x, plane, coefficient, outer, n, f)
    pltpu.make_async_copy(result, result, sem).wait()


def finish_kernel(low, high, outer, ye, yo, ce, co, _before, out, own_e, own_o, result, sem):
    output_planes((0, 1, 14, 15), (low, high, outer), out, result, sem)
    widen(ye, ce, own_e)
    widen(yo, co, own_o)
    pltpu.make_async_copy(result, result, sem).wait()


def last_side(side, sign, own, other, out, rows, patch, sem, f):
    came = {e: n for n, e in enumerate(entries(1, sign))}
    mine = {e: n for n, e in enumerate(entries(1, -sign))}
    for line in range(2):
        for block in range(3):
            start = 1 + 8 * block
            dist = []
            for q in range(19):
                cx, cy, _z = VELOCITY[q]
                if cy == sign:
                    which, n = other, came[(q, 1 - line)]
                elif cy == 0:
                    which, n = (other, came[(q, 0)]) if line == 0 else (own, mine[(q, 0)])
                else:
                    which, n = own, mine[(q, line)]
                at = n * EXT + start - cx
                dist.append(which[at : at + 8, :])
            where = other if line == 0 else own
            fixed = [where[(19 + j) * EXT + start : (19 + j) * EXT + start + 8, :] for j in range(2)]
            after = collide(dist, fixed[0], fixed[1], f)
            for q in range(19):
                if VELOCITY[q][1] == sign or (VELOCITY[q][1] == 0 and line == 1):
                    rows[line, q, 8 * block : 8 * block + 8, :] = shift_z(after[q], q)
    number = 19 * side
    for depth in range(2):
        listed = [q for q in range(19) if VELOCITY[q][1] in ((sign, 0) if depth == 0 else (sign,))]
        y = depth if sign == 1 else 15 - depth
        begin = 0
        for n, q in enumerate(listed):
            cx, cy, _z = VELOCITY[q]
            line = 1 if depth == 1 or cy == 0 else 0
            patch[number + n] = rows[line, q, 1 - cx : 17 - cx, :] * INVERSE[q] - 1.0
            if n + 1 == len(listed) or listed[n + 1] != q + 1:
                count = n + 1 - begin
                pltpu.make_async_copy(
                    patch.at[pl.ds(number + begin, count)],
                    out.at[pl.ds(q + 1 - count, count), :, y, :],
                    sem,
                ).start()
                begin = n + 1
        number += len(listed)


def last_kernel(
    odd, force, mine_e, mine_o, came_e, rows_o, ends_o, _before, out, came_o, rows, patch, sem
):
    widen(rows_o, ends_o, came_o)
    f = [force[axis : axis + 1, :] for axis in range(3)]
    for even in range(2):

        @pl.when(odd[1] == even)
        def _():
            low = (mine_o, came_o) if even == 0 else (mine_e, came_e)
            high = (mine_e, came_e) if even == 0 else (mine_o, came_o)
            last_side(0, 1, *low, out, rows, patch, sem, f)
            last_side(1, -1, *high, out, rows, patch, sem, f)

    pltpu.make_async_copy(patch, patch, sem).wait()


def swap(value, axis, first):
    n = lax.axis_size(axis)
    pairs = [(i, (i + 1) % n if (i % 2 == 0) == first else (i - 1) % n) for i in range(n)]
    return lax.ppermute(value, axis, pairs)


def halves_of(porosity, relaxation):
    lo = lax.axis_index("gy") % 2
    slab = jnp.stack([porosity, relaxation]).reshape(2, 2, 4, 2, 16, 128)
    other = lax.dynamic_index_in_dim(slab, 1 - lo, axis=3, keepdims=False)
    mine = lax.dynamic_index_in_dim(slab, lo, axis=3, keepdims=False)
    return mine, lax.ppermute(other, "gy", [(i, i ^ 1) for i in range(8)])


def pieces_of(mine, came):
    b = lax.axis_index("gy")
    hi, lo = b // 2, b % 2
    both = jnp.stack([jnp.where(lo == 0, mine, came), jnp.where(lo == 0, came, mine)])
    parts = [lax.dynamic_index_in_dim(both, hi, axis=3, keepdims=False)]
    for k in range(1, 4):
        message = lax.dynamic_index_in_dim(both, hi ^ k, axis=3, keepdims=False)
        parts.append(lax.ppermute(message, "gy", [(i, i ^ (2 * k)) for i in range(8)]))
    return parts


def block_of(parts):
    hi = lax.axis_index("gy") // 2
    stacked = jnp.stack(parts)
    ordered = [
        lax.dynamic_index_in_dim(stacked, hi ^ y, axis=0, keepdims=False) for y in range(4)
    ]
    whole = jnp.stack(ordered)
    return whole.transpose(2, 0, 1, 3, 4, 5).reshape(2, 16, 16, 128)


def local(pdf_old, tile_target, porosity, relaxation, solid_mask, force):
    mine, came = halves_of(porosity, relaxation)
    rows = pdf_old.reshape(16, 8, 19, 2, 128).transpose(2, 0, 3, 1, 4).reshape(19, 256, 128)
    packed = pack(tile_target, rows)
    packed, came = lax.optimization_barrier((packed, came))
    arrived = lax.all_to_all(
        packed, ("gx", "gy"), split_axis=0, concat_axis=0, tiled=True
    )
    block = block_of(pieces_of(mine, came))
    solid = block[0] + solid_mask.astype(F32) * (1.0 - block[0])
    coef = jnp.stack([solid, block[1]])
    odd = jnp.stack([lax.axis_index("gx") % 2, lax.axis_index("gy") % 2]).astype(jnp.int32)
    drive = jnp.broadcast_to(jnp.pad(force, (0, 5))[:, None], (8, 128))
    coef, odd, drive = lax.optimization_barrier((coef, odd, drive))
    hbm = pl.BlockSpec(memory_space=pltpu.HBM)
    def planes(n):
        return jax.ShapeDtypeStruct((19, n, 32, 128), F32)

    tiles, edge, xe = pl.pallas_call(
        edge_kernel,
        out_shape=[jax.ShapeDtypeStruct((HELD * ROWS, 128), F32), planes(4), FACE],
        in_specs=[SMEM_SPEC, VMEM_SPEC, hbm, VMEM_SPEC],
        out_specs=[VMEM_SPEC] * 3,
        scratch_shapes=[
            pltpu.VMEM((DEVICES, 128), F32),
            pltpu.VMEM((8, 128), jnp.int32),
            pltpu.SMEM((8, 128), jnp.int32),
            pltpu.SemaphoreType.DMA((16,)),
            pltpu.SemaphoreType.DMA((2,)),
        ],
        compiler_params=pltpu.CompilerParams(vmem_limit_bytes=VMEM_LIMIT),
        cost_estimate=pl.CostEstimate(flops=2_000_000, bytes_accessed=8_000_000, transcendentals=0),
    )(odd, drive, arrived, coef)
    from_xe = swap(xe, "gx", True)
    inner_a, xo = call(
        partial(inner_kernel, 2), [planes(6), FACE], (odd, drive, tiles, coef, edge), 3_000_000
    )
    from_xo = swap(xo, "gx", False)
    inner_b, ye = call(
        partial(inner_kernel, 8), [planes(6), FACE], (odd, drive, tiles, coef, edge, inner_a), 3_000_000
    )
    from_ye = swap(ye, "gy", True)
    low, yo = call(
        low_kernel, [planes(7), FACE], (odd, drive, edge, inner_a, inner_b, coef, from_xe), 4_000_000
    )
    from_yo = swap(yo, "gy", False)
    high, ce = call(
        high_kernel,
        [planes(7), CORNER],
        (odd, drive, edge, inner_a, inner_b, coef, from_xe, from_xo, yo),
        4_000_000,
    )
    from_ce = swap(ce, "gy", True)
    whole = jax.ShapeDtypeStruct((19, 16, 16, 128), F32)
    outer, co, result = call(
        outer_kernel,
        [planes(4), CORNER, whole],
        (odd, drive, edge, inner_a, inner_b, coef, from_xe, from_xo, low, high),
        4_000_000,
        out_specs=[VMEM_SPEC, VMEM_SPEC, hbm],
        scratch_shapes=[
            pltpu.VMEM((19, 4, 32, 128), F32),
            pltpu.VMEM((2, 2, 16, 128), F32),
            pltpu.VMEM((12, 19, 16, 128), F32),
            pltpu.SemaphoreType.DMA,
        ],
    )
    from_co = swap(co, "gy", False)
    result, own_e, own_o = pl.pallas_call(
        finish_kernel,
        out_shape=[whole, SIDE, SIDE],
        in_specs=[VMEM_SPEC] * 7 + [hbm],
        out_specs=[hbm, VMEM_SPEC, VMEM_SPEC],
        input_output_aliases={7: 0},
        scratch_shapes=[pltpu.VMEM((4, 19, 16, 128), F32), pltpu.SemaphoreType.DMA],
        compiler_params=pltpu.CompilerParams(vmem_limit_bytes=VMEM_LIMIT),
        cost_estimate=pl.CostEstimate(flops=2_000_000, bytes_accessed=2_000_000, transcendentals=0),
    )(low, high, outer, ye, yo, ce, co, result)
    came_e = call(widen, SIDE, (from_ye, from_ce), 200_000, scalars=0)
    return pl.pallas_call(
        last_kernel,
        out_shape=jax.ShapeDtypeStruct((19, 16, 16, 128), F32),
        in_specs=[SMEM_SPEC] + [VMEM_SPEC] * 6 + [hbm],
        out_specs=hbm,
        input_output_aliases={7: 0},
        scratch_shapes=[
            pltpu.VMEM((SIDE_ROWS, 128), F32),
            pltpu.VMEM((2, 19, 24, 128), F32),
            pltpu.VMEM((38, 16, 128), F32),
            pltpu.SemaphoreType.DMA,
        ],
        compiler_params=pltpu.CompilerParams(vmem_limit_bytes=VMEM_LIMIT),
        cost_estimate=pl.CostEstimate(flops=2_000_000, bytes_accessed=2_000_000, transcendentals=0),
    )(odd, drive, own_e, own_o, came_e, from_yo, from_co, result)


def solution(mesh):
    return jax.shard_map(
        local,
        mesh=mesh,
        in_specs=(
            P(("gx", "gy"), None, None),
            P(("gx", "gy")),
            P(("gx", "gy"), None, None),
            P(("gx", "gy"), None, None),
            P("gx", "gy", None),
            P(),
        ),
        out_specs=P(None, "gx", "gy", None),
        check_vma=False,
    )
```

```python
import jax
import jax.numpy as jnp
from jax import lax
from jax.experimental import pallas as pl
from jax.experimental.pallas import tpu as pltpu
from jax.sharding import PartitionSpec as P

VELOCITY = (
    (0, 0, 0),
    (1, 0, 0),
    (-1, 0, 0),
    (0, 1, 0),
    (0, -1, 0),
    (0, 0, 1),
    (0, 0, -1),
    (1, 1, 0),
    (-1, -1, 0),
    (1, -1, 0),
    (-1, 1, 0),
    (1, 0, 1),
    (-1, 0, -1),
    (1, 0, -1),
    (-1, 0, 1),
    (0, 1, 1),
    (0, -1, -1),
    (0, 1, -1),
    (0, -1, 1),
)
WEIGHT = [1.0 / 3.0] + [1.0 / 18.0] * 6 + [1.0 / 36.0] * 12
INVERSE = [3.0] + [18.0] * 6 + [36.0] * 12
DEVICES = 128
HELD = 128
CAP = 2
TILE = 38
PAIR = 2 * TILE + 1
ROWS = 41
APART = 257
EXT = 20
VMEM_LIMIT = 48 * 1024 * 1024
VMEM_MOST = 61 * 1024 * 1024
F32 = jnp.float32


def entries(axis, sign):
    far = [(q, 1) for q in range(19) if VELOCITY[q][axis] == sign]
    near = [(q, 0) for q in range(19) if VELOCITY[q][axis] in (0, sign)]
    return far + near


COUNT = 21
SIDE_ROWS = 432
SENT_ROWS = 384


def collide(dist, solid, omega, force):
    plus = [None] * 19
    minus = [None] * 19
    for i in range(1, 19, 2):
        plus[i] = dist[i] + dist[i + 1]
        minus[i] = dist[i] - dist[i + 1]
    density = dist[0]
    for i in range(1, 19, 2):
        density = density + plus[i]
    flow = []
    for axis in range(3):
        total = None
        for i in range(1, 19, 2):
            c = VELOCITY[i][axis]
            if c:
                if total is None:
                    total = minus[i]
                else:
                    total = total + minus[i] if c == 1 else total - minus[i]
        flow.append(total + 0.5 * force[axis])
    base = density - 1.5 * (flow[0] * flow[0] + flow[1] * flow[1] + flow[2] * flow[2])
    open_ = 1.0 - solid
    a = open_ * omega
    b = open_ * ((2.0 - omega) / (1.0 - 0.125 * omega))
    keep = 0.5 - 0.5 * a
    turn = 0.5 - solid - 0.5 * b
    post = [None] * 19
    at = a * base
    post[0] = (keep + keep) * dist[0] + at * (1.0 / 3.0)
    drive = [b * flow[axis] + open_ * force[axis] for axis in range(3)]
    for group, w in ((range(1, 7, 2), 1.0 / 18.0), (range(7, 19, 2), 1.0 / 36.0)):
        even_base = at * w
        square = a * (4.5 * w)
        pull = [drive[axis] * (3.0 * w) for axis in range(3)]
        for i in group:
            along = None
            odd = None
            for axis in range(3):
                c = VELOCITY[i][axis]
                if c:
                    if along is None:
                        along, odd = flow[axis], pull[axis]
                    elif c == 1:
                        along, odd = along + flow[axis], odd + pull[axis]
                    else:
                        along, odd = along - flow[axis], odd - pull[axis]
            even = keep * plus[i] + (even_base + square * (along * along))
            odd = turn * minus[i] + odd
            post[i] = even + odd
            post[i + 1] = even - odd
    return post


def shift_z(value, q):
    c = VELOCITY[q][2]
    return value if c == 0 else pltpu.roll(value, c % 128, 1)


def pack_kernel(target_hbm, pdf_hbm, out, target, used, pdf, tiles, labels, sems, small, sent):
    listing = pltpu.make_async_copy(target_hbm, target, small.at[0])
    listing.start()
    quarters = []
    for part in range(4):
        rows = pl.ds(part * 64, 64)
        copy = pltpu.make_async_copy(pdf_hbm.at[:, rows, :], pdf.at[:, rows, 0, :], sems.at[part])
        copy.start()
        quarters.append(copy)
    flat = pdf.reshape(19 * APART, 128)
    rows_ = tiles.reshape(HELD * TILE, 128)
    empty = jnp.full((8, 128), -1.0, F32)
    for block in range(DEVICES // 8):
        labels[8 * block : 8 * block + 8, 0, :] = empty

    def clear(i, _):
        used[i] = 0
        return 0

    lax.fori_loop(0, DEVICES, clear, 0, unroll=8)
    half = lax.broadcasted_iota(jnp.int32, (1, 128), 1) // 64
    listing.wait()

    def put(k, _):
        t = target[k]
        owner = lax.shift_right_logical(t, 7)
        rank = used[owner]
        used[owner] = rank + 1
        near = lax.shift_right_logical(k, 3) * 16 + (k & 7)
        for r in range(2):
            for q in (0, 8, 16):
                n = min(8, 19 - q)
                value = flat[pl.ds(near + r * 8 + q * APART, n, stride=APART), :]
                rows_[pl.ds(k * TILE + r * 19 + q, n), :] = value
        pltpu.make_async_copy(
            tiles.at[pl.ds(k * TILE, TILE)],
            out.at[owner, pl.ds(rank * TILE, TILE)],
            sent,
        ).start()
        line = labels[owner]
        labels[owner] = jnp.where(half == rank, (t & 127).astype(F32), line)
        return 0

    for part in range(4):
        quarters[part].wait()
        lax.fori_loop(part * 32, part * 32 + 32, put, 0, unroll=4)
    named = pltpu.make_async_copy(labels, out.at[:, 2 * TILE], small.at[1])
    named.start()
    pltpu.make_async_copy(tiles, tiles, sent).wait()
    named.wait()


def pack(target, pdf):
    hbm = pl.BlockSpec(memory_space=pltpu.HBM)
    return pl.pallas_call(
        pack_kernel,
        out_shape=jax.ShapeDtypeStruct((DEVICES, PAIR, 1, 128), F32),
        in_specs=[hbm, hbm],
        out_specs=hbm,
        scratch_shapes=[
            pltpu.SMEM((HELD,), jnp.int32),
            pltpu.SMEM((DEVICES,), jnp.int32),
            pltpu.VMEM((19, APART, 1, 128), F32),
            pltpu.VMEM((HELD * TILE, 1, 128), F32),
            pltpu.VMEM((DEVICES, 1, 128), F32),
            pltpu.SemaphoreType.DMA((4,)),
            pltpu.SemaphoreType.DMA((2,)),
            pltpu.SemaphoreType.DMA,
        ],
        compiler_params=pltpu.CompilerParams(vmem_limit_bytes=VMEM_MOST),
        cost_estimate=pl.CostEstimate(flops=0, bytes_accessed=8_000_000, transcendentals=0),
    )(target, pdf)


def pick(flag, even, odd):
    return jnp.where(flag == 0, even, odd)


def plane_step(x, at, tiles, coef, post, f):
    for r in range(2):
        dist = []
        for q in range(19):
            value = tiles[pl.ds(at * (8 * ROWS) + r * 19 + q, 8, stride=ROWS), :]
            dist.append(WEIGHT[q] * value + WEIGHT[q])
        solid = coef[0, x, pl.ds(r, 8, stride=2), :]
        omega = coef[1, x, pl.ds(r, 8, stride=2), :]
        after = collide(dist, solid, omega, f)
        for q in range(19):
            post[q, at, pl.ds(r, 8, stride=2), :] = shift_z(after[q], q)


def fetch(source, arrived, tiles, sem, slot, at):
    p = source[0, slot]
    pltpu.make_async_copy(
        arrived.at[lax.shift_right_logical(p, 1), pl.ds((p & 1) * TILE, TILE), 0, :],
        tiles.at[pl.ds(at * ROWS, TILE), :],
        sem,
    ).start()


def arrive(tiles, sem):
    whole = tiles.at[pl.ds(0, 8 * TILE), :]
    pltpu.make_async_copy(whole, whole, sem).wait()


def edge_kernel(
    odd, force, arrived, coef, found, edge, xe, xo, tiles, labels, source, sems, small
):
    pull = pltpu.make_async_copy(arrived.at[:, 2 * TILE, 0, :], labels, small.at[0])
    pull.start()
    f = [force[axis : axis + 1, :] for axis in range(3)]
    lane = lax.broadcasted_iota(jnp.int32, (8, 128), 1)
    lane_f = lane.astype(F32)
    sub = lax.broadcasted_iota(jnp.int32, (8, 128), 0)
    low = lane < 64
    total = jnp.zeros((8, 128), jnp.int32)
    pull.wait()
    for group in range(DEVICES // 8):
        line = labels[8 * group : 8 * group + 8, :]
        other = pltpu.roll(line, 64, 1)
        number = (sub + 8 * group) * 2
        total = total + jnp.where(jnp.where(low, line, other) == lane_f, number, 0)
        total = total + jnp.where(jnp.where(low, other, line) == lane_f, number + 1, 0)
    found[...] = jnp.broadcast_to(jnp.sum(total, axis=0, keepdims=True), (8, 128))
    hand = pltpu.make_async_copy(found, source, small.at[1])
    hand.start()
    hand.wait()
    for j, x in enumerate((0, 1, 14, 15)):
        for i in range(8):
            fetch(source, arrived, tiles, sems.at[j], 8 * x + i, 8 * j + i)

    def plane(j, _):
        arrive(tiles, sems.at[j])
        plane_step(jnp.where(j < 2, j, j + 12), j, tiles, coef, edge, f)
        return 0

    lax.fori_loop(0, 4, plane, 0)
    for even in range(2):

        @pl.when(odd[0] == even)
        def _():
            for out, sign in ((xe, 1 - 2 * even), (xo, 2 * even - 1)):
                for i, (q, layer) in enumerate(entries(0, sign)):
                    out[i] = edge[q, 3 - layer if sign == 1 else layer]
                for j in range(2):
                    out[19 + j] = coef[j, 15 if sign == 1 else 0]


def inner_kernel(odd, force, found, arrived, coef, edge, inner, ye, yo, tiles, source, sems, small):
    hand = pltpu.make_async_copy(found, source, small)
    hand.start()
    f = [force[axis : axis + 1, :] for axis in range(3)]
    hand.wait()

    for j in range(12):
        for i in range(8):
            fetch(source, arrived, tiles, sems.at[j], 16 + 8 * j + i, 8 * j + i)

    def plane(j, _):
        arrive(tiles, sems.at[j])
        plane_step(j + 2, j, tiles, coef, inner, f)
        return 0

    lax.fori_loop(0, 12, plane, 0)
    for even in range(2):

        @pl.when(odd[1] == even)
        def _():
            for out, sign in ((ye, 1 - 2 * even), (yo, 2 * even - 1)):
                for i, (q, layer) in enumerate(entries(1, sign)):
                    row = 15 - layer if sign == 1 else layer
                    for x in range(16):
                        if 2 <= x < 14:
                            value = inner[q, x - 2, row : row + 1, :]
                        else:
                            value = edge[q, x if x < 2 else x - 12, row : row + 1, :]
                        out[16 * i + x : 16 * i + x + 1, :] = value
                row = 15 if sign == 1 else 0
                for j in range(2):
                    for x in range(16):
                        at = (19 + j) * 16 + x
                        out[at : at + 1, :] = coef[j, x, row : row + 1, :]


VMEM_SPEC = pl.BlockSpec(memory_space=pltpu.VMEM)
SMEM_SPEC = pl.BlockSpec(memory_space=pltpu.SMEM)
FACE = jax.ShapeDtypeStruct((COUNT, 16, 128), F32)
SIDE = jax.ShapeDtypeStruct((SIDE_ROWS, 128), F32)
SENT = jax.ShapeDtypeStruct((SENT_ROWS, 128), F32)


def call(kernel, out_shape, operands, work, scalars=1, **more):
    return pl.pallas_call(
        kernel,
        out_shape=out_shape,
        in_specs=[SMEM_SPEC] * scalars + [VMEM_SPEC] * (len(operands) - scalars),
        compiler_params=pltpu.CompilerParams(vmem_limit_bytes=VMEM_LIMIT),
        cost_estimate=pl.CostEstimate(flops=work, bytes_accessed=work, transcendentals=0),
        **more,
    )(*operands)


def corners(sign):
    listed = []
    for toward, side in enumerate((1, -1)):
        have = {e: n for n, e in enumerate(entries(0, side) + [(19, 0), (20, 0)])}
        for deep in range(2):
            column = 1 - deep if toward == 0 else 18 + deep
            for i, (q, layer) in enumerate(entries(1, sign) + [(19, 0), (20, 0)]):
                if (q, deep) in have:
                    row = 15 - layer if sign == 1 else layer
                    listed.append((i, column, toward, have[(q, deep)], row))
    return listed


def join_kernel(odd, xe, xo, own_e, own_o, ye, yo):
    for own, out in ((own_e, ye), (own_o, yo)):
        for block in range(COUNT * 2):
            out[8 * block : 8 * block + 8, :] = own[8 * block : 8 * block + 8, :]
        out[SENT_ROWS - 8 : SENT_ROWS, :] = jnp.zeros((8, 128), F32)
    for even_x in range(2):
        for even_y in range(2):

            @pl.when((odd[0] == even_x) & (odd[1] == even_y))
            def _():
                halves = (xo, xe) if even_x == 0 else (xe, xo)
                for out, sign in ((ye, 1 - 2 * even_y), (yo, 2 * even_y - 1)):
                    for n, (_i, _column, toward, there, row) in enumerate(corners(sign)):
                        at = COUNT * 16 + n
                        out[at : at + 1, :] = halves[toward][there, row : row + 1, :]


def widen(message, sign, out):
    for i in range(COUNT):
        out[i * EXT + 2 : i * EXT + 18, :] = message[16 * i : 16 * i + 16, :]
    for n, (i, column, *_rest) in enumerate(corners(sign)):
        at = COUNT * 16 + n
        out[i * EXT + column : i * EXT + column + 1, :] = message[at : at + 1, :]


def middle_kernel(
    odd, force, edge, inner, coef, xe, xo, ye, yo, out, went_dn, went_up, wide, again, result, sems
):
    flag = odd[0]
    for j in range(4):
        for q in range(19):
            wide[q, (j if j < 2 else j + 12) + 2, 8:24, :] = edge[q, j]

    def copy(x, _):
        for q in range(19):
            wide[q, x + 4, 8:24, :] = inner[q, x]
        return 0

    lax.fori_loop(0, 12, copy, 0)
    sides = []
    for toward, sign in ((0, 1), (1, -1)):
        even, odd_ = (xo, xe) if toward == 0 else (xe, xo)
        for i, (q, layer) in enumerate(entries(0, sign)):
            at = 1 - layer if toward == 0 else 18 + layer
            wide[q, at, 8:24, :] = pick(flag, even[i], odd_[i])
        sides.append([pick(flag, even[19 + j], odd_[19 + j]) for j in range(2)])
    f = [force[axis : axis + 1, :] for axis in range(3)]

    def one(x, solids, omegas):
        for block in range(2):
            dist = []
            for q in range(19):
                cx, cy, _z = VELOCITY[q]
                dist.append(wide[q, x + 1 - cx, 8 + 8 * block - cy : 16 + 8 * block - cy, :])
            after = collide(dist, solids[block], omegas[block], f)
            for q in range(19):
                again[q, x, 8 + 8 * block : 16 + 8 * block, :] = shift_z(after[q], q)

    def plane(x, _):
        solids = [coef[0, x - 1, 8 * block : 8 * block + 8, :] for block in range(2)]
        omegas = [coef[1, x - 1, 8 * block : 8 * block + 8, :] for block in range(2)]
        one(x, solids, omegas)
        return 0

    one(0, *[[v[0:8], v[8:16]] for v in sides[0]])
    one(17, *[[v[0:8], v[8:16]] for v in sides[1]])
    lax.fori_loop(1, 17, plane, 0)

    def finish(x, _):
        for q in range(19):
            cx, cy, _z = VELOCITY[q]
            for block in range(2):
                start = 8 + 8 * block - cy
                value = again[q, x + 1 - cx, start : start + 8, :]
                result[x, q, 8 * block : 8 * block + 8, :] = value * INVERSE[q] - 1.0
        pltpu.make_async_copy(result.at[x], out.at[:, x], sems.at[x]).start()
        return 0

    lax.fori_loop(0, 16, finish, 0)
    for even in range(2):

        @pl.when(odd[1] == even)
        def _():
            widen(ye if even == 0 else yo, 1, went_up)
            widen(yo if even == 0 else ye, -1, went_dn)

    for x in range(16):
        pltpu.make_async_copy(result.at[x], out.at[:, x], sems.at[x]).wait()


def last_side(side, sign, own, other, out, rows, patch, sem, f):
    came = {e: n for n, e in enumerate(entries(1, sign))}
    mine = {e: n for n, e in enumerate(entries(1, -sign))}
    for line in range(2):
        for block in range(3):
            start = 1 + 8 * block
            dist = []
            for q in range(19):
                cx, cy, _z = VELOCITY[q]
                if cy == sign:
                    which, n = other, came[(q, 1 - line)]
                elif cy == 0:
                    which, n = (other, came[(q, 0)]) if line == 0 else (own, mine[(q, 0)])
                else:
                    which, n = own, mine[(q, line)]
                at = n * EXT + start - cx
                dist.append(which[at : at + 8, :])
            where = other if line == 0 else own
            fixed = [where[(19 + j) * EXT + start : (19 + j) * EXT + start + 8, :] for j in range(2)]
            after = collide(dist, fixed[0], fixed[1], f)
            for q in range(19):
                if VELOCITY[q][1] == sign or (VELOCITY[q][1] == 0 and line == 1):
                    rows[line, q, 8 * block : 8 * block + 8, :] = shift_z(after[q], q)
    number = 19 * side
    for depth in range(2):
        listed = [q for q in range(19) if VELOCITY[q][1] in ((sign, 0) if depth == 0 else (sign,))]
        y = depth if sign == 1 else 15 - depth
        begin = 0
        for n, q in enumerate(listed):
            cx, cy, _z = VELOCITY[q]
            line = 1 if depth == 1 or cy == 0 else 0
            patch[number + n] = rows[line, q, 1 - cx : 17 - cx, :] * INVERSE[q] - 1.0
            if n + 1 == len(listed) or listed[n + 1] != q + 1:
                count = n + 1 - begin
                pltpu.make_async_copy(
                    patch.at[pl.ds(number + begin, count)],
                    out.at[pl.ds(q + 1 - count, count), :, y, :],
                    sem,
                ).start()
                begin = n + 1
        number += len(listed)


def last_kernel(
    odd, force, went_dn, went_up, came_e, came_o, _before, out, below, above, rows, patch, sem
):
    f = [force[axis : axis + 1, :] for axis in range(3)]
    for even in range(2):

        @pl.when(odd[1] == even)
        def _():
            widen(came_o if even == 0 else came_e, 1, below)
            widen(came_e if even == 0 else came_o, -1, above)

    last_side(0, 1, went_dn, below, out, rows, patch, sem, f)
    last_side(1, -1, went_up, above, out, rows, patch, sem, f)
    pltpu.make_async_copy(patch, patch, sem).wait()


def swap(value, axis, first):
    n = lax.axis_size(axis)
    pairs = [(i, (i + 1) % n if (i % 2 == 0) == first else (i - 1) % n) for i in range(n)]
    return lax.ppermute(value, axis, pairs)


def halves_of(porosity, relaxation):
    lo = lax.axis_index("gy") % 2
    slab = jnp.stack([porosity, relaxation]).reshape(2, 2, 4, 2, 16, 128)
    other = lax.dynamic_index_in_dim(slab, 1 - lo, axis=3, keepdims=False)
    mine = lax.dynamic_index_in_dim(slab, lo, axis=3, keepdims=False)
    return mine, lax.ppermute(other, "gy", [(i, i ^ 1) for i in range(8)])


def pieces_of(mine, came):
    b = lax.axis_index("gy")
    hi, lo = b // 2, b % 2
    both = jnp.stack([jnp.where(lo == 0, mine, came), jnp.where(lo == 0, came, mine)])
    parts = [lax.dynamic_index_in_dim(both, hi, axis=3, keepdims=False)]
    for k in range(1, 4):
        message = lax.dynamic_index_in_dim(both, hi ^ k, axis=3, keepdims=False)
        parts.append(lax.ppermute(message, "gy", [(i, i ^ (2 * k)) for i in range(8)]))
    return parts


def block_of(parts):
    hi = lax.axis_index("gy") // 2
    stacked = jnp.stack(parts)
    ordered = [
        lax.dynamic_index_in_dim(stacked, hi ^ y, axis=0, keepdims=False) for y in range(4)
    ]
    whole = jnp.stack(ordered)
    return whole.transpose(2, 0, 1, 3, 4, 5).reshape(2, 16, 16, 128)


def local(pdf_old, tile_target, porosity, relaxation, solid_mask, force):
    mine, came = halves_of(porosity, relaxation)
    rows = pdf_old.reshape(16, 8, 19, 2, 128).transpose(2, 0, 3, 1, 4).reshape(19, 256, 128)
    packed = pack(tile_target, rows)
    packed, came = lax.optimization_barrier((packed, came))
    arrived = lax.all_to_all(
        packed, ("gx", "gy"), split_axis=0, concat_axis=0, tiled=True
    )
    block = block_of(pieces_of(mine, came))
    solid = block[0] + solid_mask.astype(F32) * (1.0 - block[0])
    coef = jnp.stack([solid, block[1]])
    odd = jnp.stack([lax.axis_index("gx") % 2, lax.axis_index("gy") % 2]).astype(jnp.int32)
    drive = jnp.broadcast_to(jnp.pad(force, (0, 5))[:, None], (8, 128))
    coef, odd, drive = lax.optimization_barrier((coef, odd, drive))
    hbm = pl.BlockSpec(memory_space=pltpu.HBM)
    posts = [jax.ShapeDtypeStruct((19, n, 16, 128), F32) for n in (4, 12)]
    found, edge, xe, xo = pl.pallas_call(
        edge_kernel,
        out_shape=[jax.ShapeDtypeStruct((8, 128), jnp.int32), posts[0], FACE, FACE],
        in_specs=[SMEM_SPEC, VMEM_SPEC, hbm, VMEM_SPEC],
        out_specs=[VMEM_SPEC] * 4,
        scratch_shapes=[
            pltpu.VMEM((32 * ROWS, 128), F32),
            pltpu.VMEM((DEVICES, 128), F32),
            pltpu.SMEM((8, 128), jnp.int32),
            pltpu.SemaphoreType.DMA((4,)),
            pltpu.SemaphoreType.DMA((2,)),
        ],
        compiler_params=pltpu.CompilerParams(vmem_limit_bytes=VMEM_LIMIT),
        cost_estimate=pl.CostEstimate(flops=2_000_000, bytes_accessed=8_000_000, transcendentals=0),
    )(odd, drive, arrived, coef)
    from_xo = swap(xo, "gx", False)
    from_xe = swap(xe, "gx", True)
    inner, own_ye, own_yo = pl.pallas_call(
        inner_kernel,
        out_shape=[posts[1], SENT, SENT],
        in_specs=[SMEM_SPEC, VMEM_SPEC, VMEM_SPEC, hbm, VMEM_SPEC, VMEM_SPEC],
        out_specs=[VMEM_SPEC] * 3,
        scratch_shapes=[
            pltpu.VMEM((96 * ROWS, 128), F32),
            pltpu.SMEM((8, 128), jnp.int32),
            pltpu.SemaphoreType.DMA((12,)),
            pltpu.SemaphoreType.DMA,
        ],
        compiler_params=pltpu.CompilerParams(vmem_limit_bytes=VMEM_LIMIT),
        cost_estimate=pl.CostEstimate(flops=6_000_000, bytes_accessed=8_000_000, transcendentals=0),
    )(odd, drive, found, arrived, coef, edge)
    ye, yo = call(join_kernel, [SENT, SENT], (odd, from_xe, from_xo, own_ye, own_yo), 500_000)
    from_yo = swap(yo, "gy", False)
    from_ye = swap(ye, "gy", True)
    result, went_dn, went_up = call(
        middle_kernel,
        [jax.ShapeDtypeStruct((19, 16, 16, 128), F32), SIDE, SIDE],
        (odd, drive, edge, inner, coef, from_xe, from_xo, ye, yo),
        12_000_000,
        out_specs=[hbm, VMEM_SPEC, VMEM_SPEC],
        scratch_shapes=[
            pltpu.VMEM((19, EXT, 32, 128), F32),
            pltpu.VMEM((19, 18, 32, 128), F32),
            pltpu.VMEM((16, 19, 16, 128), F32),
            pltpu.SemaphoreType.DMA((16,)),
        ],
    )
    return pl.pallas_call(
        last_kernel,
        out_shape=jax.ShapeDtypeStruct((19, 16, 16, 128), F32),
        in_specs=[SMEM_SPEC] + [VMEM_SPEC] * 5 + [hbm],
        out_specs=hbm,
        input_output_aliases={6: 0},
        scratch_shapes=[
            pltpu.VMEM((SIDE_ROWS, 128), F32),
            pltpu.VMEM((SIDE_ROWS, 128), F32),
            pltpu.VMEM((2, 19, 24, 128), F32),
            pltpu.VMEM((38, 16, 128), F32),
            pltpu.SemaphoreType.DMA,
        ],
        compiler_params=pltpu.CompilerParams(vmem_limit_bytes=VMEM_LIMIT),
        cost_estimate=pl.CostEstimate(flops=2_000_000, bytes_accessed=2_000_000, transcendentals=0),
    )(odd, drive, went_dn, went_up, from_ye, from_yo, result)


def solution(mesh):
    return jax.shard_map(
        local,
        mesh=mesh,
        in_specs=(
            P(("gx", "gy"), None, None),
            P(("gx", "gy")),
            P(("gx", "gy"), None, None),
            P(("gx", "gy"), None, None),
            P("gx", "gy", None),
            P(),
        ),
        out_specs=P(None, "gx", "gy", None),
        check_vma=False,
    )
```

```python
import jax
import jax.numpy as jnp
from jax import lax
from jax.experimental import pallas as pl
from jax.experimental.pallas import tpu as pltpu
from jax.sharding import PartitionSpec as P

VELOCITY = (
    (0, 0, 0),
    (1, 0, 0),
    (-1, 0, 0),
    (0, 1, 0),
    (0, -1, 0),
    (0, 0, 1),
    (0, 0, -1),
    (1, 1, 0),
    (-1, -1, 0),
    (1, -1, 0),
    (-1, 1, 0),
    (1, 0, 1),
    (-1, 0, -1),
    (1, 0, -1),
    (-1, 0, 1),
    (0, 1, 1),
    (0, -1, -1),
    (0, 1, -1),
    (0, -1, 1),
)
WEIGHT = [1.0 / 3.0] + [1.0 / 18.0] * 6 + [1.0 / 36.0] * 12
INVERSE = [3.0] + [18.0] * 6 + [36.0] * 12
DEVICES = 128
HELD = 128
CAP = 2
TILE = 38
PAIR = 2 * TILE + 1
ROWS = 41
APART = 257
EXT = 20
VMEM_LIMIT = 48 * 1024 * 1024
VMEM_MOST = 61 * 1024 * 1024
F32 = jnp.float32


def entries(axis, sign):
    far = [(q, 1) for q in range(19) if VELOCITY[q][axis] == sign]
    near = [(q, 0) for q in range(19) if VELOCITY[q][axis] in (0, sign)]
    return far + near


COUNT = 21
SIDE_ROWS = 432
SENT_ROWS = 384


def parity(axis):
    return lax.rem(lax.axis_index(axis), 2)


def collide(dist, solid, omega, force):
    plus = [None] * 19
    minus = [None] * 19
    for i in range(1, 19, 2):
        plus[i] = dist[i] + dist[i + 1]
        minus[i] = dist[i] - dist[i + 1]
    density = dist[0]
    for i in range(1, 19, 2):
        density = density + plus[i]
    flow = []
    for axis in range(3):
        total = None
        for i in range(1, 19, 2):
            c = VELOCITY[i][axis]
            if c:
                if total is None:
                    total = minus[i]
                else:
                    total = total + minus[i] if c == 1 else total - minus[i]
        flow.append(total + 0.5 * force[axis])
    base = density - 1.5 * (flow[0] * flow[0] + flow[1] * flow[1] + flow[2] * flow[2])
    open_ = 1.0 - solid
    a = open_ * omega
    b = open_ * ((2.0 - omega) / (1.0 - 0.125 * omega))
    keep = 0.5 - 0.5 * a
    turn = 0.5 - solid - 0.5 * b
    post = [None] * 19
    at = a * base
    post[0] = (keep + keep) * dist[0] + at * (1.0 / 3.0)
    drive = [b * flow[axis] + open_ * force[axis] for axis in range(3)]
    for group, w in ((range(1, 7, 2), 1.0 / 18.0), (range(7, 19, 2), 1.0 / 36.0)):
        even_base = at * w
        square = a * (4.5 * w)
        pull = [drive[axis] * (3.0 * w) for axis in range(3)]
        for i in group:
            along = None
            odd = None
            for axis in range(3):
                c = VELOCITY[i][axis]
                if c:
                    if along is None:
                        along, odd = flow[axis], pull[axis]
                    elif c == 1:
                        along, odd = along + flow[axis], odd + pull[axis]
                    else:
                        along, odd = along - flow[axis], odd - pull[axis]
            even = keep * plus[i] + (even_base + square * (along * along))
            odd = turn * minus[i] + odd
            post[i] = even + odd
            post[i + 1] = even - odd
    return post


def shift_z(value, q):
    c = VELOCITY[q][2]
    return value if c == 0 else pltpu.roll(value, c % 128, 1)


def pack_kernel(target_hbm, pdf_hbm, out, target, used, pdf, tiles, labels, sems, small, sent):
    listing = pltpu.make_async_copy(target_hbm, target, small.at[0])
    listing.start()
    quarters = []
    for part in range(4):
        rows = pl.ds(part * 64, 64)
        copy = pltpu.make_async_copy(pdf_hbm.at[:, rows, :], pdf.at[:, rows, 0, :], sems.at[part])
        copy.start()
        quarters.append(copy)
    flat = pdf.reshape(19 * APART, 128)
    rows_ = tiles.reshape(HELD * TILE, 128)
    empty = jnp.full((8, 128), -1.0, F32)
    for block in range(DEVICES // 8):
        labels[8 * block : 8 * block + 8, 0, :] = empty

    def clear(i, _):
        used[i] = 0
        return 0

    lax.fori_loop(0, DEVICES, clear, 0, unroll=8)
    half = lax.broadcasted_iota(jnp.int32, (1, 128), 1) // 64
    listing.wait()

    def put(k, _):
        t = target[k]
        owner = lax.shift_right_logical(t, 7)
        rank = used[owner]
        used[owner] = rank + 1
        near = lax.shift_right_logical(k, 3) * 16 + (k & 7)
        for r in range(2):
            for q in (0, 8, 16):
                n = min(8, 19 - q)
                value = flat[pl.ds(near + r * 8 + q * APART, n, stride=APART), :]
                rows_[pl.ds(k * TILE + r * 19 + q, n), :] = value
        pltpu.make_async_copy(
            tiles.at[pl.ds(k * TILE, TILE)],
            out.at[owner, pl.ds(rank * TILE, TILE)],
            sent,
        ).start()
        line = labels[owner]
        labels[owner] = jnp.where(half == rank, (t & 127).astype(F32), line)
        return 0

    for part in range(4):
        quarters[part].wait()
        lax.fori_loop(part * 32, part * 32 + 32, put, 0, unroll=4)
    named = pltpu.make_async_copy(labels, out.at[:, 2 * TILE], small.at[1])
    named.start()
    pltpu.make_async_copy(tiles, tiles, sent).wait()
    named.wait()


def pack(target, pdf):
    hbm = pl.BlockSpec(memory_space=pltpu.HBM)
    return pl.pallas_call(
        pack_kernel,
        out_shape=jax.ShapeDtypeStruct((DEVICES, PAIR, 1, 128), F32),
        in_specs=[hbm, hbm],
        out_specs=hbm,
        scratch_shapes=[
            pltpu.SMEM((HELD,), jnp.int32),
            pltpu.SMEM((DEVICES,), jnp.int32),
            pltpu.VMEM((19, APART, 1, 128), F32),
            pltpu.VMEM((HELD * TILE, 1, 128), F32),
            pltpu.VMEM((DEVICES, 1, 128), F32),
            pltpu.SemaphoreType.DMA((4,)),
            pltpu.SemaphoreType.DMA((2,)),
            pltpu.SemaphoreType.DMA,
        ],
        compiler_params=pltpu.CompilerParams(vmem_limit_bytes=VMEM_MOST),
        cost_estimate=pl.CostEstimate(flops=0, bytes_accessed=8_000_000, transcendentals=0),
    )(target, pdf)


def pick(flag, even, odd):
    return jnp.where(flag == 0, even, odd)


def plane_step(x, at, tiles, coef, post, f):
    for r in range(2):
        dist = []
        for q in range(19):
            value = tiles[pl.ds(at * (8 * ROWS) + r * 19 + q, 8, stride=ROWS), :]
            dist.append(WEIGHT[q] * value + WEIGHT[q])
        solid = coef[0, x, pl.ds(r, 8, stride=2), :]
        omega = coef[1, x, pl.ds(r, 8, stride=2), :]
        after = collide(dist, solid, omega, f)
        for q in range(19):
            post[q, at, pl.ds(r, 8, stride=2), :] = shift_z(after[q], q)


def fetch(source, arrived, tiles, sem, slot, at):
    p = source[0, slot]
    pltpu.make_async_copy(
        arrived.at[lax.shift_right_logical(p, 1), pl.ds((p & 1) * TILE, TILE), 0, :],
        tiles.at[pl.ds(at * ROWS, TILE), :],
        sem,
    ).start()


def arrive(tiles, sem):
    whole = tiles.at[pl.ds(0, 8 * TILE), :]
    pltpu.make_async_copy(whole, whole, sem).wait()


def edge_kernel(
    force, arrived, coef, found, edge, xe, xo, tiles, labels, source, sems, small
):
    pull = pltpu.make_async_copy(arrived.at[:, 2 * TILE, 0, :], labels, small.at[0])
    pull.start()
    f = [force[axis : axis + 1, :] for axis in range(3)]
    lane = lax.broadcasted_iota(jnp.int32, (8, 128), 1)
    lane_f = lane.astype(F32)
    sub = lax.broadcasted_iota(jnp.int32, (8, 128), 0)
    low = lane < 64
    total = jnp.zeros((8, 128), jnp.int32)
    pull.wait()
    for group in range(DEVICES // 8):
        line = labels[8 * group : 8 * group + 8, :]
        other = pltpu.roll(line, 64, 1)
        number = (sub + 8 * group) * 2
        total = total + jnp.where(jnp.where(low, line, other) == lane_f, number, 0)
        total = total + jnp.where(jnp.where(low, other, line) == lane_f, number + 1, 0)
    found[...] = jnp.broadcast_to(jnp.sum(total, axis=0, keepdims=True), (8, 128))
    hand = pltpu.make_async_copy(found, source, small.at[1])
    hand.start()
    hand.wait()
    for j, x in enumerate((0, 1, 14, 15)):
        for i in range(8):
            fetch(source, arrived, tiles, sems.at[j], 8 * x + i, 8 * j + i)

    def plane(j, _):
        arrive(tiles, sems.at[j])
        plane_step(jnp.where(j < 2, j, j + 12), j, tiles, coef, edge, f)
        return 0

    lax.fori_loop(0, 4, plane, 0)
    for even in range(2):

        @pl.when(parity("gx") == even)
        def _():
            for out, sign in ((xe, 1 - 2 * even), (xo, 2 * even - 1)):
                for i, (q, layer) in enumerate(entries(0, sign)):
                    out[i] = edge[q, 3 - layer if sign == 1 else layer]
                for j in range(2):
                    out[19 + j] = coef[j, 15 if sign == 1 else 0]


def inner_kernel(force, found, arrived, coef, edge, inner, ye, yo, tiles, source, sems, small):
    hand = pltpu.make_async_copy(found, source, small)
    hand.start()
    f = [force[axis : axis + 1, :] for axis in range(3)]
    hand.wait()

    for j in range(12):
        for i in range(8):
            fetch(source, arrived, tiles, sems.at[j], 16 + 8 * j + i, 8 * j + i)

    def plane(j, _):
        arrive(tiles, sems.at[j])
        plane_step(j + 2, j, tiles, coef, inner, f)
        return 0

    lax.fori_loop(0, 12, plane, 0)
    for even in range(2):

        @pl.when(parity("gy") == even)
        def _():
            for out, sign in ((ye, 1 - 2 * even), (yo, 2 * even - 1)):
                for i, (q, layer) in enumerate(entries(1, sign)):
                    row = 15 - layer if sign == 1 else layer
                    for x in range(16):
                        if 2 <= x < 14:
                            value = inner[q, x - 2, row : row + 1, :]
                        else:
                            value = edge[q, x if x < 2 else x - 12, row : row + 1, :]
                        out[16 * i + x : 16 * i + x + 1, :] = value
                row = 15 if sign == 1 else 0
                for j in range(2):
                    for x in range(16):
                        at = (19 + j) * 16 + x
                        out[at : at + 1, :] = coef[j, x, row : row + 1, :]


VMEM_SPEC = pl.BlockSpec(memory_space=pltpu.VMEM)
FACE = jax.ShapeDtypeStruct((COUNT, 16, 128), F32)
SIDE = jax.ShapeDtypeStruct((SIDE_ROWS, 128), F32)
SENT = jax.ShapeDtypeStruct((SENT_ROWS, 128), F32)


def call(kernel, out_shape, operands, work, **more):
    return pl.pallas_call(
        kernel,
        out_shape=out_shape,
        in_specs=[VMEM_SPEC] * len(operands),
        compiler_params=pltpu.CompilerParams(vmem_limit_bytes=VMEM_LIMIT),
        cost_estimate=pl.CostEstimate(flops=work, bytes_accessed=work, transcendentals=0),
        **more,
    )(*operands)


def corners(sign):
    listed = []
    for toward, side in enumerate((1, -1)):
        have = {e: n for n, e in enumerate(entries(0, side) + [(19, 0), (20, 0)])}
        for deep in range(2):
            column = 1 - deep if toward == 0 else 18 + deep
            for i, (q, layer) in enumerate(entries(1, sign) + [(19, 0), (20, 0)]):
                if (q, deep) in have:
                    row = 15 - layer if sign == 1 else layer
                    listed.append((i, column, toward, have[(q, deep)], row))
    return listed


def join_kernel(xe, xo, own_e, own_o, ye, yo):
    for own, out in ((own_e, ye), (own_o, yo)):
        for block in range(COUNT * 2):
            out[8 * block : 8 * block + 8, :] = own[8 * block : 8 * block + 8, :]
        out[SENT_ROWS - 8 : SENT_ROWS, :] = jnp.zeros((8, 128), F32)
    for even_x in range(2):
        for even_y in range(2):

            @pl.when((parity("gx") == even_x) & (parity("gy") == even_y))
            def _():
                halves = (xo, xe) if even_x == 0 else (xe, xo)
                for out, sign in ((ye, 1 - 2 * even_y), (yo, 2 * even_y - 1)):
                    for n, (_i, _column, toward, there, row) in enumerate(corners(sign)):
                        at = COUNT * 16 + n
                        out[at : at + 1, :] = halves[toward][there, row : row + 1, :]


def widen(message, sign, out):
    for i in range(COUNT):
        out[i * EXT + 2 : i * EXT + 18, :] = message[16 * i : 16 * i + 16, :]
    for n, (i, column, *_rest) in enumerate(corners(sign)):
        at = COUNT * 16 + n
        out[i * EXT + column : i * EXT + column + 1, :] = message[at : at + 1, :]


def middle_kernel(
    force, edge, inner, coef, xe, xo, ye, yo, out, went_dn, went_up, wide, again, result, sems
):
    flag = parity("gx")
    for j in range(4):
        for q in range(19):
            wide[q, (j if j < 2 else j + 12) + 2, 8:24, :] = edge[q, j]

    def copy(x, _):
        for q in range(19):
            wide[q, x + 4, 8:24, :] = inner[q, x]
        return 0

    lax.fori_loop(0, 12, copy, 0)
    sides = []
    for toward, sign in ((0, 1), (1, -1)):
        even, odd_ = (xo, xe) if toward == 0 else (xe, xo)
        for i, (q, layer) in enumerate(entries(0, sign)):
            at = 1 - layer if toward == 0 else 18 + layer
            wide[q, at, 8:24, :] = pick(flag, even[i], odd_[i])
        sides.append([pick(flag, even[19 + j], odd_[19 + j]) for j in range(2)])
    f = [force[axis : axis + 1, :] for axis in range(3)]

    def one(x, solids, omegas):
        for block in range(2):
            dist = []
            for q in range(19):
                cx, cy, _z = VELOCITY[q]
                dist.append(wide[q, x + 1 - cx, 8 + 8 * block - cy : 16 + 8 * block - cy, :])
            after = collide(dist, solids[block], omegas[block], f)
            for q in range(19):
                again[q, x, 8 + 8 * block : 16 + 8 * block, :] = shift_z(after[q], q)

    def plane(x, _):
        solids = [coef[0, x - 1, 8 * block : 8 * block + 8, :] for block in range(2)]
        omegas = [coef[1, x - 1, 8 * block : 8 * block + 8, :] for block in range(2)]
        one(x, solids, omegas)
        return 0

    one(0, *[[v[0:8], v[8:16]] for v in sides[0]])
    one(17, *[[v[0:8], v[8:16]] for v in sides[1]])
    lax.fori_loop(1, 17, plane, 0)

    def finish(x, _):
        for q in range(19):
            cx, cy, _z = VELOCITY[q]
            for block in range(2):
                start = 8 + 8 * block - cy
                value = again[q, x + 1 - cx, start : start + 8, :]
                result[x, q, 8 * block : 8 * block + 8, :] = value * INVERSE[q] - 1.0
        pltpu.make_async_copy(result.at[x], out.at[:, x], sems.at[x]).start()
        return 0

    lax.fori_loop(0, 16, finish, 0)
    for even in range(2):

        @pl.when(parity("gy") == even)
        def _():
            widen(ye if even == 0 else yo, 1, went_up)
            widen(yo if even == 0 else ye, -1, went_dn)

    for x in range(16):
        pltpu.make_async_copy(result.at[x], out.at[:, x], sems.at[x]).wait()


def last_side(side, sign, own, other, out, rows, patch, sem, f):
    came = {e: n for n, e in enumerate(entries(1, sign))}
    mine = {e: n for n, e in enumerate(entries(1, -sign))}
    for line in range(2):
        for block in range(3):
            start = 1 + 8 * block
            dist = []
            for q in range(19):
                cx, cy, _z = VELOCITY[q]
                if cy == sign:
                    which, n = other, came[(q, 1 - line)]
                elif cy == 0:
                    which, n = (other, came[(q, 0)]) if line == 0 else (own, mine[(q, 0)])
                else:
                    which, n = own, mine[(q, line)]
                at = n * EXT + start - cx
                dist.append(which[at : at + 8, :])
            where = other if line == 0 else own
            fixed = [where[(19 + j) * EXT + start : (19 + j) * EXT + start + 8, :] for j in range(2)]
            after = collide(dist, fixed[0], fixed[1], f)
            for q in range(19):
                if VELOCITY[q][1] == sign or (VELOCITY[q][1] == 0 and line == 1):
                    rows[line, q, 8 * block : 8 * block + 8, :] = shift_z(after[q], q)
    number = 19 * side
    for depth in range(2):
        listed = [q for q in range(19) if VELOCITY[q][1] in ((sign, 0) if depth == 0 else (sign,))]
        y = depth if sign == 1 else 15 - depth
        begin = 0
        for n, q in enumerate(listed):
            cx, cy, _z = VELOCITY[q]
            line = 1 if depth == 1 or cy == 0 else 0
            patch[number + n] = rows[line, q, 1 - cx : 17 - cx, :] * INVERSE[q] - 1.0
            if n + 1 == len(listed) or listed[n + 1] != q + 1:
                count = n + 1 - begin
                pltpu.make_async_copy(
                    patch.at[pl.ds(number + begin, count)],
                    out.at[pl.ds(q + 1 - count, count), :, y, :],
                    sem,
                ).start()
                begin = n + 1
        number += len(listed)


def last_kernel(
    force, went_dn, went_up, came_e, came_o, _before, out, below, above, rows, patch, sem
):
    f = [force[axis : axis + 1, :] for axis in range(3)]
    for even in range(2):

        @pl.when(parity("gy") == even)
        def _():
            widen(came_o if even == 0 else came_e, 1, below)
            widen(came_e if even == 0 else came_o, -1, above)

    last_side(0, 1, went_dn, below, out, rows, patch, sem, f)
    last_side(1, -1, went_up, above, out, rows, patch, sem, f)
    pltpu.make_async_copy(patch, patch, sem).wait()


def swap(value, axis, first):
    n = lax.axis_size(axis)
    pairs = [(i, (i + 1) % n if (i % 2 == 0) == first else (i - 1) % n) for i in range(n)]
    return lax.ppermute(value, axis, pairs)


def halves_of(porosity, relaxation):
    hi = lax.axis_index("gy") // 4
    slab = jnp.stack([porosity, relaxation]).reshape(2, 2, 8, 16, 128)
    other = lax.dynamic_slice_in_dim(slab, (1 - hi) * 4, 4, axis=2)
    mine = lax.dynamic_slice_in_dim(slab, hi * 4, 4, axis=2)
    return mine, lax.ppermute(other, "gy", [(i, i ^ 4) for i in range(8)])


def pieces_of(mine, came):
    b = lax.axis_index("gy")
    hi, lo = b // 4, b % 4
    both = jnp.stack([jnp.where(hi == 0, mine, came), jnp.where(hi == 0, came, mine)])
    parts = [lax.dynamic_index_in_dim(both, lo, axis=3, keepdims=False)]
    for k in range(1, 4):
        message = lax.dynamic_index_in_dim(both, lo ^ k, axis=3, keepdims=False)
        parts.append(lax.ppermute(message, "gy", [(i, i ^ k) for i in range(8)]))
    return parts


def block_of(parts):
    lo = lax.axis_index("gy") % 4
    stacked = jnp.stack(parts)
    ordered = [
        lax.dynamic_index_in_dim(stacked, lo ^ y, axis=0, keepdims=False) for y in range(4)
    ]
    whole = jnp.stack(ordered)
    return whole.transpose(2, 1, 0, 3, 4, 5).reshape(2, 16, 16, 128)


def local(pdf_old, tile_target, porosity, relaxation, solid_mask, force):
    mine, came = halves_of(porosity, relaxation)
    rows = pdf_old.reshape(16, 8, 19, 2, 128).transpose(2, 0, 3, 1, 4).reshape(19, 256, 128)
    packed = pack(tile_target, rows)
    packed, came = lax.optimization_barrier((packed, came))
    arrived = lax.all_to_all(
        packed, ("gx", "gy"), split_axis=0, concat_axis=0, tiled=True
    )
    block = block_of(pieces_of(mine, came))
    solid = block[0] + solid_mask.astype(F32) * (1.0 - block[0])
    coef = jnp.stack([solid, block[1]])
    drive = jnp.broadcast_to(jnp.pad(force, (0, 5))[:, None], (8, 128))
    coef, drive = lax.optimization_barrier((coef, drive))
    hbm = pl.BlockSpec(memory_space=pltpu.HBM)
    posts = [jax.ShapeDtypeStruct((19, n, 16, 128), F32) for n in (4, 12)]
    found, edge, xe, xo = pl.pallas_call(
        edge_kernel,
        out_shape=[jax.ShapeDtypeStruct((8, 128), jnp.int32), posts[0], FACE, FACE],
        in_specs=[VMEM_SPEC, hbm, VMEM_SPEC],
        out_specs=[VMEM_SPEC] * 4,
        scratch_shapes=[
            pltpu.VMEM((32 * ROWS, 128), F32),
            pltpu.VMEM((DEVICES, 128), F32),
            pltpu.SMEM((8, 128), jnp.int32),
            pltpu.SemaphoreType.DMA((4,)),
            pltpu.SemaphoreType.DMA((2,)),
        ],
        compiler_params=pltpu.CompilerParams(vmem_limit_bytes=VMEM_LIMIT),
        cost_estimate=pl.CostEstimate(flops=2_000_000, bytes_accessed=8_000_000, transcendentals=0),
    )(drive, arrived, coef)
    from_xo = swap(xo, "gx", False)
    from_xe = swap(xe, "gx", True)
    inner, own_ye, own_yo = pl.pallas_call(
        inner_kernel,
        out_shape=[posts[1], SENT, SENT],
        in_specs=[VMEM_SPEC, VMEM_SPEC, hbm, VMEM_SPEC, VMEM_SPEC],
        out_specs=[VMEM_SPEC] * 3,
        scratch_shapes=[
            pltpu.VMEM((96 * ROWS, 128), F32),
            pltpu.SMEM((8, 128), jnp.int32),
            pltpu.SemaphoreType.DMA((12,)),
            pltpu.SemaphoreType.DMA,
        ],
        compiler_params=pltpu.CompilerParams(vmem_limit_bytes=VMEM_LIMIT),
        cost_estimate=pl.CostEstimate(flops=6_000_000, bytes_accessed=8_000_000, transcendentals=0),
    )(drive, found, arrived, coef, edge)
    ye, yo = call(join_kernel, [SENT, SENT], (from_xe, from_xo, own_ye, own_yo), 500_000)
    from_yo = swap(yo, "gy", False)
    from_ye = swap(ye, "gy", True)
    result, went_dn, went_up = call(
        middle_kernel,
        [jax.ShapeDtypeStruct((19, 16, 16, 128), F32), SIDE, SIDE],
        (drive, edge, inner, coef, from_xe, from_xo, ye, yo),
        12_000_000,
        out_specs=[hbm, VMEM_SPEC, VMEM_SPEC],
        scratch_shapes=[
            pltpu.VMEM((19, EXT, 32, 128), F32),
            pltpu.VMEM((19, 18, 32, 128), F32),
            pltpu.VMEM((16, 19, 16, 128), F32),
            pltpu.SemaphoreType.DMA((16,)),
        ],
    )
    return pl.pallas_call(
        last_kernel,
        out_shape=jax.ShapeDtypeStruct((19, 16, 16, 128), F32),
        in_specs=[VMEM_SPEC] * 5 + [hbm],
        out_specs=hbm,
        input_output_aliases={5: 0},
        scratch_shapes=[
            pltpu.VMEM((SIDE_ROWS, 128), F32),
            pltpu.VMEM((SIDE_ROWS, 128), F32),
            pltpu.VMEM((2, 19, 24, 128), F32),
            pltpu.VMEM((38, 16, 128), F32),
            pltpu.SemaphoreType.DMA,
        ],
        compiler_params=pltpu.CompilerParams(vmem_limit_bytes=VMEM_LIMIT),
        cost_estimate=pl.CostEstimate(flops=2_000_000, bytes_accessed=2_000_000, transcendentals=0),
    )(drive, went_dn, went_up, from_ye, from_yo, result)


def solution(mesh):
    return jax.shard_map(
        local,
        mesh=mesh,
        in_specs=(
            P(("gx", "gy"), None, None),
            P(("gx", "gy")),
            P(("gx", "gy"), None, None),
            P(("gx", "gy"), None, None),
            P("gx", "gy", None),
            P(),
        ),
        out_specs=P(None, "gx", "gy", None),
        check_vma=False,
    )
```

```python
import jax
import jax.numpy as jnp
from jax import lax
from jax.experimental import pallas as pl
from jax.experimental.pallas import tpu as pltpu
from jax.sharding import PartitionSpec as P

VELOCITY = (
    (0, 0, 0),
    (1, 0, 0),
    (-1, 0, 0),
    (0, 1, 0),
    (0, -1, 0),
    (0, 0, 1),
    (0, 0, -1),
    (1, 1, 0),
    (-1, -1, 0),
    (1, -1, 0),
    (-1, 1, 0),
    (1, 0, 1),
    (-1, 0, -1),
    (1, 0, -1),
    (-1, 0, 1),
    (0, 1, 1),
    (0, -1, -1),
    (0, 1, -1),
    (0, -1, 1),
)
WEIGHT = [1.0 / 3.0] + [1.0 / 18.0] * 6 + [1.0 / 36.0] * 12
INVERSE = [3.0] + [18.0] * 6 + [36.0] * 12
DEVICES = 128
HELD = 128
CAP = 2
TILE = 38
PAIR = 2 * TILE + 1
ROWS = 41
APART = 257
EXT = 20
VMEM_LIMIT = 48 * 1024 * 1024
VMEM_MOST = 61 * 1024 * 1024
F32 = jnp.float32


def entries(axis, sign):
    far = [(q, 1) for q in range(19) if VELOCITY[q][axis] == sign]
    near = [(q, 0) for q in range(19) if VELOCITY[q][axis] in (0, sign)]
    return far + near


COUNT = 21
SIDE_ROWS = 432
SENT_ROWS = 384


def parity(axis):
    return lax.rem(lax.axis_index(axis), 2)


def collide(dist, solid, omega, force):
    plus = [None] * 19
    minus = [None] * 19
    for i in range(1, 19, 2):
        plus[i] = dist[i] + dist[i + 1]
        minus[i] = dist[i] - dist[i + 1]
    density = dist[0]
    for i in range(1, 19, 2):
        density = density + plus[i]
    flow = []
    for axis in range(3):
        total = None
        for i in range(1, 19, 2):
            c = VELOCITY[i][axis]
            if c:
                if total is None:
                    total = minus[i]
                else:
                    total = total + minus[i] if c == 1 else total - minus[i]
        flow.append(total + 0.5 * force[axis])
    base = density - 1.5 * (flow[0] * flow[0] + flow[1] * flow[1] + flow[2] * flow[2])
    open_ = 1.0 - solid
    a = open_ * omega
    b = open_ * ((2.0 - omega) / (1.0 - 0.125 * omega))
    keep = 0.5 - 0.5 * a
    turn = 0.5 - solid - 0.5 * b
    post = [None] * 19
    at = a * base
    post[0] = (keep + keep) * dist[0] + at * (1.0 / 3.0)
    drive = [b * flow[axis] + open_ * force[axis] for axis in range(3)]
    for group, w in ((range(1, 7, 2), 1.0 / 18.0), (range(7, 19, 2), 1.0 / 36.0)):
        even_base = at * w
        square = a * (4.5 * w)
        pull = [drive[axis] * (3.0 * w) for axis in range(3)]
        for i in group:
            along = None
            odd = None
            for axis in range(3):
                c = VELOCITY[i][axis]
                if c:
                    if along is None:
                        along, odd = flow[axis], pull[axis]
                    elif c == 1:
                        along, odd = along + flow[axis], odd + pull[axis]
                    else:
                        along, odd = along - flow[axis], odd - pull[axis]
            even = keep * plus[i] + (even_base + square * (along * along))
            odd = turn * minus[i] + odd
            post[i] = even + odd
            post[i + 1] = even - odd
    return post


def shift_z(value, q):
    c = VELOCITY[q][2]
    return value if c == 0 else pltpu.roll(value, c % 128, 1)


def pack_kernel(target_hbm, pdf_hbm, out, target, used, pdf, tiles, labels, sems, small, sent):
    listing = pltpu.make_async_copy(target_hbm, target, small.at[0])
    listing.start()
    quarters = []
    for part in range(4):
        rows = pl.ds(part * 64, 64)
        copy = pltpu.make_async_copy(pdf_hbm.at[:, rows, :], pdf.at[:, rows, 0, :], sems.at[part])
        copy.start()
        quarters.append(copy)
    flat = pdf.reshape(19 * APART, 128)
    rows_ = tiles.reshape(HELD * TILE, 128)
    empty = jnp.full((8, 128), -1.0, F32)
    for block in range(DEVICES // 8):
        labels[8 * block : 8 * block + 8, 0, :] = empty

    def clear(i, _):
        used[i] = 0
        return 0

    lax.fori_loop(0, DEVICES, clear, 0, unroll=8)
    half = lax.broadcasted_iota(jnp.int32, (1, 128), 1) // 64
    listing.wait()

    def put(k, _):
        t = target[k]
        owner = lax.shift_right_logical(t, 7)
        rank = used[owner]
        used[owner] = rank + 1
        near = lax.shift_right_logical(k, 3) * 16 + (k & 7)
        for r in range(2):
            for q in (0, 8, 16):
                n = min(8, 19 - q)
                value = flat[pl.ds(near + r * 8 + q * APART, n, stride=APART), :]
                rows_[pl.ds(k * TILE + r * 19 + q, n), :] = value
        pltpu.make_async_copy(
            tiles.at[pl.ds(k * TILE, TILE)],
            out.at[owner, pl.ds(rank * TILE, TILE)],
            sent,
        ).start()
        line = labels[owner]
        labels[owner] = jnp.where(half == rank, (t & 127).astype(F32), line)
        return 0

    for part in range(4):
        quarters[part].wait()
        lax.fori_loop(part * 32, part * 32 + 32, put, 0, unroll=4)
    named = pltpu.make_async_copy(labels, out.at[:, 2 * TILE], small.at[1])
    named.start()
    pltpu.make_async_copy(tiles, tiles, sent).wait()
    named.wait()


def pack(target, pdf):
    hbm = pl.BlockSpec(memory_space=pltpu.HBM)
    return pl.pallas_call(
        pack_kernel,
        out_shape=jax.ShapeDtypeStruct((DEVICES, PAIR, 1, 128), F32),
        in_specs=[hbm, hbm],
        out_specs=hbm,
        scratch_shapes=[
            pltpu.SMEM((HELD,), jnp.int32),
            pltpu.SMEM((DEVICES,), jnp.int32),
            pltpu.VMEM((19, APART, 1, 128), F32),
            pltpu.VMEM((HELD * TILE, 1, 128), F32),
            pltpu.VMEM((DEVICES, 1, 128), F32),
            pltpu.SemaphoreType.DMA((4,)),
            pltpu.SemaphoreType.DMA((2,)),
            pltpu.SemaphoreType.DMA,
        ],
        compiler_params=pltpu.CompilerParams(vmem_limit_bytes=VMEM_MOST),
        cost_estimate=pl.CostEstimate(flops=0, bytes_accessed=8_000_000, transcendentals=0),
    )(target, pdf)


def pick(flag, even, odd):
    return jnp.where(flag == 0, even, odd)


def plane_step(x, at, tiles, coef, post, f):
    for r in range(2):
        dist = []
        for q in range(19):
            value = tiles[pl.ds(at * (8 * ROWS) + r * 19 + q, 8, stride=ROWS), :]
            dist.append(WEIGHT[q] * value + WEIGHT[q])
        solid = coef[0, x, pl.ds(r, 8, stride=2), :]
        omega = coef[1, x, pl.ds(r, 8, stride=2), :]
        after = collide(dist, solid, omega, f)
        for q in range(19):
            post[q, at, pl.ds(r, 8, stride=2), :] = shift_z(after[q], q)


def fetch(p, arrived, tiles, sem, at):
    pltpu.make_async_copy(
        arrived.at[lax.shift_right_logical(p, 1), pl.ds((p & 1) * TILE, TILE), 0, :],
        tiles.at[pl.ds(at * ROWS, TILE), :],
        sem,
    ).start()


def arrive(tiles, sem):
    whole = tiles.at[pl.ds(0, 8 * TILE), :]
    pltpu.make_async_copy(whole, whole, sem).wait()


def edge_kernel(
    force, arrived, coef, found, edge, xe, xo, tiles, labels, sems, small
):
    pull = pltpu.make_async_copy(arrived.at[:, 2 * TILE, 0, :], labels, small)
    pull.start()
    f = [force[axis : axis + 1, :] for axis in range(3)]
    lane = lax.broadcasted_iota(jnp.int32, (8, 128), 1)
    lane_f = lane.astype(F32)
    sub = lax.broadcasted_iota(jnp.int32, (8, 128), 0)
    low = lane < 64
    total = jnp.zeros((8, 128), jnp.int32)
    pull.wait()
    for group in range(DEVICES // 8):
        line = labels[8 * group : 8 * group + 8, :]
        other = pltpu.roll(line, 64, 1)
        number = (sub + 8 * group) * 2
        total = total + jnp.where(jnp.where(low, line, other) == lane_f, number, 0)
        total = total + jnp.where(jnp.where(low, other, line) == lane_f, number + 1, 0)
    numbers = jnp.sum(total, axis=0, keepdims=True)
    found[...] = jnp.broadcast_to(numbers, (8, 128))
    for j, x in enumerate((0, 1, 14, 15)):
        for i in range(8):
            fetch(numbers[0, 8 * x + i], arrived, tiles, sems.at[j], 8 * j + i)

    def plane(j, _):
        arrive(tiles, sems.at[j])
        plane_step(jnp.where(j < 2, j, j + 12), j, tiles, coef, edge, f)
        return 0

    lax.fori_loop(0, 4, plane, 0)
    for even in range(2):

        @pl.when(parity("gx") == even)
        def _():
            for out, sign in ((xe, 1 - 2 * even), (xo, 2 * even - 1)):
                for i, (q, layer) in enumerate(entries(0, sign)):
                    out[i] = edge[q, 3 - layer if sign == 1 else layer]
                for j in range(2):
                    out[19 + j] = coef[j, 15 if sign == 1 else 0]


def inner_kernel(force, found, arrived, coef, edge, inner, ye, yo, tiles, source, sems, small):
    hand = pltpu.make_async_copy(found, source, small)
    hand.start()
    f = [force[axis : axis + 1, :] for axis in range(3)]
    hand.wait()

    for j in range(12):
        for i in range(8):
            fetch(source[0, 16 + 8 * j + i], arrived, tiles, sems.at[j], 8 * j + i)

    def plane(j, _):
        arrive(tiles, sems.at[j])
        plane_step(j + 2, j, tiles, coef, inner, f)
        return 0

    lax.fori_loop(0, 12, plane, 0)
    for even in range(2):

        @pl.when(parity("gy") == even)
        def _():
            for out, sign in ((ye, 1 - 2 * even), (yo, 2 * even - 1)):
                for i, (q, layer) in enumerate(entries(1, sign)):
                    row = 15 - layer if sign == 1 else layer
                    for x in range(16):
                        if 2 <= x < 14:
                            value = inner[q, x - 2, row : row + 1, :]
                        else:
                            value = edge[q, x if x < 2 else x - 12, row : row + 1, :]
                        out[16 * i + x : 16 * i + x + 1, :] = value
                row = 15 if sign == 1 else 0
                for j in range(2):
                    for x in range(16):
                        at = (19 + j) * 16 + x
                        out[at : at + 1, :] = coef[j, x, row : row + 1, :]


VMEM_SPEC = pl.BlockSpec(memory_space=pltpu.VMEM)
FACE = jax.ShapeDtypeStruct((COUNT, 16, 128), F32)
SIDE = jax.ShapeDtypeStruct((SIDE_ROWS, 128), F32)
SENT = jax.ShapeDtypeStruct((SENT_ROWS, 128), F32)


def call(kernel, out_shape, operands, work, **more):
    return pl.pallas_call(
        kernel,
        out_shape=out_shape,
        in_specs=[VMEM_SPEC] * len(operands),
        compiler_params=pltpu.CompilerParams(vmem_limit_bytes=VMEM_LIMIT),
        cost_estimate=pl.CostEstimate(flops=work, bytes_accessed=work, transcendentals=0),
        **more,
    )(*operands)


def corners(sign):
    listed = []
    for toward, side in enumerate((1, -1)):
        have = {e: n for n, e in enumerate(entries(0, side) + [(19, 0), (20, 0)])}
        for deep in range(2):
            column = 1 - deep if toward == 0 else 18 + deep
            for i, (q, layer) in enumerate(entries(1, sign) + [(19, 0), (20, 0)]):
                if (q, deep) in have:
                    row = 15 - layer if sign == 1 else layer
                    listed.append((i, column, toward, have[(q, deep)], row))
    return listed


def join_kernel(xe, xo, own_e, own_o, ye, yo):
    for own, out in ((own_e, ye), (own_o, yo)):
        for block in range(COUNT * 2):
            out[8 * block : 8 * block + 8, :] = own[8 * block : 8 * block + 8, :]
        out[SENT_ROWS - 8 : SENT_ROWS, :] = jnp.zeros((8, 128), F32)
    for even_x in range(2):
        for even_y in range(2):

            @pl.when((parity("gx") == even_x) & (parity("gy") == even_y))
            def _():
                halves = (xo, xe) if even_x == 0 else (xe, xo)
                for out, sign in ((ye, 1 - 2 * even_y), (yo, 2 * even_y - 1)):
                    for n, (_i, _column, toward, there, row) in enumerate(corners(sign)):
                        at = COUNT * 16 + n
                        out[at : at + 1, :] = halves[toward][there, row : row + 1, :]


def widen(message, sign, out):
    for i in range(COUNT):
        out[i * EXT + 2 : i * EXT + 18, :] = message[16 * i : 16 * i + 16, :]
    for n, (i, column, *_rest) in enumerate(corners(sign)):
        at = COUNT * 16 + n
        out[i * EXT + column : i * EXT + column + 1, :] = message[at : at + 1, :]


def middle_kernel(
    force, edge, inner, coef, xe, xo, ye, yo, out, went_dn, went_up, wide, again, result, sems
):
    flag = parity("gx")
    for j in range(4):
        for q in range(19):
            wide[q, (j if j < 2 else j + 12) + 2, 8:24, :] = edge[q, j]

    def copy(x, _):
        for q in range(19):
            wide[q, x + 4, 8:24, :] = inner[q, x]
        return 0

    lax.fori_loop(0, 12, copy, 0)
    sides = []
    for toward, sign in ((0, 1), (1, -1)):
        even, odd_ = (xo, xe) if toward == 0 else (xe, xo)
        for i, (q, layer) in enumerate(entries(0, sign)):
            at = 1 - layer if toward == 0 else 18 + layer
            wide[q, at, 8:24, :] = pick(flag, even[i], odd_[i])
        sides.append([pick(flag, even[19 + j], odd_[19 + j]) for j in range(2)])
    f = [force[axis : axis + 1, :] for axis in range(3)]

    def one(x, solids, omegas):
        for block in range(2):
            dist = []
            for q in range(19):
                cx, cy, _z = VELOCITY[q]
                dist.append(wide[q, x + 1 - cx, 8 + 8 * block - cy : 16 + 8 * block - cy, :])
            after = collide(dist, solids[block], omegas[block], f)
            for q in range(19):
                again[q, x, 8 + 8 * block : 16 + 8 * block, :] = shift_z(after[q], q)

    def plane(x, _):
        solids = [coef[0, x - 1, 8 * block : 8 * block + 8, :] for block in range(2)]
        omegas = [coef[1, x - 1, 8 * block : 8 * block + 8, :] for block in range(2)]
        one(x, solids, omegas)
        return 0

    one(0, *[[v[0:8], v[8:16]] for v in sides[0]])
    one(17, *[[v[0:8], v[8:16]] for v in sides[1]])
    lax.fori_loop(1, 17, plane, 0)

    def finish(x, _):
        for q in range(19):
            cx, cy, _z = VELOCITY[q]
            for block in range(2):
                start = 8 + 8 * block - cy
                value = again[q, x + 1 - cx, start : start + 8, :]
                result[x, q, 8 * block : 8 * block + 8, :] = value * INVERSE[q] - 1.0
        pltpu.make_async_copy(result.at[x], out.at[:, x], sems.at[x]).start()
        return 0

    lax.fori_loop(0, 16, finish, 0)
    for even in range(2):

        @pl.when(parity("gy") == even)
        def _():
            widen(ye if even == 0 else yo, 1, went_up)
            widen(yo if even == 0 else ye, -1, went_dn)

    for x in range(16):
        pltpu.make_async_copy(result.at[x], out.at[:, x], sems.at[x]).wait()


def last_side(side, sign, own, other, out, rows, patch, sem, f):
    came = {e: n for n, e in enumerate(entries(1, sign))}
    mine = {e: n for n, e in enumerate(entries(1, -sign))}
    for line in range(2):
        for block in range(3):
            start = 1 + 8 * block
            dist = []
            for q in range(19):
                cx, cy, _z = VELOCITY[q]
                if cy == sign:
                    which, n = other, came[(q, 1 - line)]
                elif cy == 0:
                    which, n = (other, came[(q, 0)]) if line == 0 else (own, mine[(q, 0)])
                else:
                    which, n = own, mine[(q, line)]
                at = n * EXT + start - cx
                dist.append(which[at : at + 8, :])
            where = other if line == 0 else own
            fixed = [where[(19 + j) * EXT + start : (19 + j) * EXT + start + 8, :] for j in range(2)]
            after = collide(dist, fixed[0], fixed[1], f)
            for q in range(19):
                if VELOCITY[q][1] == sign or (VELOCITY[q][1] == 0 and line == 1):
                    rows[line, q, 8 * block : 8 * block + 8, :] = shift_z(after[q], q)
    number = 19 * side
    for depth in range(2):
        listed = [q for q in range(19) if VELOCITY[q][1] in ((sign, 0) if depth == 0 else (sign,))]
        y = depth if sign == 1 else 15 - depth
        begin = 0
        for n, q in enumerate(listed):
            cx, cy, _z = VELOCITY[q]
            line = 1 if depth == 1 or cy == 0 else 0
            patch[number + n] = rows[line, q, 1 - cx : 17 - cx, :] * INVERSE[q] - 1.0
            if n + 1 == len(listed) or listed[n + 1] != q + 1:
                count = n + 1 - begin
                pltpu.make_async_copy(
                    patch.at[pl.ds(number + begin, count)],
                    out.at[pl.ds(q + 1 - count, count), :, y, :],
                    sem,
                ).start()
                begin = n + 1
        number += len(listed)


def last_kernel(
    force, went_dn, went_up, came_e, came_o, _before, out, below, above, rows, patch, sem
):
    f = [force[axis : axis + 1, :] for axis in range(3)]
    for even in range(2):

        @pl.when(parity("gy") == even)
        def _():
            widen(came_o if even == 0 else came_e, 1, below)
            widen(came_e if even == 0 else came_o, -1, above)

    last_side(0, 1, went_dn, below, out, rows, patch, sem, f)
    last_side(1, -1, went_up, above, out, rows, patch, sem, f)
    pltpu.make_async_copy(patch, patch, sem).wait()


def swap(value, axis, first):
    n = lax.axis_size(axis)
    pairs = [(i, (i + 1) % n if (i % 2 == 0) == first else (i - 1) % n) for i in range(n)]
    return lax.ppermute(value, axis, pairs)


def halves_of(porosity, relaxation):
    hi = lax.axis_index("gy") // 4
    slab = jnp.stack([porosity, relaxation]).reshape(2, 2, 8, 16, 128)
    other = lax.dynamic_slice_in_dim(slab, (1 - hi) * 4, 4, axis=2)
    mine = lax.dynamic_slice_in_dim(slab, hi * 4, 4, axis=2)
    return mine, lax.ppermute(other, "gy", [(i, i ^ 4) for i in range(8)])


def pieces_of(mine, came):
    b = lax.axis_index("gy")
    hi, lo = b // 4, b % 4
    both = jnp.stack([jnp.where(hi == 0, mine, came), jnp.where(hi == 0, came, mine)])
    parts = [lax.dynamic_index_in_dim(both, lo, axis=3, keepdims=False)]
    for k in range(1, 4):
        message = lax.dynamic_index_in_dim(both, lo ^ k, axis=3, keepdims=False)
        parts.append(lax.ppermute(message, "gy", [(i, i ^ k) for i in range(8)]))
    return parts


def block_of(parts):
    lo = lax.axis_index("gy") % 4
    stacked = jnp.stack(parts)
    ordered = [
        lax.dynamic_index_in_dim(stacked, lo ^ y, axis=0, keepdims=False) for y in range(4)
    ]
    whole = jnp.stack(ordered)
    return whole.transpose(2, 1, 0, 3, 4, 5).reshape(2, 16, 16, 128)


def local(pdf_old, tile_target, porosity, relaxation, solid_mask, force):
    mine, came = halves_of(porosity, relaxation)
    rows = pdf_old.reshape(16, 8, 19, 2, 128).transpose(2, 0, 3, 1, 4).reshape(19, 256, 128)
    packed = pack(tile_target, rows)
    packed, came = lax.optimization_barrier((packed, came))
    arrived = lax.all_to_all(
        packed, ("gx", "gy"), split_axis=0, concat_axis=0, tiled=True
    )
    block = block_of(pieces_of(mine, came))
    solid = block[0] + solid_mask.astype(F32) * (1.0 - block[0])
    coef = jnp.stack([solid, block[1]])
    drive = jnp.broadcast_to(jnp.pad(force, (0, 5))[:, None], (8, 128))
    coef, drive = lax.optimization_barrier((coef, drive))
    hbm = pl.BlockSpec(memory_space=pltpu.HBM)
    posts = [jax.ShapeDtypeStruct((19, n, 16, 128), F32) for n in (4, 12)]
    found, edge, xe, xo = pl.pallas_call(
        edge_kernel,
        out_shape=[jax.ShapeDtypeStruct((8, 128), jnp.int32), posts[0], FACE, FACE],
        in_specs=[VMEM_SPEC, hbm, VMEM_SPEC],
        out_specs=[VMEM_SPEC] * 4,
        scratch_shapes=[
            pltpu.VMEM((32 * ROWS, 128), F32),
            pltpu.VMEM((DEVICES, 128), F32),
            pltpu.SemaphoreType.DMA((4,)),
            pltpu.SemaphoreType.DMA,
        ],
        compiler_params=pltpu.CompilerParams(vmem_limit_bytes=VMEM_LIMIT),
        cost_estimate=pl.CostEstimate(flops=2_000_000, bytes_accessed=8_000_000, transcendentals=0),
    )(drive, arrived, coef)
    from_xo = swap(xo, "gx", False)
    from_xe = swap(xe, "gx", True)
    inner, own_ye, own_yo = pl.pallas_call(
        inner_kernel,
        out_shape=[posts[1], SENT, SENT],
        in_specs=[VMEM_SPEC, VMEM_SPEC, hbm, VMEM_SPEC, VMEM_SPEC],
        out_specs=[VMEM_SPEC] * 3,
        scratch_shapes=[
            pltpu.VMEM((96 * ROWS, 128), F32),
            pltpu.SMEM((8, 128), jnp.int32),
            pltpu.SemaphoreType.DMA((12,)),
            pltpu.SemaphoreType.DMA,
        ],
        compiler_params=pltpu.CompilerParams(vmem_limit_bytes=VMEM_LIMIT),
        cost_estimate=pl.CostEstimate(flops=6_000_000, bytes_accessed=8_000_000, transcendentals=0),
    )(drive, found, arrived, coef, edge)
    ye, yo = call(join_kernel, [SENT, SENT], (from_xe, from_xo, own_ye, own_yo), 500_000)
    from_yo = swap(yo, "gy", False)
    from_ye = swap(ye, "gy", True)
    result, went_dn, went_up = call(
        middle_kernel,
        [jax.ShapeDtypeStruct((19, 16, 16, 128), F32), SIDE, SIDE],
        (drive, edge, inner, coef, from_xe, from_xo, ye, yo),
        12_000_000,
        out_specs=[hbm, VMEM_SPEC, VMEM_SPEC],
        scratch_shapes=[
            pltpu.VMEM((19, EXT, 32, 128), F32),
            pltpu.VMEM((19, 18, 32, 128), F32),
            pltpu.VMEM((16, 19, 16, 128), F32),
            pltpu.SemaphoreType.DMA((16,)),
        ],
    )
    return pl.pallas_call(
        last_kernel,
        out_shape=jax.ShapeDtypeStruct((19, 16, 16, 128), F32),
        in_specs=[VMEM_SPEC] * 5 + [hbm],
        out_specs=hbm,
        input_output_aliases={5: 0},
        scratch_shapes=[
            pltpu.VMEM((SIDE_ROWS, 128), F32),
            pltpu.VMEM((SIDE_ROWS, 128), F32),
            pltpu.VMEM((2, 19, 24, 128), F32),
            pltpu.VMEM((38, 16, 128), F32),
            pltpu.SemaphoreType.DMA,
        ],
        compiler_params=pltpu.CompilerParams(vmem_limit_bytes=VMEM_LIMIT),
        cost_estimate=pl.CostEstimate(flops=2_000_000, bytes_accessed=2_000_000, transcendentals=0),
    )(drive, went_dn, went_up, from_ye, from_yo, result)


def solution(mesh):
    return jax.shard_map(
        local,
        mesh=mesh,
        in_specs=(
            P(("gx", "gy"), None, None),
            P(("gx", "gy")),
            P(("gx", "gy"), None, None),
            P(("gx", "gy"), None, None),
            P("gx", "gy", None),
            P(),
        ),
        out_specs=P(None, "gx", "gy", None),
        check_vma=False,
    )
```

```python
import jax
import jax.numpy as jnp
from jax import lax
from jax.experimental import pallas as pl
from jax.experimental.pallas import tpu as pltpu
from jax.sharding import PartitionSpec as P

VELOCITY = (
    (0, 0, 0),
    (1, 0, 0),
    (-1, 0, 0),
    (0, 1, 0),
    (0, -1, 0),
    (0, 0, 1),
    (0, 0, -1),
    (1, 1, 0),
    (-1, -1, 0),
    (1, -1, 0),
    (-1, 1, 0),
    (1, 0, 1),
    (-1, 0, -1),
    (1, 0, -1),
    (-1, 0, 1),
    (0, 1, 1),
    (0, -1, -1),
    (0, 1, -1),
    (0, -1, 1),
)
WEIGHT = [1.0 / 3.0] + [1.0 / 18.0] * 6 + [1.0 / 36.0] * 12
INVERSE = [3.0] + [18.0] * 6 + [36.0] * 12
DEVICES = 128
HELD = 128
CAP = 2
TILE = 38
PAIR = 2 * TILE + 1
ROWS = 41
APART = 257
EXT = 20
VMEM_LIMIT = 48 * 1024 * 1024
VMEM_MOST = 61 * 1024 * 1024
F32 = jnp.float32


def entries(axis, sign):
    far = [(q, 1) for q in range(19) if VELOCITY[q][axis] == sign]
    near = [(q, 0) for q in range(19) if VELOCITY[q][axis] in (0, sign)]
    return far + near


COUNT = 21
SIDE_ROWS = 432
SENT_ROWS = 384


def parity(axis):
    return lax.rem(lax.axis_index(axis), 2)


def collide(dist, solid, omega, force):
    plus = [None] * 19
    minus = [None] * 19
    for i in range(1, 19, 2):
        plus[i] = dist[i] + dist[i + 1]
        minus[i] = dist[i] - dist[i + 1]
    density = dist[0]
    for i in range(1, 19, 2):
        density = density + plus[i]
    flow = []
    for axis in range(3):
        total = None
        for i in range(1, 19, 2):
            c = VELOCITY[i][axis]
            if c:
                if total is None:
                    total = minus[i]
                else:
                    total = total + minus[i] if c == 1 else total - minus[i]
        flow.append(total + 0.5 * force[axis])
    base = density - 1.5 * (flow[0] * flow[0] + flow[1] * flow[1] + flow[2] * flow[2])
    open_ = 1.0 - solid
    a = open_ * omega
    b = open_ * ((2.0 - omega) / (1.0 - 0.125 * omega))
    keep = 0.5 - 0.5 * a
    turn = 0.5 - solid - 0.5 * b
    post = [None] * 19
    at = a * base
    post[0] = (keep + keep) * dist[0] + at * (1.0 / 3.0)
    drive = [b * flow[axis] + open_ * force[axis] for axis in range(3)]
    for group, w in ((range(1, 7, 2), 1.0 / 18.0), (range(7, 19, 2), 1.0 / 36.0)):
        even_base = at * w
        square = a * (4.5 * w)
        pull = [drive[axis] * (3.0 * w) for axis in range(3)]
        for i in group:
            along = None
            odd = None
            for axis in range(3):
                c = VELOCITY[i][axis]
                if c:
                    if along is None:
                        along, odd = flow[axis], pull[axis]
                    elif c == 1:
                        along, odd = along + flow[axis], odd + pull[axis]
                    else:
                        along, odd = along - flow[axis], odd - pull[axis]
            even = keep * plus[i] + (even_base + square * (along * along))
            odd = turn * minus[i] + odd
            post[i] = even + odd
            post[i + 1] = even - odd
    return post


def shift_z(value, q):
    c = VELOCITY[q][2]
    return value if c == 0 else pltpu.roll(value, c % 128, 1)


def pack_kernel(target_hbm, pdf_hbm, out, target, used, pdf, tiles, labels, sems, small, sent):
    listing = pltpu.make_async_copy(target_hbm, target, small.at[0])
    listing.start()
    quarters = []
    for part in range(4):
        rows = pl.ds(part * 64, 64)
        copy = pltpu.make_async_copy(pdf_hbm.at[:, rows, :], pdf.at[:, rows, 0, :], sems.at[part])
        copy.start()
        quarters.append(copy)
    flat = pdf.reshape(19 * APART, 128)
    rows_ = tiles.reshape(HELD * TILE, 128)
    empty = jnp.full((8, 128), -1.0, F32)
    for block in range(DEVICES // 8):
        labels[8 * block : 8 * block + 8, 0, :] = empty

    def clear(i, _):
        used[i] = 0
        return 0

    lax.fori_loop(0, DEVICES, clear, 0, unroll=8)
    half = lax.broadcasted_iota(jnp.int32, (1, 128), 1) // 64
    listing.wait()

    def put(k, _):
        t = target[k]
        owner = lax.shift_right_logical(t, 7)
        rank = used[owner]
        used[owner] = rank + 1
        near = lax.shift_right_logical(k, 3) * 16 + (k & 7)
        for r in range(2):
            for q in (0, 8, 16):
                n = min(8, 19 - q)
                value = flat[pl.ds(near + r * 8 + q * APART, n, stride=APART), :]
                rows_[pl.ds(k * TILE + r * 19 + q, n), :] = value
        pltpu.make_async_copy(
            tiles.at[pl.ds(k * TILE, TILE)],
            out.at[owner, pl.ds(rank * TILE, TILE)],
            sent,
        ).start()
        line = labels[owner]
        labels[owner] = jnp.where(half == rank, (t & 127).astype(F32), line)
        return 0

    for part in range(4):
        quarters[part].wait()
        lax.fori_loop(part * 32, part * 32 + 32, put, 0, unroll=4)
    named = pltpu.make_async_copy(labels, out.at[:, 2 * TILE], small.at[1])
    named.start()
    pltpu.make_async_copy(tiles, tiles, sent).wait()
    named.wait()


def pack(target, pdf):
    hbm = pl.BlockSpec(memory_space=pltpu.HBM)
    return pl.pallas_call(
        pack_kernel,
        out_shape=jax.ShapeDtypeStruct((DEVICES, PAIR, 1, 128), F32),
        in_specs=[hbm, hbm],
        out_specs=hbm,
        scratch_shapes=[
            pltpu.SMEM((HELD,), jnp.int32),
            pltpu.SMEM((DEVICES,), jnp.int32),
            pltpu.VMEM((19, APART, 1, 128), F32),
            pltpu.VMEM((HELD * TILE, 1, 128), F32),
            pltpu.VMEM((DEVICES, 1, 128), F32),
            pltpu.SemaphoreType.DMA((4,)),
            pltpu.SemaphoreType.DMA((2,)),
            pltpu.SemaphoreType.DMA,
        ],
        compiler_params=pltpu.CompilerParams(vmem_limit_bytes=VMEM_MOST),
        cost_estimate=pl.CostEstimate(flops=0, bytes_accessed=8_000_000, transcendentals=0),
    )(target, pdf)


def pick(flag, even, odd):
    return jnp.where(flag == 0, even, odd)


def plane_step(x, at, tiles, coef, post, f):
    for r in range(2):
        dist = []
        for q in range(19):
            value = tiles[pl.ds(at * (8 * ROWS) + r * 19 + q, 8, stride=ROWS), :]
            dist.append(WEIGHT[q] * value + WEIGHT[q])
        solid = coef[0, x, pl.ds(r, 8, stride=2), :]
        omega = coef[1, x, pl.ds(r, 8, stride=2), :]
        after = collide(dist, solid, omega, f)
        for q in range(19):
            post[q, at, pl.ds(r, 8, stride=2), :] = shift_z(after[q], q)


def fetch(p, arrived, tiles, sem, at):
    pltpu.make_async_copy(
        arrived.at[lax.shift_right_logical(p, 1), pl.ds((p & 1) * TILE, TILE), 0, :],
        tiles.at[pl.ds(at * ROWS, TILE), :],
        sem,
    ).start()


def arrive(tiles, sem):
    whole = tiles.at[pl.ds(0, 8 * TILE), :]
    pltpu.make_async_copy(whole, whole, sem).wait()


def edge_kernel(
    force, arrived, coef, found, edge, xe, xo, tiles, labels, sems, small
):
    pull = pltpu.make_async_copy(arrived.at[:, 2 * TILE, 0, :], labels, small)
    pull.start()
    f = [force[axis : axis + 1, :] for axis in range(3)]
    lane = lax.broadcasted_iota(jnp.int32, (8, 128), 1)
    lane_f = lane.astype(F32)
    sub = lax.broadcasted_iota(jnp.int32, (8, 128), 0)
    low = lane < 64
    total = jnp.zeros((8, 128), jnp.int32)
    pull.wait()
    for group in range(DEVICES // 8):
        line = labels[8 * group : 8 * group + 8, :]
        other = pltpu.roll(line, 64, 1)
        number = (sub + 8 * group) * 2
        total = total + jnp.where(jnp.where(low, line, other) == lane_f, number, 0)
        total = total + jnp.where(jnp.where(low, other, line) == lane_f, number + 1, 0)
    numbers = jnp.sum(total, axis=0, keepdims=True)
    found[...] = jnp.broadcast_to(numbers, (8, 128))
    for j, x in enumerate((0, 1, 14, 15)):
        for i in range(8):
            fetch(numbers[0, 8 * x + i], arrived, tiles, sems.at[j], 8 * j + i)

    def plane(j, _):
        arrive(tiles, sems.at[j])
        plane_step(jnp.where(j < 2, j, j + 12), j, tiles, coef, edge, f)
        return 0

    lax.fori_loop(0, 4, plane, 0)
    for even in range(2):

        @pl.when(parity("gx") == even)
        def _():
            for out, sign in ((xe, 1 - 2 * even), (xo, 2 * even - 1)):
                for i, (q, layer) in enumerate(entries(0, sign)):
                    out[i] = edge[q, 3 - layer if sign == 1 else layer]
                for j in range(2):
                    out[19 + j] = coef[j, 15 if sign == 1 else 0]


def inner_kernel(force, found, arrived, coef, edge, inner, ye, yo, tiles, source, sems, small):
    hand = pltpu.make_async_copy(found, source, small)
    hand.start()
    f = [force[axis : axis + 1, :] for axis in range(3)]
    hand.wait()

    for j in range(12):
        for i in range(8):
            fetch(source[0, 16 + 8 * j + i], arrived, tiles, sems.at[j], 8 * j + i)

    def plane(j, _):
        arrive(tiles, sems.at[j])
        plane_step(j + 2, j, tiles, coef, inner, f)
        return 0

    lax.fori_loop(0, 12, plane, 0)
    for even in range(2):

        @pl.when(parity("gy") == even)
        def _():
            for out, sign in ((ye, 1 - 2 * even), (yo, 2 * even - 1)):
                for i, (q, layer) in enumerate(entries(1, sign)):
                    row = 15 - layer if sign == 1 else layer
                    for x in range(16):
                        if 2 <= x < 14:
                            value = inner[q, x - 2, row : row + 1, :]
                        else:
                            value = edge[q, x if x < 2 else x - 12, row : row + 1, :]
                        out[16 * i + x : 16 * i + x + 1, :] = value
                row = 15 if sign == 1 else 0
                for j in range(2):
                    for x in range(16):
                        at = (19 + j) * 16 + x
                        out[at : at + 1, :] = coef[j, x, row : row + 1, :]


VMEM_SPEC = pl.BlockSpec(memory_space=pltpu.VMEM)
FACE = jax.ShapeDtypeStruct((COUNT, 16, 128), F32)
SIDE = jax.ShapeDtypeStruct((SIDE_ROWS, 128), F32)
SENT = jax.ShapeDtypeStruct((SENT_ROWS, 128), F32)


def call(kernel, out_shape, operands, work, **more):
    return pl.pallas_call(
        kernel,
        out_shape=out_shape,
        in_specs=[VMEM_SPEC] * len(operands),
        compiler_params=pltpu.CompilerParams(vmem_limit_bytes=VMEM_LIMIT),
        cost_estimate=pl.CostEstimate(flops=work, bytes_accessed=work, transcendentals=0),
        **more,
    )(*operands)


def corners(sign):
    listed = []
    for toward, side in enumerate((1, -1)):
        have = {e: n for n, e in enumerate(entries(0, side) + [(19, 0), (20, 0)])}
        for deep in range(2):
            column = 1 - deep if toward == 0 else 18 + deep
            for i, (q, layer) in enumerate(entries(1, sign) + [(19, 0), (20, 0)]):
                if (q, deep) in have:
                    row = 15 - layer if sign == 1 else layer
                    listed.append((i, column, toward, have[(q, deep)], row))
    return listed


def join_kernel(xe, xo, own_e, own_o, ye, yo):
    for own, out in ((own_e, ye), (own_o, yo)):
        for block in range(COUNT * 2):
            out[8 * block : 8 * block + 8, :] = own[8 * block : 8 * block + 8, :]
        out[SENT_ROWS - 8 : SENT_ROWS, :] = jnp.zeros((8, 128), F32)
    for even_x in range(2):
        for even_y in range(2):

            @pl.when((parity("gx") == even_x) & (parity("gy") == even_y))
            def _():
                halves = (xo, xe) if even_x == 0 else (xe, xo)
                for out, sign in ((ye, 1 - 2 * even_y), (yo, 2 * even_y - 1)):
                    for n, (_i, _column, toward, there, row) in enumerate(corners(sign)):
                        at = COUNT * 16 + n
                        out[at : at + 1, :] = halves[toward][there, row : row + 1, :]


def widen(message, sign, out):
    for i in range(COUNT):
        out[i * EXT + 2 : i * EXT + 18, :] = message[16 * i : 16 * i + 16, :]
    for n, (i, column, *_rest) in enumerate(corners(sign)):
        at = COUNT * 16 + n
        out[i * EXT + column : i * EXT + column + 1, :] = message[at : at + 1, :]


def middle_kernel(
    force, edge, inner, coef, xe, xo, ye, yo, out, went_dn, went_up, wide, again, result, sems
):
    flag = parity("gx")
    for j in range(4):
        for q in range(19):
            wide[q, (j if j < 2 else j + 12) + 2, 8:24, :] = edge[q, j]

    def copy(x, _):
        for q in range(19):
            wide[q, x + 4, 8:24, :] = inner[q, x]
        return 0

    lax.fori_loop(0, 12, copy, 0)
    sides = []
    for toward, sign in ((0, 1), (1, -1)):
        even, odd_ = (xo, xe) if toward == 0 else (xe, xo)
        for i, (q, layer) in enumerate(entries(0, sign)):
            at = 1 - layer if toward == 0 else 18 + layer
            wide[q, at, 8:24, :] = pick(flag, even[i], odd_[i])
        sides.append([pick(flag, even[19 + j], odd_[19 + j]) for j in range(2)])
    f = [force[axis : axis + 1, :] for axis in range(3)]

    def one(x, solids, omegas):
        for block in range(2):
            dist = []
            for q in range(19):
                cx, cy, _z = VELOCITY[q]
                dist.append(wide[q, x + 1 - cx, 8 + 8 * block - cy : 16 + 8 * block - cy, :])
            after = collide(dist, solids[block], omegas[block], f)
            for q in range(19):
                again[q, x, 8 + 8 * block : 16 + 8 * block, :] = shift_z(after[q], q)

    def plane(x, _):
        solids = [coef[0, x - 1, 8 * block : 8 * block + 8, :] for block in range(2)]
        omegas = [coef[1, x - 1, 8 * block : 8 * block + 8, :] for block in range(2)]
        one(x, solids, omegas)
        return 0

    one(0, *[[v[0:8], v[8:16]] for v in sides[0]])
    one(17, *[[v[0:8], v[8:16]] for v in sides[1]])
    lax.fori_loop(1, 17, plane, 0)

    def finish(x, _):
        for q in range(19):
            cx, cy, _z = VELOCITY[q]
            for block in range(2):
                start = 8 + 8 * block - cy
                value = again[q, x + 1 - cx, start : start + 8, :]
                result[x, q, 8 * block : 8 * block + 8, :] = value * INVERSE[q] - 1.0
        pltpu.make_async_copy(result.at[x], out.at[:, x], sems.at[x]).start()
        return 0

    lax.fori_loop(0, 16, finish, 0)
    for even in range(2):

        @pl.when(parity("gy") == even)
        def _():
            widen(ye if even == 0 else yo, 1, went_up)
            widen(yo if even == 0 else ye, -1, went_dn)

    for x in range(16):
        pltpu.make_async_copy(result.at[x], out.at[:, x], sems.at[x]).wait()


def last_side(side, sign, own, other, out, rows, patch, sem, f):
    came = {e: n for n, e in enumerate(entries(1, sign))}
    mine = {e: n for n, e in enumerate(entries(1, -sign))}
    for line in range(2):
        for block in range(3):
            start = 1 + 8 * block
            dist = []
            for q in range(19):
                cx, cy, _z = VELOCITY[q]
                if cy == sign:
                    which, n = other, came[(q, 1 - line)]
                elif cy == 0:
                    which, n = (other, came[(q, 0)]) if line == 0 else (own, mine[(q, 0)])
                else:
                    which, n = own, mine[(q, line)]
                at = n * EXT + start - cx
                dist.append(which[at : at + 8, :])
            where = other if line == 0 else own
            fixed = [where[(19 + j) * EXT + start : (19 + j) * EXT + start + 8, :] for j in range(2)]
            after = collide(dist, fixed[0], fixed[1], f)
            for q in range(19):
                if VELOCITY[q][1] == sign or (VELOCITY[q][1] == 0 and line == 1):
                    rows[line, q, 8 * block : 8 * block + 8, :] = shift_z(after[q], q)
    number = 19 * side
    for depth in range(2):
        listed = [q for q in range(19) if VELOCITY[q][1] in ((sign, 0) if depth == 0 else (sign,))]
        y = depth if sign == 1 else 15 - depth
        begin = 0
        for n, q in enumerate(listed):
            cx, cy, _z = VELOCITY[q]
            line = 1 if depth == 1 or cy == 0 else 0
            patch[number + n] = rows[line, q, 1 - cx : 17 - cx, :] * INVERSE[q] - 1.0
            if n + 1 == len(listed) or listed[n + 1] != q + 1:
                count = n + 1 - begin
                pltpu.make_async_copy(
                    patch.at[pl.ds(number + begin, count)],
                    out.at[pl.ds(q + 1 - count, count), :, y, :],
                    sem,
                ).start()
                begin = n + 1
        number += len(listed)


def last_kernel(
    force, went_dn, went_up, came_e, came_o, _before, out, below, above, rows, patch, sem
):
    f = [force[axis : axis + 1, :] for axis in range(3)]
    for even in range(2):

        @pl.when(parity("gy") == even)
        def _():
            widen(came_o if even == 0 else came_e, 1, below)
            widen(came_e if even == 0 else came_o, -1, above)

    last_side(0, 1, went_dn, below, out, rows, patch, sem, f)
    last_side(1, -1, went_up, above, out, rows, patch, sem, f)
    pltpu.make_async_copy(patch, patch, sem).wait()


def swap(value, axis, first):
    n = lax.axis_size(axis)
    pairs = [(i, (i + 1) % n if (i % 2 == 0) == first else (i - 1) % n) for i in range(n)]
    return lax.ppermute(value, axis, pairs)


def halves_of(porosity, relaxation):
    lo = lax.axis_index("gy") % 2
    slab = jnp.stack([porosity, relaxation]).reshape(2, 2, 4, 2, 16, 128)
    other = lax.dynamic_index_in_dim(slab, 1 - lo, axis=3, keepdims=False)
    mine = lax.dynamic_index_in_dim(slab, lo, axis=3, keepdims=False)
    return mine, lax.ppermute(other, "gy", [(i, i ^ 1) for i in range(8)])


def pieces_of(mine, came):
    b = lax.axis_index("gy")
    hi, lo = b // 2, b % 2
    both = jnp.stack([jnp.where(lo == 0, mine, came), jnp.where(lo == 0, came, mine)])
    parts = [lax.dynamic_index_in_dim(both, hi, axis=3, keepdims=False)]
    for k in range(1, 4):
        message = lax.dynamic_index_in_dim(both, hi ^ k, axis=3, keepdims=False)
        parts.append(lax.ppermute(message, "gy", [(i, i ^ (2 * k)) for i in range(8)]))
    return parts


def block_of(parts):
    hi = lax.axis_index("gy") // 2
    stacked = jnp.stack(parts)
    ordered = [
        lax.dynamic_index_in_dim(stacked, hi ^ y, axis=0, keepdims=False) for y in range(4)
    ]
    whole = jnp.stack(ordered)
    return whole.transpose(2, 0, 1, 3, 4, 5).reshape(2, 16, 16, 128)


def local(pdf_old, tile_target, porosity, relaxation, solid_mask, force):
    mine, came = halves_of(porosity, relaxation)
    rows = pdf_old.reshape(16, 8, 19, 2, 128).transpose(2, 0, 3, 1, 4).reshape(19, 256, 128)
    packed = pack(tile_target, rows)
    packed, came = lax.optimization_barrier((packed, came))
    arrived = lax.all_to_all(
        packed, ("gx", "gy"), split_axis=0, concat_axis=0, tiled=True
    )
    block = block_of(pieces_of(mine, came))
    solid = block[0] + solid_mask.astype(F32) * (1.0 - block[0])
    coef = jnp.stack([solid, block[1]])
    drive = jnp.broadcast_to(jnp.pad(force, (0, 5))[:, None], (8, 128))
    coef, drive = lax.optimization_barrier((coef, drive))
    hbm = pl.BlockSpec(memory_space=pltpu.HBM)
    posts = [jax.ShapeDtypeStruct((19, n, 16, 128), F32) for n in (4, 12)]
    found, edge, xe, xo = pl.pallas_call(
        edge_kernel,
        out_shape=[jax.ShapeDtypeStruct((8, 128), jnp.int32), posts[0], FACE, FACE],
        in_specs=[VMEM_SPEC, hbm, VMEM_SPEC],
        out_specs=[VMEM_SPEC] * 4,
        scratch_shapes=[
            pltpu.VMEM((32 * ROWS, 128), F32),
            pltpu.VMEM((DEVICES, 128), F32),
            pltpu.SemaphoreType.DMA((4,)),
            pltpu.SemaphoreType.DMA,
        ],
        compiler_params=pltpu.CompilerParams(vmem_limit_bytes=VMEM_LIMIT),
        cost_estimate=pl.CostEstimate(flops=2_000_000, bytes_accessed=8_000_000, transcendentals=0),
    )(drive, arrived, coef)
    from_xo = swap(xo, "gx", False)
    from_xe = swap(xe, "gx", True)
    inner, own_ye, own_yo = pl.pallas_call(
        inner_kernel,
        out_shape=[posts[1], SENT, SENT],
        in_specs=[VMEM_SPEC, VMEM_SPEC, hbm, VMEM_SPEC, VMEM_SPEC],
        out_specs=[VMEM_SPEC] * 3,
        scratch_shapes=[
            pltpu.VMEM((96 * ROWS, 128), F32),
            pltpu.SMEM((8, 128), jnp.int32),
            pltpu.SemaphoreType.DMA((12,)),
            pltpu.SemaphoreType.DMA,
        ],
        compiler_params=pltpu.CompilerParams(vmem_limit_bytes=VMEM_LIMIT),
        cost_estimate=pl.CostEstimate(flops=6_000_000, bytes_accessed=8_000_000, transcendentals=0),
    )(drive, found, arrived, coef, edge)
    ye, yo = call(join_kernel, [SENT, SENT], (from_xe, from_xo, own_ye, own_yo), 500_000)
    from_yo = swap(yo, "gy", False)
    from_ye = swap(ye, "gy", True)
    result, went_dn, went_up = call(
        middle_kernel,
        [jax.ShapeDtypeStruct((19, 16, 16, 128), F32), SIDE, SIDE],
        (drive, edge, inner, coef, from_xe, from_xo, ye, yo),
        12_000_000,
        out_specs=[hbm, VMEM_SPEC, VMEM_SPEC],
        scratch_shapes=[
            pltpu.VMEM((19, EXT, 32, 128), F32),
            pltpu.VMEM((19, 18, 32, 128), F32),
            pltpu.VMEM((16, 19, 16, 128), F32),
            pltpu.SemaphoreType.DMA((16,)),
        ],
    )
    return pl.pallas_call(
        last_kernel,
        out_shape=jax.ShapeDtypeStruct((19, 16, 16, 128), F32),
        in_specs=[VMEM_SPEC] * 5 + [hbm],
        out_specs=hbm,
        input_output_aliases={5: 0},
        scratch_shapes=[
            pltpu.VMEM((SIDE_ROWS, 128), F32),
            pltpu.VMEM((SIDE_ROWS, 128), F32),
            pltpu.VMEM((2, 19, 24, 128), F32),
            pltpu.VMEM((38, 16, 128), F32),
            pltpu.SemaphoreType.DMA,
        ],
        compiler_params=pltpu.CompilerParams(vmem_limit_bytes=VMEM_LIMIT),
        cost_estimate=pl.CostEstimate(flops=2_000_000, bytes_accessed=2_000_000, transcendentals=0),
    )(drive, went_dn, went_up, from_ye, from_yo, result)


def solution(mesh):
    return jax.shard_map(
        local,
        mesh=mesh,
        in_specs=(
            P(("gx", "gy"), None, None),
            P(("gx", "gy")),
            P(("gx", "gy"), None, None),
            P(("gx", "gy"), None, None),
            P("gx", "gy", None),
            P(),
        ),
        out_specs=P(None, "gx", "gy", None),
        check_vma=False,
    )
```
